256 devices in a mesh: ctx: 32 (over y_lo, z, core), head: 8 (over x, y_hi).
Axes of the slice: x: 4, y: 4 (y_hi: 2, y_lo: 2; y = y_hi * 2 + y_lo), z: 8, core: 2. Of those that a mesh axis runs over, the one named last changes fastest.
Arguments:
- queries: bfloat16 [2, 6144, 8192], P(None, 'ctx', 'head'), may hold values from -10 to 10
- key_states: bfloat16 [2, 6144, 1024], P(None, 'ctx', 'head'), may hold values from -6 to 6
- value_states: bfloat16 [2, 6144, 1024], P(None, 'ctx', 'head'), may hold values from -6 to 6
- segment_ids: int32 [12288], replicated, may hold values from 0 to 3, never falling along the last dimension, each value on 1 to 6144 neighbouring positions
Outputs:
- attended: bfloat16 [2, 6144, 8192], P(None, 'ctx', 'head')
- key_cache: bfloat16 [12288, 1024], P(('ctx', 'head'))
- value_cache: bfloat16 [12288, 1024], P(('ctx', 'head'))
The draws below stay inside these ranges and needn't reach their ends.
Inputs may be any that keep to these rules, and one draw needn't show every extreme that they name: `segment_ids`: segment numbers never fall along positions; each segment spans 1 to 6144 positions, and one spans exactly 6144.
All inputs are finite; a program needn't handle non-finite values.
Results may differ from the reference program's by a relative error of at most 0.0055.
Values may be sent and summed in bfloat16 or wider, within the bound.
A program may use at most 64 MiB of HBM per device.

```python
import math
from functools import partial
import jax
import jax.numpy as jnp
import numpy as np
from jax import lax

HEADS = 64
KV_HEADS = 8
DH = 128
SEGS = 4
KW = 1024
HALF = 6144
LENGTH = 12288


def draw_queries(key, part):
    key = jax.random.fold_in(key, 11)
    array_shape = (2, HALF, HEADS * DH)
    return jnp.clip(jax.random.normal(key, array_shape, jnp.float32) * 2.2, -10.0, 10.0).astype(jnp.bfloat16)


def draw_key_states(key, part):
    key = jax.random.fold_in(key, 23)
    array_shape = (2, HALF, KV_HEADS * DH)
    return jnp.clip(jax.random.normal(key, array_shape, jnp.float32) * 1.2, -6.0, 6.0).astype(jnp.bfloat16)


def block_scale(key, shape, cuts, least, top_value):
    def one(axis_at, blocks):
        steps = jax.random.uniform(jax.random.fold_in(jax.random.fold_in(key, 6), axis_at), (blocks,), jnp.float32, least / len(cuts), top_value / len(cuts))
        return jnp.repeat(jnp.exp(steps), shape[axis_at] // blocks).reshape((-1,) + (1,) * (len(shape) - axis_at - 1))

    gain = one(*cuts[0])
    for cut in cuts[1:]:
        gain = gain * one(*cut)
    return gain


def length_profile(amount, total, bound, lean):
    loads = [(1 << 20) // math.isqrt(standing ** lean) + 1 for standing in range(2, amount + 1)]
    surplus, holding = total - bound - (amount - 1), [1] * (amount - 1)
    while surplus > 0:
        movable = [i for i in range(amount - 1) if holding[i] < bound]
        mass, remaining = sum([loads[i] for i in movable]), surplus
        for i in movable:
            addition = min(bound - holding[i], max(1, remaining * loads[i] // mass), surplus)
            holding[i] = holding[i] + addition
            surplus = surplus - addition
    return np.array([bound] + holding)


def uneven_parts(key, count, total, most, slope):
    if count == 2:
        one = jax.random.randint(key, (), max(1, total - most), min(most, total - 1) + 1)
        return jnp.stack([one, total - one])
    tallies = jnp.asarray(length_profile(count, total, most, slope), jnp.int32)
    twos = (count - 1) // 2
    giver, receiver = tallies[1:1 + 2 * twos:2], tallies[2:2 + 2 * twos:2]
    slack = jnp.minimum(giver - 1, most - receiver)
    moved = jax.random.randint(jax.random.fold_in(key, 1), (twos,), 0, 1 << 20) % (slack + 1)
    tallies = tallies.at[1:1 + 2 * twos:2].set(giver - moved).at[2:2 + 2 * twos:2].set(receiver + moved)
    return tallies[jax.random.permutation(jax.random.fold_in(key, 2), count)]


def gaussian(rng, extent, deviation, bound, cuts=(), kind=jnp.bfloat16):
    values = jax.random.normal(rng, extent, jnp.float32) * deviation
    if len(cuts) > 0:
        values = block_scale(rng, extent, cuts, -0.22, 0.18) * values
    return jnp.clip(values, min=-bound, max=bound).astype(kind)


def setup_inputs(seed: int = 0) -> dict:
    key_list = jax.random.split(jax.random.key(seed), 5)
    return {
        "queries": draw_queries(jax.random.fold_in(key_list[4], 71), 0),
        "key_states": draw_key_states(jax.random.fold_in(key_list[4], 71), 0),
        "value_states": gaussian(key_list[2], (2, HALF, KW), 1.0, 6.0, ((1, 32), (2, 8))),
        "segment_ids": jnp.searchsorted(jnp.cumsum(uneven_parts(key_list[3], SEGS, LENGTH, LENGTH // 2, 0)), jnp.arange(LENGTH), side="right").astype(jnp.int32),
    }


def head_attention(head_items, visible_mask, score_scale):
    head_queries, head_keys, head_values = head_items
    scores = jnp.einsum('tgd,ud->gtu', head_queries.astype(jnp.float32), head_keys.astype(jnp.float32)) * score_scale
    scores = jnp.where(visible_mask[None], scores, -jnp.inf)
    peak_score = lax.optimization_barrier(jnp.max(scores, axis=-1, keepdims=True))
    weights = jnp.where(visible_mask[None], jnp.exp(scores - peak_score), 0.0)
    denominator = lax.optimization_barrier(jnp.sum(weights, axis=-1))
    rounded = lax.optimization_barrier(weights.astype(jnp.bfloat16))
    numerator = jnp.einsum('gtu,ud->gtd', rounded.astype(jnp.float32), head_values.astype(jnp.float32))
    return (numerator / denominator[..., None]).astype(jnp.bfloat16)

def reference(queries, key_states, value_states, segment_ids):
    length = 2 * HALF
    groups = HEADS // KV_HEADS
    q_all = queries.reshape(length, KV_HEADS, groups, DH).transpose(1, 0, 2, 3)
    k_all = key_states.reshape(length, KV_HEADS, DH).transpose(1, 0, 2)
    v_all = value_states.reshape(length, KV_HEADS, DH).transpose(1, 0, 2)
    score_scale = 1.0 / math.sqrt(DH)
    block_rows = math.gcd(length, 1024)
    pieces = []
    for block_start in range(0, length, block_rows):
        block_end = block_start + block_rows
        query_pos = jnp.arange(block_start, block_end, dtype=jnp.int32)
        key_pos = jnp.arange(block_end, dtype=jnp.int32)
        same_segment = segment_ids[:block_end][None, :] == segment_ids[block_start:block_end][:, None]
        visible_mask = (key_pos[None, :] <= query_pos[:, None]) & same_segment
        outputs = lax.map(partial(head_attention, visible_mask=visible_mask, score_scale=score_scale), (q_all[:, block_start:block_end], k_all[:, :block_end], v_all[:, :block_end]))
        pieces.append(outputs.transpose(2, 0, 1, 3).reshape(block_rows, HEADS * DH))
    attended = jnp.concatenate(pieces, axis=0).reshape(2, HALF, HEADS * DH)
    key_cache = key_states.reshape(length, KV_HEADS * DH)
    value_cache = value_states.reshape(length, KV_HEADS * DH)
    return (attended, key_cache, value_cache)
```

```python
import math

import jax
import jax.numpy as jnp
from jax import lax
from jax.experimental import pallas as pl
from jax.experimental.pallas import tpu as pltpu
from jax.sharding import PartitionSpec as P

MESH = pl.DeviceIdType.MESH
DH = 128
GROUPS = 8
ROWS = 192
CTX = 32
HEAD = 8
KEYS = 4 * ROWS
CACHE = 48
TILE = 2
OTHER = -(2.0 ** 20)
LATER = -(2.0 ** 22)
START = -(2.0 ** 23)
SCALE = math.log2(math.e) / math.sqrt(DH)

LOW, HIGH = 0, 1


def transfers():
    out = {}

    def add(name, link, row, dz, half, source):
        out[name] = (link, row, dz, half, source)

    for half, tag in ((LOW, "L"), (HIGH, "H")):
        for d in (1, 2, 3):
            add(f"U{d}{tag}", "up", 0, -d, half, f"U{d - 1}{tag}" if d > 1 else None)
            add(f"D{d}{tag}", "down", 0, d, half, f"D{d - 1}{tag}" if d > 1 else None)
        add(f"Y0{tag}", "y", 1, 0, half, None)
        for d in (1, 2):
            add(f"YU{d}{tag}", "y", 1, -d, half, f"U{d}{tag}")
            add(f"YD{d}{tag}", "y", 1, d, half, f"D{d}{tag}")
        add(f"OU3{tag}", "up", 1, -3, half, f"YU2{tag}")
        add(f"OD3{tag}", "down", 1, 3, half, f"YD2{tag}")
    add("U4L", "up", 0, -4, LOW, "U3L")
    add("D4H", "down", 0, 4, HIGH, "D3H")
    add("OU4L", "up", 1, -4, LOW, "OU3L")
    add("OD4H", "down", 1, 4, HIGH, "OD3H")
    for name in list(out):
        link, row, dz, half, source = out[name]
        add("C" + name, "core", row, dz, half, name)
    add("C0L", "core", 0, 0, LOW, None)
    add("C0H", "core", 0, 0, HIGH, None)
    return {
        name + tag: (link, row, dz, half, kv, source and source + tag)
        for name, (link, row, dz, half, source) in out.items()
        for kv, tag in ((0, "k"), (1, "v"))
    }


TRANSFERS = transfers()
INDEX = {name: i for i, name in enumerate(TRANSFERS)}
FORWARDS = {name: [k for k, v in TRANSFERS.items() if v[5] == name] for name in TRANSFERS}
FIRST = [n + half + kv for half in "LH" for kv in "kv" for n in ("U1", "D1", "Y0", "C0")]

ARRIVALS = [
    ["U1L", "D1L", "Y0L"],
    ["U1H", "D1H", "Y0H"],
    ["U2L", "D2L", "YU1L"],
    ["U2H", "D2H", "YD1L"],
    ["U3L", "D3L", "YU2L"],
    ["U3H", "D3H", "YD2L"],
    ["U4L", "D4H", "YU2H"],
    ["OU3L", "OD3L", "YD2H"],
    ["OU3H", "OD3H", "YU1H"],
    ["OU4L", "OD4H", "YD1H"],
]
OWN, NEAR, FAR, OPP = 0, 1, 2, 3
PLAN = [
    2,
    (OWN, 0, LOW),
    3,
    (NEAR, 0, LOW),
    (NEAR, 0, HIGH),
    4,
    (OWN, 1, LOW),
    5,
    (FAR, 0, LOW),
    (FAR, 0, HIGH),
    6,
    (NEAR, 1, LOW),
    (OPP, 0, LOW),
    7,
    (OPP, 0, HIGH),
    (FAR, 1, LOW),
    8,
    (FAR, 1, HIGH),
    9,
    (OPP, 1, LOW),
    (OWN, 1, HIGH),
    (NEAR, 1, HIGH),
    (OPP, 1, HIGH),
]


REACH = {OWN: (0, 1), NEAR: (1, 2), FAR: (2, 3), OPP: (3, 4)}


def needs(kind, row, half):
    return [
        name
        for name, (link, r, dz, hf, kv, _) in TRANSFERS.items()
        if link == "core" and r == row and hf == half and abs(dz) in REACH[kind]
    ]


def steps_of(plan):
    jobs, before, pending, seen = [], [], [], set(needs(OWN, 0, LOW) + needs(OWN, 0, HIGH))
    for entry in plan:
        if isinstance(entry, int):
            pending.append(entry)
        else:
            jobs.append(entry)
            fresh = [name for name in needs(*entry) if name not in seen]
            seen.update(fresh)
            before.append((pending, fresh))
            pending = []
    assert seen == {name for name in TRANSFERS if TRANSFERS[name][0] == "core"}
    return jobs, before


JOBS, BEFORE = steps_of(PLAN)


def kernel(q_ref, k_ref, v_ref, seg_ref, out_ref, kc_ref, vc_ref, buf, kfeat, qx, acc, peak, send, recv, csend, crecv):
    c = lax.axis_index("ctx")
    h = lax.axis_index("head")
    y, z, core = c // 16, (c % 16) // 2, c % 2

    def index_of(row, zz, kk):
        return row * 16 + (zz % 8) * 2 + kk

    up_to = index_of(y, z + 1, core)
    down_to = index_of(y, z + 7, core)
    y_to = index_of(1 - y, z, core)
    core_to = index_of(y, z, 1 - core)
    target = {"up": up_to, "down": down_to, "y": y_to, "core": core_to}

    barrier = pltpu.get_barrier_semaphore()
    for peer in (up_to, down_to, y_to, core_to):
        pl.semaphore_signal(barrier, inc=1, device_id=(peer, h), device_id_type=MESH)
    for d in range(1, HEAD):
        pl.semaphore_signal(barrier, inc=1, device_id=(c, (h + d) % HEAD), device_id_type=MESH)

    buf[0, c] = k_ref[0]
    buf[1, c] = v_ref[0]
    buf[2, c] = k_ref[1]
    buf[3, c] = v_ref[1]
    pl.semaphore_wait(barrier, 4 + HEAD - 1)

    def copy_of(name):
        link, row, dz, half, kv, _ = TRANSFERS[name]
        if link == "up":
            block = index_of(y if row == 0 else 1 - y, z + dz + 1 + 8, core)
        elif link == "down":
            block = index_of(y if row == 0 else 1 - y, z + dz - 1 + 8, core)
        elif link == "y":
            block = index_of(y, z + dz + 8, core)
        else:
            block = index_of(y if row == 0 else 1 - y, z + dz + 8, core)
        ref = buf.at[2 * half + kv, block]
        i = INDEX[name]
        return pltpu.make_async_remote_copy(
            src_ref=ref,
            dst_ref=ref,
            send_sem=send.at[i],
            recv_sem=recv.at[i],
            device_id=(target[link], h),
            device_id_type=MESH,
        )

    for name in FIRST:
        copy_of(name).start()

    def arrive(names):
        for name in [n + kv for kv in "kv" for n in names]:
            copy_of(name).wait_recv()
            for onward in FORWARDS[name]:
                copy_of(onward).start()

    seg = seg_ref[...]
    lane = lax.broadcasted_iota(jnp.int32, (1, DH), 1)
    low = jnp.zeros((1, DH), jnp.float32)
    high = jnp.zeros((1, DH), jnp.float32)
    for s in range(4):
        below = jnp.sum(jnp.where(seg < s, 1.0, 0.0), axis=(0, 1), keepdims=True)
        upto = jnp.sum(jnp.where(seg <= s, 1.0, 0.0), axis=(0, 1), keepdims=True)
        low = jnp.where(lane == s, below, low)
        high = jnp.where(lane == s, upto, high)
    used = jnp.where(lane < 4, 1.0, 0.0)

    def inside(first, rows):
        at = (lax.broadcasted_iota(jnp.int32, (rows, DH), 0) + first).astype(jnp.float32)
        return jnp.where((at >= low) & (at < high), 1.0, 0.0)

    def prepare_keys(i, carry):
        kfeat[i] = inside(i * ROWS, ROWS).astype(jnp.bfloat16)
        return carry

    for s in range(2):
        feature = ((used - inside(s * CTX * ROWS + c * ROWS, ROWS)) * OTHER).astype(jnp.bfloat16)
        for g in range(GROUPS):
            qx[s, g, :, :DH] = q_ref[s, :, g * DH : (g + 1) * DH]
            qx[s, g, :, DH:] = feature
    lax.fori_loop(0, 2 * CTX, prepare_keys, 0)
    peak[...] = jnp.full(peak.shape, START, jnp.float32)
    acc[...] = jnp.zeros(acc.shape, jnp.float32)

    rows = TILE * ROWS
    lanes = KEYS // DH
    ones = jnp.ones((KEYS, DH), jnp.bfloat16)

    def attend(qs, half, block, causal):
        first = block * 4
        keys = buf[2 * half, pl.ds(first, 4)].reshape(KEYS, DH)
        values = buf[2 * half + 1, pl.ds(first, 4)].reshape(KEYS, DH)
        features = kfeat[pl.ds(half * CTX + first, 4)].reshape(KEYS, DH)
        keys = jnp.concatenate([keys, features], axis=1)
        values = jnp.concatenate([values, ones], axis=1)
        if causal:
            at = c * ROWS - first * ROWS
            row = lax.broadcasted_iota(jnp.int32, (ROWS, KEYS), 0) + at
            col = lax.broadcasted_iota(jnp.int32, (ROWS, KEYS), 1)
            seen = jnp.concatenate([row >= col] * TILE, axis=0)
        for t in range(GROUPS // TILE):
            heads = pl.ds(t * TILE, TILE)
            queries = qx[qs, heads].reshape(rows, 2 * DH)
            scores = lax.dot_general(
                queries, keys, (((1,), (1,)), ((), ())), preferred_element_type=jnp.float32
            )
            if causal:
                scores = jnp.where(seen, scores, LATER)
            parts = [scores[:, i * DH : (i + 1) * DH] for i in range(lanes)]
            top = parts[0]
            for part in parts[1:]:
                top = jnp.maximum(top, part)
            old = peak[qs, heads].reshape(rows, DH)
            new = jnp.maximum(old, jnp.max(top, axis=1, keepdims=True))
            weights = jnp.concatenate(
                [jnp.exp2((part - new) * SCALE).astype(jnp.bfloat16) for part in parts], axis=1
            )
            factor = jnp.exp2((old - new) * SCALE)
            product = jnp.dot(weights, values, preferred_element_type=jnp.float32)
            held = acc[qs, heads].reshape(rows, 2 * DH)
            held = held * jnp.concatenate([factor, factor], axis=1) + product
            acc[qs, heads] = held.reshape(TILE, ROWS, 2 * DH)
            peak[qs, heads] = new.reshape(TILE, ROWS, DH)

    zb = z // 2
    own = y * 4 + zb
    toward = 1 - 2 * (z % 2)

    arrive(ARRIVALS[0])
    arrive(ARRIVALS[1])
    for name in needs(OWN, 0, LOW) + needs(OWN, 0, HIGH):
        copy_of(name).wait_recv()

    def own_step(half, carry):
        attend(half, half, own, True)
        return carry

    lax.fori_loop(0, 2, own_step, 0)

    def step_body(step, carry):
        def pick(values):
            value = jnp.int32(values[0])
            for i in range(1, len(values)):
                if values[i] != values[0]:
                    value = jnp.where(step == i, jnp.int32(values[i]), value)
            return value

        for i, (events, names) in enumerate(BEFORE):
            if events or names:

                @pl.when(step == i)
                def _(events=events, names=names):
                    for event in events:
                        arrive(ARRIVALS[event])
                    for name in names:
                        copy_of(name).wait_recv()

        row = pick([job[1] for job in JOBS])
        half = pick([job[2] for job in JOBS])
        move = pick([{OWN: 0, NEAR: 0, FAR: 0, OPP: 2}[job[0]] for job in JOBS]) + toward * pick(
            [{OWN: 0, NEAR: -1, FAR: 1, OPP: 0}[job[0]] for job in JOBS]
        )
        block = jnp.where(row == 0, y, 1 - y) * 4 + (zb + move + 4) % 4
        qs = jnp.where(jnp.logical_or(half == 1, block >= own), 1, 0)

        @pl.when(jnp.logical_or(half == 0, block < own))
        def _():
            attend(qs, half, block, False)

        return carry

    lax.fori_loop(0, len(JOBS), step_body, 0)

    half = c // 16

    def cache_source(kv, to):
        return buf.at[2 * half + kv, 2 * (c % 16) + to // 4, pl.ds(pl.multiple_of(CACHE * (to % 4), 16), CACHE)]

    columns = pl.ds(pl.multiple_of(h * DH, DH), DH)

    def cache_copies(d):
        to = (h + d) % HEAD
        return [
            pltpu.make_async_remote_copy(
                src_ref=cache_source(kv, to),
                dst_ref=ref.at[:, columns],
                send_sem=csend.at[kv, d],
                recv_sem=crecv.at[kv, d],
                device_id=(c, to),
                device_id_type=MESH,
            )
            for kv, ref in ((0, kc_ref), (1, vc_ref))
        ]

    for d in range(1, HEAD):
        for copy in cache_copies(d):
            copy.start()
    for kv, ref in ((0, kc_ref), (1, vc_ref)):
        ref[:, columns] = buf[2 * half + kv, 2 * (c % 16) + h // 4, pl.ds(pl.multiple_of(CACHE * (h % 4), 16), CACHE)]

    def finish(g, carry):
        for s in range(2):
            held = acc[s, g]
            out_ref[s, :, pl.ds(pl.multiple_of(g * DH, DH), DH)] = (held[:, :DH] / held[:, DH:]).astype(jnp.bfloat16)
        return carry

    lax.fori_loop(0, GROUPS, finish, 0)

    for name in TRANSFERS:
        copy_of(name).wait_send()
    for d in range(1, HEAD):
        for copy in cache_copies(d):
            copy.wait()


def body(queries, key_states, value_states, segment_ids):
    vmem = pl.BlockSpec(memory_space=pltpu.VMEM)
    count = len(TRANSFERS)
    return pl.pallas_call(
        kernel,
        out_shape=(
            jax.ShapeDtypeStruct((2, ROWS, GROUPS * DH), jnp.bfloat16),
            jax.ShapeDtypeStruct((CACHE, HEAD * DH), jnp.bfloat16),
            jax.ShapeDtypeStruct((CACHE, HEAD * DH), jnp.bfloat16),
        ),
        in_specs=[vmem] * 4,
        out_specs=(vmem,) * 3,
        scratch_shapes=[
            pltpu.VMEM((4, CTX, ROWS, DH), jnp.bfloat16),
            pltpu.VMEM((2 * CTX, ROWS, DH), jnp.bfloat16),
            pltpu.VMEM((2, GROUPS, ROWS, 2 * DH), jnp.bfloat16),
            pltpu.VMEM((2, GROUPS, ROWS, 2 * DH), jnp.float32),
            pltpu.VMEM((2, GROUPS, ROWS, DH), jnp.float32),
            pltpu.SemaphoreType.DMA((count,)),
            pltpu.SemaphoreType.DMA((count,)),
            pltpu.SemaphoreType.DMA((2, HEAD)),
            pltpu.SemaphoreType.DMA((2, HEAD)),
        ],
        compiler_params=pltpu.CompilerParams(
            collective_id=0, has_side_effects=True, vmem_limit_bytes=56 * 1024 * 1024
        ),
        name="attend_gather",
    )(queries, key_states, value_states, segment_ids.reshape(-1, DH))


def solution(mesh):
    in_specs = (P(None, "ctx", "head"), P(None, "ctx", "head"), P(None, "ctx", "head"), P())
    out_specs = (P(None, "ctx", "head"), P(("ctx", "head"), None), P(("ctx", "head"), None))
    return jax.shard_map(body, mesh=mesh, in_specs=in_specs, out_specs=out_specs, check_vma=False)
```

```python
import math

import jax
import jax.numpy as jnp
from jax import lax
from jax.experimental import pallas as pl
from jax.experimental.pallas import tpu as pltpu
from jax.sharding import PartitionSpec as P

MESH = pl.DeviceIdType.MESH
DH = 128
GROUPS = 8
ROWS = 192
CTX = 32
HEAD = 8
KEYS = 4 * ROWS
CACHE = 48
TILE = 2
OTHER = -(2.0 ** 20)
LATER = -(2.0 ** 22)
START = -(2.0 ** 23)
SCALE = math.log2(math.e) / math.sqrt(DH)

LOW, HIGH = 0, 1


def transfers():
    out = {}

    def add(name, link, row, dz, half, source):
        out[name] = (link, row, dz, half, source)

    for half, tag in ((LOW, "L"), (HIGH, "H")):
        for d in (1, 2, 3):
            add(f"U{d}{tag}", "up", 0, -d, half, f"U{d - 1}{tag}" if d > 1 else None)
            add(f"D{d}{tag}", "down", 0, d, half, f"D{d - 1}{tag}" if d > 1 else None)
        add(f"Y0{tag}", "y", 1, 0, half, None)
        for d in (1, 2):
            add(f"YU{d}{tag}", "y", 1, -d, half, f"U{d}{tag}")
            add(f"YD{d}{tag}", "y", 1, d, half, f"D{d}{tag}")
        add(f"OU3{tag}", "up", 1, -3, half, f"YU2{tag}")
        add(f"OD3{tag}", "down", 1, 3, half, f"YD2{tag}")
    add("U4L", "up", 0, -4, LOW, "U3L")
    add("D4H", "down", 0, 4, HIGH, "D3H")
    add("OU4L", "up", 1, -4, LOW, "OU3L")
    add("OD4H", "down", 1, 4, HIGH, "OD3H")
    for name in list(out):
        link, row, dz, half, source = out[name]
        add("C" + name, "core", row, dz, half, name)
    add("C0L", "core", 0, 0, LOW, None)
    add("C0H", "core", 0, 0, HIGH, None)
    return {
        name + tag: (link, row, dz, half, kv, source and source + tag)
        for name, (link, row, dz, half, source) in out.items()
        for kv, tag in ((0, "k"), (1, "v"))
    }


TRANSFERS = transfers()
INDEX = {name: i for i, name in enumerate(TRANSFERS)}
FORWARDS = {name: [k for k, v in TRANSFERS.items() if v[5] == name] for name in TRANSFERS}
FIRST = [n + half + kv for half in "LH" for kv in "kv" for n in ("U1", "D1", "Y0", "C0")]

ARRIVALS = [
    ["U1L", "D1L", "Y0L"],
    ["U1H", "D1H", "Y0H"],
    ["U2L", "D2L", "YU1L"],
    ["U2H", "D2H", "YD1L"],
    ["U3L", "D3L", "YU2L"],
    ["U3H", "D3H", "YD2L"],
    ["U4L", "D4H", "YU2H"],
    ["OU3L", "OD3L", "YD2H"],
    ["OU3H", "OD3H", "YU1H"],
    ["OU4L", "OD4H", "YD1H"],
]
OWN, NEAR, FAR, OPP = 0, 1, 2, 3
PLAN = [
    2,
    3,
    (OWN, 0, LOW),
    (NEAR, 0, LOW),
    (NEAR, 0, HIGH),
    (OWN, 1, LOW),
    4,
    5,
    (FAR, 0, LOW),
    (FAR, 0, HIGH),
    (NEAR, 1, LOW),
    6,
    7,
    (OPP, 0, LOW),
    (OPP, 0, HIGH),
    (FAR, 1, LOW),
    8,
    9,
    (FAR, 1, HIGH),
    (OPP, 1, LOW),
    (OWN, 1, HIGH),
    (NEAR, 1, HIGH),
    (OPP, 1, HIGH),
]


REACH = {OWN: (0, 1), NEAR: (1, 2), FAR: (2, 3), OPP: (3, 4)}


def needs(kind, row, half):
    return [
        name
        for name, (link, r, dz, hf, kv, _) in TRANSFERS.items()
        if link == "core" and r == row and hf == half and abs(dz) in REACH[kind]
    ]


def steps_of(plan):
    jobs, before, pending, seen = [], [], [], set(needs(OWN, 0, LOW) + needs(OWN, 0, HIGH))
    for entry in plan:
        if isinstance(entry, int):
            pending.append(entry)
        else:
            jobs.append(entry)
            fresh = [name for name in needs(*entry) if name not in seen]
            seen.update(fresh)
            before.append((pending, fresh))
            pending = []
    assert seen == {name for name in TRANSFERS if TRANSFERS[name][0] == "core"}
    return jobs, before


JOBS, BEFORE = steps_of(PLAN)


def kernel(q_ref, k_ref, v_ref, seg_ref, out_ref, kc_ref, vc_ref, buf, kfeat, qx, acc, peak, send, recv, csend, crecv):
    c = lax.axis_index("ctx")
    h = lax.axis_index("head")
    y, z, core = c // 16, (c % 16) // 2, c % 2

    def index_of(row, zz, kk):
        return row * 16 + (zz % 8) * 2 + kk

    up_to = index_of(y, z + 1, core)
    down_to = index_of(y, z + 7, core)
    y_to = index_of(1 - y, z, core)
    core_to = index_of(y, z, 1 - core)
    target = {"up": up_to, "down": down_to, "y": y_to, "core": core_to}

    barrier = pltpu.get_barrier_semaphore()
    for peer in (up_to, down_to, y_to, core_to):
        pl.semaphore_signal(barrier, inc=1, device_id=(peer, h), device_id_type=MESH)
    for d in range(1, HEAD):
        pl.semaphore_signal(barrier, inc=1, device_id=(c, (h + d) % HEAD), device_id_type=MESH)

    buf[0, c] = k_ref[0]
    buf[1, c] = v_ref[0]
    buf[2, c] = k_ref[1]
    buf[3, c] = v_ref[1]
    pl.semaphore_wait(barrier, 4 + HEAD - 1)

    def copy_of(name):
        link, row, dz, half, kv, _ = TRANSFERS[name]
        if link == "up":
            block = index_of(y if row == 0 else 1 - y, z + dz + 1 + 8, core)
        elif link == "down":
            block = index_of(y if row == 0 else 1 - y, z + dz - 1 + 8, core)
        elif link == "y":
            block = index_of(y, z + dz + 8, core)
        else:
            block = index_of(y if row == 0 else 1 - y, z + dz + 8, core)
        ref = buf.at[2 * half + kv, block]
        i = INDEX[name]
        return pltpu.make_async_remote_copy(
            src_ref=ref,
            dst_ref=ref,
            send_sem=send.at[i],
            recv_sem=recv.at[i],
            device_id=(target[link], h),
            device_id_type=MESH,
        )

    for name in FIRST:
        copy_of(name).start()

    def arrive(names):
        for name in [n + kv for kv in "kv" for n in names]:
            copy_of(name).wait_recv()
            for onward in FORWARDS[name]:
                copy_of(onward).start()

    seg = seg_ref[...]
    lane = lax.broadcasted_iota(jnp.int32, (1, DH), 1)
    low = jnp.zeros((1, DH), jnp.float32)
    high = jnp.zeros((1, DH), jnp.float32)
    for s in range(4):
        below = jnp.sum(jnp.where(seg < s, 1.0, 0.0), axis=(0, 1), keepdims=True)
        upto = jnp.sum(jnp.where(seg <= s, 1.0, 0.0), axis=(0, 1), keepdims=True)
        low = jnp.where(lane == s, below, low)
        high = jnp.where(lane == s, upto, high)
    used = jnp.where(lane < 4, 1.0, 0.0)

    def inside(first, rows):
        at = (lax.broadcasted_iota(jnp.int32, (rows, DH), 0) + first).astype(jnp.float32)
        return jnp.where((at >= low) & (at < high), 1.0, 0.0)

    def prepare_keys(i, carry):
        kfeat[i] = inside(i * ROWS, ROWS).astype(jnp.bfloat16)
        return carry

    for s in range(2):
        feature = ((used - inside(s * CTX * ROWS + c * ROWS, ROWS)) * OTHER).astype(jnp.bfloat16)
        for g in range(GROUPS):
            qx[s, g, :, :DH] = q_ref[s, :, g * DH : (g + 1) * DH]
            qx[s, g, :, DH:] = feature
    lax.fori_loop(0, 2 * CTX, prepare_keys, 0)
    peak[...] = jnp.full(peak.shape, START, jnp.float32)
    acc[...] = jnp.zeros(acc.shape, jnp.float32)

    rows = TILE * ROWS
    lanes = KEYS // DH
    ones = jnp.ones((KEYS, DH), jnp.bfloat16)

    def attend(qs, half, block, causal):
        first = block * 4
        keys = buf[2 * half, pl.ds(first, 4)].reshape(KEYS, DH)
        values = buf[2 * half + 1, pl.ds(first, 4)].reshape(KEYS, DH)
        features = kfeat[pl.ds(half * CTX + first, 4)].reshape(KEYS, DH)
        keys = jnp.concatenate([keys, features], axis=1)
        values = jnp.concatenate([values, ones], axis=1)
        if causal:
            at = c * ROWS - first * ROWS
            row = lax.broadcasted_iota(jnp.int32, (ROWS, KEYS), 0) + at
            col = lax.broadcasted_iota(jnp.int32, (ROWS, KEYS), 1)
            seen = jnp.concatenate([row >= col] * TILE, axis=0)
        for t in range(GROUPS // TILE):
            heads = pl.ds(t * TILE, TILE)
            queries = qx[qs, heads].reshape(rows, 2 * DH)
            scores = lax.dot_general(
                queries, keys, (((1,), (1,)), ((), ())), preferred_element_type=jnp.float32
            )
            if causal:
                scores = jnp.where(seen, scores, LATER)
            parts = [scores[:, i * DH : (i + 1) * DH] for i in range(lanes)]
            top = parts[0]
            for part in parts[1:]:
                top = jnp.maximum(top, part)
            old = peak[qs, heads].reshape(rows, DH)
            new = jnp.maximum(old, jnp.max(top, axis=1, keepdims=True))
            weights = jnp.concatenate(
                [jnp.exp2((part - new) * SCALE).astype(jnp.bfloat16) for part in parts], axis=1
            )
            factor = jnp.exp2((old - new) * SCALE)
            product = jnp.dot(weights, values, preferred_element_type=jnp.float32)
            held = acc[qs, heads].reshape(rows, 2 * DH)
            held = held * jnp.concatenate([factor, factor], axis=1) + product
            acc[qs, heads] = held.reshape(TILE, ROWS, 2 * DH)
            peak[qs, heads] = new.reshape(TILE, ROWS, DH)

    zb = z // 2
    own = y * 4 + zb
    toward = 1 - 2 * (z % 2)

    arrive(ARRIVALS[0])
    arrive(ARRIVALS[1])
    for name in needs(OWN, 0, LOW) + needs(OWN, 0, HIGH):
        copy_of(name).wait_recv()

    def own_step(half, carry):
        attend(half, half, own, True)
        return carry

    lax.fori_loop(0, 2, own_step, 0)

    def step_body(step, carry):
        def pick(values):
            value = jnp.int32(values[0])
            for i in range(1, len(values)):
                if values[i] != values[0]:
                    value = jnp.where(step == i, jnp.int32(values[i]), value)
            return value

        for i, (events, names) in enumerate(BEFORE):
            if events or names:

                @pl.when(step == i)
                def _(events=events, names=names):
                    for event in events:
                        arrive(ARRIVALS[event])
                    for name in names:
                        copy_of(name).wait_recv()

        row = pick([job[1] for job in JOBS])
        half = pick([job[2] for job in JOBS])
        move = pick([{OWN: 0, NEAR: 0, FAR: 0, OPP: 2}[job[0]] for job in JOBS]) + toward * pick(
            [{OWN: 0, NEAR: -1, FAR: 1, OPP: 0}[job[0]] for job in JOBS]
        )
        block = jnp.where(row == 0, y, 1 - y) * 4 + (zb + move + 4) % 4
        qs = jnp.where(jnp.logical_or(half == 1, block >= own), 1, 0)

        @pl.when(jnp.logical_or(half == 0, block < own))
        def _():
            attend(qs, half, block, False)

        return carry

    lax.fori_loop(0, len(JOBS), step_body, 0)

    half = c // 16

    def cache_source(kv, to):
        return buf.at[2 * half + kv, 2 * (c % 16) + to // 4, pl.ds(pl.multiple_of(CACHE * (to % 4), 16), CACHE)]

    columns = pl.ds(pl.multiple_of(h * DH, DH), DH)

    def cache_copies(d):
        to = (h + d) % HEAD
        return [
            pltpu.make_async_remote_copy(
                src_ref=cache_source(kv, to),
                dst_ref=ref.at[:, columns],
                send_sem=csend.at[kv, d],
                recv_sem=crecv.at[kv, d],
                device_id=(c, to),
                device_id_type=MESH,
            )
            for kv, ref in ((0, kc_ref), (1, vc_ref))
        ]

    for d in range(1, HEAD):
        for copy in cache_copies(d):
            copy.start()
    for kv, ref in ((0, kc_ref), (1, vc_ref)):
        ref[:, columns] = buf[2 * half + kv, 2 * (c % 16) + h // 4, pl.ds(pl.multiple_of(CACHE * (h % 4), 16), CACHE)]

    def finish(g, carry):
        for s in range(2):
            held = acc[s, g]
            out_ref[s, :, pl.ds(pl.multiple_of(g * DH, DH), DH)] = (held[:, :DH] / held[:, DH:]).astype(jnp.bfloat16)
        return carry

    lax.fori_loop(0, GROUPS, finish, 0)

    for name in TRANSFERS:
        copy_of(name).wait_send()
    for d in range(1, HEAD):
        for copy in cache_copies(d):
            copy.wait()


def body(queries, key_states, value_states, segment_ids):
    vmem = pl.BlockSpec(memory_space=pltpu.VMEM)
    count = len(TRANSFERS)
    return pl.pallas_call(
        kernel,
        out_shape=(
            jax.ShapeDtypeStruct((2, ROWS, GROUPS * DH), jnp.bfloat16),
            jax.ShapeDtypeStruct((CACHE, HEAD * DH), jnp.bfloat16),
            jax.ShapeDtypeStruct((CACHE, HEAD * DH), jnp.bfloat16),
        ),
        in_specs=[vmem] * 4,
        out_specs=(vmem,) * 3,
        scratch_shapes=[
            pltpu.VMEM((4, CTX, ROWS, DH), jnp.bfloat16),
            pltpu.VMEM((2 * CTX, ROWS, DH), jnp.bfloat16),
            pltpu.VMEM((2, GROUPS, ROWS, 2 * DH), jnp.bfloat16),
            pltpu.VMEM((2, GROUPS, ROWS, 2 * DH), jnp.float32),
            pltpu.VMEM((2, GROUPS, ROWS, DH), jnp.float32),
            pltpu.SemaphoreType.DMA((count,)),
            pltpu.SemaphoreType.DMA((count,)),
            pltpu.SemaphoreType.DMA((2, HEAD)),
            pltpu.SemaphoreType.DMA((2, HEAD)),
        ],
        compiler_params=pltpu.CompilerParams(
            collective_id=0, has_side_effects=True, vmem_limit_bytes=56 * 1024 * 1024
        ),
        name="attend_gather",
    )(queries, key_states, value_states, segment_ids.reshape(-1, DH))


def solution(mesh):
    in_specs = (P(None, "ctx", "head"), P(None, "ctx", "head"), P(None, "ctx", "head"), P())
    out_specs = (P(None, "ctx", "head"), P(("ctx", "head"), None), P(("ctx", "head"), None))
    return jax.shard_map(body, mesh=mesh, in_specs=in_specs, out_specs=out_specs, check_vma=False)
```

```python
import math

import jax
import jax.numpy as jnp
from jax import lax
from jax.experimental import pallas as pl
from jax.experimental.pallas import tpu as pltpu
from jax.sharding import PartitionSpec as P

MESH = pl.DeviceIdType.MESH
DH = 128
GROUPS = 8
ROWS = 192
CTX = 32
HEAD = 8
KEYS = 4 * ROWS
CACHE = 48
TILE = 2
OTHER = -(2.0 ** 20)
LATER = -(2.0 ** 22)
START = -(2.0 ** 23)
SCALE = math.log2(math.e) / math.sqrt(DH)

LOW, HIGH = 0, 1


def transfers():
    out = {}

    def add(name, link, row, dz, half, source):
        out[name] = (link, row, dz, half, source)

    for half, tag in ((LOW, "L"), (HIGH, "H")):
        for d in (1, 2, 3):
            add(f"U{d}{tag}", "up", 0, -d, half, f"U{d - 1}{tag}" if d > 1 else None)
            add(f"D{d}{tag}", "down", 0, d, half, f"D{d - 1}{tag}" if d > 1 else None)
        add(f"Y0{tag}", "y", 1, 0, half, None)
        for d in (1, 2):
            add(f"YU{d}{tag}", "y", 1, -d, half, f"U{d}{tag}")
            add(f"YD{d}{tag}", "y", 1, d, half, f"D{d}{tag}")
        add(f"OU3{tag}", "up", 1, -3, half, f"YU2{tag}")
        add(f"OD3{tag}", "down", 1, 3, half, f"YD2{tag}")
    add("U4L", "up", 0, -4, LOW, "U3L")
    add("D4H", "down", 0, 4, HIGH, "D3H")
    add("OU4L", "up", 1, -4, LOW, "OU3L")
    add("OD4H", "down", 1, 4, HIGH, "OD3H")
    for name in list(out):
        link, row, dz, half, source = out[name]
        add("C" + name, "core", row, dz, half, name)
    add("C0L", "core", 0, 0, LOW, None)
    add("C0H", "core", 0, 0, HIGH, None)
    return {
        name + tag: (link, row, dz, half, kv, source and source + tag)
        for name, (link, row, dz, half, source) in out.items()
        for kv, tag in ((0, "k"), (1, "v"))
    }


TRANSFERS = transfers()
INDEX = {name: i for i, name in enumerate(TRANSFERS)}
FORWARDS = {name: [k for k, v in TRANSFERS.items() if v[5] == name] for name in TRANSFERS}
ORDERS = (("up", "y", "down"), ("down", "up", "y"))

ARRIVALS = [
    ["U1L", "D1L", "Y0L"],
    ["U1H", "D1H", "Y0H"],
    ["U2L", "D2L", "YU1L"],
    ["U2H", "D2H", "YD1L"],
    ["U3L", "D3L", "YU2L"],
    ["U3H", "D3H", "YD2L"],
    ["U4L", "D4H", "YU2H"],
    ["OU3L", "OD3L", "YD2H"],
    ["OU3H", "OD3H", "YU1H"],
    ["OU4L", "OD4H", "YD1H"],
]
OWN, NEAR, FAR, OPP = 0, 1, 2, 3
PLAN = [
    2,
    3,
    (OWN, 0, LOW),
    (NEAR, 0, LOW),
    (NEAR, 0, HIGH),
    (OWN, 1, LOW),
    4,
    5,
    (FAR, 0, LOW),
    (FAR, 0, HIGH),
    (NEAR, 1, LOW),
    6,
    7,
    (OPP, 0, LOW),
    (OPP, 0, HIGH),
    (FAR, 1, LOW),
    8,
    9,
    (FAR, 1, HIGH),
    (OPP, 1, LOW),
    (OWN, 1, HIGH),
    (NEAR, 1, HIGH),
    (OPP, 1, HIGH),
]


REACH = {OWN: (0, 1), NEAR: (1, 2), FAR: (2, 3), OPP: (3, 4)}


def needs(kind, row, half):
    return [
        name
        for name, (link, r, dz, hf, kv, _) in TRANSFERS.items()
        if link == "core" and r == row and hf == half and abs(dz) in REACH[kind]
    ]


def steps_of(plan):
    jobs, before, pending, seen = [], [], [], set(needs(OWN, 0, LOW) + needs(OWN, 0, HIGH))
    for entry in plan:
        if isinstance(entry, int):
            pending.append(entry)
        else:
            jobs.append(entry)
            fresh = [name for name in needs(*entry) if name not in seen]
            seen.update(fresh)
            before.append((pending, fresh))
            pending = []
    assert seen == {name for name in TRANSFERS if TRANSFERS[name][0] == "core"}
    return jobs, before


JOBS, BEFORE = steps_of(PLAN)


def kernel(q_ref, k_ref, v_ref, seg_ref, out_ref, kc_ref, vc_ref, buf, kfeat, qx, acc, peak, send, recv, csend, crecv):
    c = lax.axis_index("ctx")
    h = lax.axis_index("head")
    y, z, core = c // 16, (c % 16) // 2, c % 2

    def index_of(row, zz, kk):
        return row * 16 + (zz % 8) * 2 + kk

    up_to = index_of(y, z + 1, core)
    down_to = index_of(y, z + 7, core)
    y_to = index_of(1 - y, z, core)
    core_to = index_of(y, z, 1 - core)
    target = {"up": up_to, "down": down_to, "y": y_to, "core": core_to}

    barrier = pltpu.get_barrier_semaphore()
    for peer in (up_to, down_to, y_to, core_to):
        pl.semaphore_signal(barrier, inc=1, device_id=(peer, h), device_id_type=MESH)
    for d in range(1, HEAD):
        pl.semaphore_signal(barrier, inc=1, device_id=(c, (h + d) % HEAD), device_id_type=MESH)

    buf[0, c] = k_ref[0]
    buf[1, c] = v_ref[0]
    buf[2, c] = k_ref[1]
    buf[3, c] = v_ref[1]
    pl.semaphore_wait(barrier, 4 + HEAD - 1)

    def copy_of(name):
        link, row, dz, half, kv, _ = TRANSFERS[name]
        if link == "up":
            block = index_of(y if row == 0 else 1 - y, z + dz + 1 + 8, core)
        elif link == "down":
            block = index_of(y if row == 0 else 1 - y, z + dz - 1 + 8, core)
        elif link == "y":
            block = index_of(y, z + dz + 8, core)
        else:
            block = index_of(y if row == 0 else 1 - y, z + dz + 8, core)
        ref = buf.at[2 * half + kv, block]
        i = INDEX[name]
        return pltpu.make_async_remote_copy(
            src_ref=ref,
            dst_ref=ref,
            send_sem=send.at[i],
            recv_sem=recv.at[i],
            device_id=(target[link], h),
            device_id_type=MESH,
        )

    def by_core(function):
        for which, order in enumerate(ORDERS):
            pl.when(core == which)(lambda order=order: function(order))

    def link_order(names, order):
        return sorted(names, key=lambda name: (name[-1], order.index(TRANSFERS[name][0]) if TRANSFERS[name][0] in order else 3))

    @by_core
    def _(order):
        for half in "LH":
            first = [n + half + kv for kv in "kv" for n in ("U1", "D1", "Y0")]
            for name in link_order(first, order):
                copy_of(name).start()
            for kv in "kv":
                copy_of("C0" + half + kv).start()

    def arrive(names):
        names = [n + kv for kv in "kv" for n in names]

        @by_core
        def _(order):
            for name in link_order(names, order):
                copy_of(name).wait_recv()
                for onward in link_order(FORWARDS[name], order):
                    if TRANSFERS[onward][0] != "core":
                        copy_of(onward).start()
            for name in names:
                copy_of("C" + name).start()

    seg = seg_ref[...]
    lane = lax.broadcasted_iota(jnp.int32, (1, DH), 1)
    low = jnp.zeros((1, DH), jnp.float32)
    high = jnp.zeros((1, DH), jnp.float32)
    for s in range(4):
        below = jnp.sum(jnp.where(seg < s, 1.0, 0.0), axis=(0, 1), keepdims=True)
        upto = jnp.sum(jnp.where(seg <= s, 1.0, 0.0), axis=(0, 1), keepdims=True)
        low = jnp.where(lane == s, below, low)
        high = jnp.where(lane == s, upto, high)
    used = jnp.where(lane < 4, 1.0, 0.0)

    def inside(first, rows):
        at = (lax.broadcasted_iota(jnp.int32, (rows, DH), 0) + first).astype(jnp.float32)
        return jnp.where((at >= low) & (at < high), 1.0, 0.0)

    def prepare_keys(i, carry):
        kfeat[i] = inside(i * ROWS, ROWS).astype(jnp.bfloat16)
        return carry

    for s in range(2):
        feature = ((used - inside(s * CTX * ROWS + c * ROWS, ROWS)) * OTHER).astype(jnp.bfloat16)
        for g in range(GROUPS):
            qx[s, g, :, :DH] = q_ref[s, :, g * DH : (g + 1) * DH]
            qx[s, g, :, DH:] = feature
    lax.fori_loop(0, 2 * CTX, prepare_keys, 0)
    peak[...] = jnp.full(peak.shape, START, jnp.float32)
    acc[...] = jnp.zeros(acc.shape, jnp.float32)

    rows = TILE * ROWS
    lanes = KEYS // DH
    ones = jnp.ones((KEYS, DH), jnp.bfloat16)

    def attend(qs, half, block, causal):
        first = block * 4
        keys = buf[2 * half, pl.ds(first, 4)].reshape(KEYS, DH)
        values = buf[2 * half + 1, pl.ds(first, 4)].reshape(KEYS, DH)
        features = kfeat[pl.ds(half * CTX + first, 4)].reshape(KEYS, DH)
        keys = jnp.concatenate([keys, features], axis=1)
        values = jnp.concatenate([values, ones], axis=1)
        if causal:
            at = c * ROWS - first * ROWS
            row = lax.broadcasted_iota(jnp.int32, (ROWS, KEYS), 0) + at
            col = lax.broadcasted_iota(jnp.int32, (ROWS, KEYS), 1)
            seen = jnp.concatenate([row >= col] * TILE, axis=0)
        for t in range(GROUPS // TILE):
            heads = pl.ds(t * TILE, TILE)
            queries = qx[qs, heads].reshape(rows, 2 * DH)
            scores = lax.dot_general(
                queries, keys, (((1,), (1,)), ((), ())), preferred_element_type=jnp.float32
            )
            if causal:
                scores = jnp.where(seen, scores, LATER)
            parts = [scores[:, i * DH : (i + 1) * DH] for i in range(lanes)]
            top = parts[0]
            for part in parts[1:]:
                top = jnp.maximum(top, part)
            old = peak[qs, heads].reshape(rows, DH)
            new = jnp.maximum(old, jnp.max(top, axis=1, keepdims=True))
            weights = jnp.concatenate(
                [jnp.exp2((part - new) * SCALE).astype(jnp.bfloat16) for part in parts], axis=1
            )
            factor = jnp.exp2((old - new) * SCALE)
            product = jnp.dot(weights, values, preferred_element_type=jnp.float32)
            held = acc[qs, heads].reshape(rows, 2 * DH)
            held = held * jnp.concatenate([factor, factor], axis=1) + product
            acc[qs, heads] = held.reshape(TILE, ROWS, 2 * DH)
            peak[qs, heads] = new.reshape(TILE, ROWS, DH)

    zb = z // 2
    own = y * 4 + zb
    toward = 1 - 2 * (z % 2)

    arrive(ARRIVALS[0])
    arrive(ARRIVALS[1])
    for name in needs(OWN, 0, LOW) + needs(OWN, 0, HIGH):
        copy_of(name).wait_recv()

    def own_step(half, carry):
        attend(half, half, own, True)
        return carry

    lax.fori_loop(0, 2, own_step, 0)

    def step_body(step, carry):
        def pick(values):
            value = jnp.int32(values[0])
            for i in range(1, len(values)):
                if values[i] != values[0]:
                    value = jnp.where(step == i, jnp.int32(values[i]), value)
            return value

        for i, (events, names) in enumerate(BEFORE):
            if events or names:

                @pl.when(step == i)
                def _(events=events, names=names):
                    for event in events:
                        arrive(ARRIVALS[event])
                    for name in names:
                        copy_of(name).wait_recv()

        row = pick([job[1] for job in JOBS])
        half = pick([job[2] for job in JOBS])
        move = pick([{OWN: 0, NEAR: 0, FAR: 0, OPP: 2}[job[0]] for job in JOBS]) + toward * pick(
            [{OWN: 0, NEAR: -1, FAR: 1, OPP: 0}[job[0]] for job in JOBS]
        )
        block = jnp.where(row == 0, y, 1 - y) * 4 + (zb + move + 4) % 4
        qs = jnp.where(jnp.logical_or(half == 1, block >= own), 1, 0)

        @pl.when(jnp.logical_or(half == 0, block < own))
        def _():
            attend(qs, half, block, False)

        return carry

    lax.fori_loop(0, len(JOBS), step_body, 0)

    half = c // 16

    def cache_source(kv, to):
        return buf.at[2 * half + kv, 2 * (c % 16) + to // 4, pl.ds(pl.multiple_of(CACHE * (to % 4), 16), CACHE)]

    columns = pl.ds(pl.multiple_of(h * DH, DH), DH)

    def cache_copies(d):
        to = (h + d) % HEAD
        return [
            pltpu.make_async_remote_copy(
                src_ref=cache_source(kv, to),
                dst_ref=ref.at[:, columns],
                send_sem=csend.at[kv, d],
                recv_sem=crecv.at[kv, d],
                device_id=(c, to),
                device_id_type=MESH,
            )
            for kv, ref in ((0, kc_ref), (1, vc_ref))
        ]

    for d in range(1, HEAD):
        for copy in cache_copies(d):
            copy.start()
    for kv, ref in ((0, kc_ref), (1, vc_ref)):
        ref[:, columns] = buf[2 * half + kv, 2 * (c % 16) + h // 4, pl.ds(pl.multiple_of(CACHE * (h % 4), 16), CACHE)]

    def finish(g, carry):
        for s in range(2):
            held = acc[s, g]
            out_ref[s, :, pl.ds(pl.multiple_of(g * DH, DH), DH)] = (held[:, :DH] / held[:, DH:]).astype(jnp.bfloat16)
        return carry

    lax.fori_loop(0, GROUPS, finish, 0)

    for name in TRANSFERS:
        copy_of(name).wait_send()
    for d in range(1, HEAD):
        for copy in cache_copies(d):
            copy.wait()


def body(queries, key_states, value_states, segment_ids):
    vmem = pl.BlockSpec(memory_space=pltpu.VMEM)
    count = len(TRANSFERS)
    return pl.pallas_call(
        kernel,
        out_shape=(
            jax.ShapeDtypeStruct((2, ROWS, GROUPS * DH), jnp.bfloat16),
            jax.ShapeDtypeStruct((CACHE, HEAD * DH), jnp.bfloat16),
            jax.ShapeDtypeStruct((CACHE, HEAD * DH), jnp.bfloat16),
        ),
        in_specs=[vmem] * 4,
        out_specs=(vmem,) * 3,
        scratch_shapes=[
            pltpu.VMEM((4, CTX, ROWS, DH), jnp.bfloat16),
            pltpu.VMEM((2 * CTX, ROWS, DH), jnp.bfloat16),
            pltpu.VMEM((2, GROUPS, ROWS, 2 * DH), jnp.bfloat16),
            pltpu.VMEM((2, GROUPS, ROWS, 2 * DH), jnp.float32),
            pltpu.VMEM((2, GROUPS, ROWS, DH), jnp.float32),
            pltpu.SemaphoreType.DMA((count,)),
            pltpu.SemaphoreType.DMA((count,)),
            pltpu.SemaphoreType.DMA((2, HEAD)),
            pltpu.SemaphoreType.DMA((2, HEAD)),
        ],
        compiler_params=pltpu.CompilerParams(
            collective_id=0, has_side_effects=True, vmem_limit_bytes=56 * 1024 * 1024
        ),
        name="attend_gather",
    )(queries, key_states, value_states, segment_ids.reshape(-1, DH))


def solution(mesh):
    in_specs = (P(None, "ctx", "head"), P(None, "ctx", "head"), P(None, "ctx", "head"), P())
    out_specs = (P(None, "ctx", "head"), P(("ctx", "head"), None), P(("ctx", "head"), None))
    return jax.shard_map(body, mesh=mesh, in_specs=in_specs, out_specs=out_specs, check_vma=False)
```

```python
import math

import jax
import jax.numpy as jnp
from jax import lax
from jax.experimental import pallas as pl
from jax.experimental.pallas import tpu as pltpu
from jax.sharding import PartitionSpec as P

MESH = pl.DeviceIdType.MESH
DH = 128
GROUPS = 8
ROWS = 192
CTX = 32
HEAD = 8
KEYS = 4 * ROWS
CACHE = 48
TILE = 4
OTHER = -(2.0 ** 20)
LATER = -(2.0 ** 22)
START = -(2.0 ** 23)
SCALE = math.log2(math.e) / math.sqrt(DH)

LOW, HIGH = 0, 1


def transfers():
    out = {}

    def add(name, link, row, dz, half, source):
        out[name] = (link, row, dz, half, source)

    for half, tag in ((LOW, "L"), (HIGH, "H")):
        for d in (1, 2, 3):
            add(f"U{d}{tag}", "up", 0, -d, half, f"U{d - 1}{tag}" if d > 1 else None)
            add(f"D{d}{tag}", "down", 0, d, half, f"D{d - 1}{tag}" if d > 1 else None)
        add(f"Y0{tag}", "y", 1, 0, half, None)
        for d in (1, 2):
            add(f"YU{d}{tag}", "y", 1, -d, half, f"U{d}{tag}")
            add(f"YD{d}{tag}", "y", 1, d, half, f"D{d}{tag}")
        add(f"OU3{tag}", "up", 1, -3, half, f"YU2{tag}")
        add(f"OD3{tag}", "down", 1, 3, half, f"YD2{tag}")
    add("U4L", "up", 0, -4, LOW, "U3L")
    add("D4H", "down", 0, 4, HIGH, "D3H")
    add("OU4L", "up", 1, -4, LOW, "OU3L")
    add("OD4H", "down", 1, 4, HIGH, "OD3H")
    for name in list(out):
        link, row, dz, half, source = out[name]
        add("C" + name, "core", row, dz, half, name)
    add("C0L", "core", 0, 0, LOW, None)
    add("C0H", "core", 0, 0, HIGH, None)
    return {
        name + tag: (link, row, dz, half, kv, source and source + tag)
        for name, (link, row, dz, half, source) in out.items()
        for kv, tag in ((0, "k"), (1, "v"))
    }


TRANSFERS = transfers()
INDEX = {name: i for i, name in enumerate(TRANSFERS)}
FORWARDS = {name: [k for k, v in TRANSFERS.items() if v[5] == name] for name in TRANSFERS}
ORDERS = (("up", "y", "down"), ("down", "up", "y"))

ARRIVALS = [
    ["U1L", "D1L", "Y0L"],
    ["U1H", "D1H", "Y0H"],
    ["U2L", "D2L", "YU1L"],
    ["U2H", "D2H", "YD1L"],
    ["U3L", "D3L", "YU2L"],
    ["U3H", "D3H", "YD2L"],
    ["U4L", "D4H", "YU2H"],
    ["OU3L", "OD3L", "YD2H"],
    ["OU3H", "OD3H", "YU1H"],
    ["OU4L", "OD4H", "YD1H"],
]
OWN, NEAR, FAR, OPP = 0, 1, 2, 3
PLAN = [
    (OWN, 0, LOW),
    4,
    5,
    (NEAR, 0, LOW),
    (NEAR, 0, HIGH),
    (OWN, 1, LOW),
    6,
    7,
    (FAR, 0, LOW),
    (FAR, 0, HIGH),
    (NEAR, 1, LOW),
    8,
    (OPP, 0, LOW),
    (OPP, 0, HIGH),
    (FAR, 1, LOW),
    9,
    (FAR, 1, HIGH),
    (OWN, 1, HIGH),
    (OPP, 1, LOW),
    (NEAR, 1, HIGH),
    (OPP, 1, HIGH),
]


REACH = {OWN: (0, 1), NEAR: (1, 2), FAR: (2, 3), OPP: (3, 4)}


def needs(kind, row, half):
    return [
        name
        for name, (link, r, dz, hf, kv, _) in TRANSFERS.items()
        if link == "core" and r == row and hf == half and abs(dz) in REACH[kind]
    ]


def steps_of(plan):
    jobs, before, pending, seen = [], [], [], set(needs(OWN, 0, LOW) + needs(OWN, 0, HIGH))
    for entry in plan:
        if isinstance(entry, int):
            pending.append(entry)
        else:
            jobs.append(entry)
            fresh = [name for name in needs(*entry) if name not in seen]
            seen.update(fresh)
            before.append((pending, fresh))
            pending = []
    assert seen == {name for name in TRANSFERS if TRANSFERS[name][0] == "core"}
    return jobs, before


JOBS, BEFORE = steps_of(PLAN)


def kernel(q_ref, k_ref, v_ref, seg_ref, out_ref, kc_ref, vc_ref, buf, kfeat, qx, acc, peak, send, recv, csend, crecv):
    c = lax.axis_index("ctx")
    h = lax.axis_index("head")
    y, z, core = c // 16, (c % 16) // 2, c % 2

    def index_of(row, zz, kk):
        return row * 16 + (zz % 8) * 2 + kk

    up_to = index_of(y, z + 1, core)
    down_to = index_of(y, z + 7, core)
    y_to = index_of(1 - y, z, core)
    core_to = index_of(y, z, 1 - core)
    target = {"up": up_to, "down": down_to, "y": y_to, "core": core_to}

    barrier = pltpu.get_barrier_semaphore()
    for peer in (up_to, down_to, y_to, core_to):
        pl.semaphore_signal(barrier, inc=1, device_id=(peer, h), device_id_type=MESH)
    for d in range(1, HEAD):
        pl.semaphore_signal(barrier, inc=1, device_id=(c, (h + d) % HEAD), device_id_type=MESH)

    buf[0, c] = k_ref[0]
    buf[1, c] = v_ref[0]
    buf[2, c] = k_ref[1]
    buf[3, c] = v_ref[1]
    pl.semaphore_wait(barrier, 4 + HEAD - 1)

    def copy_of(name):
        link, row, dz, half, kv, _ = TRANSFERS[name]
        if link == "up":
            block = index_of(y if row == 0 else 1 - y, z + dz + 1 + 8, core)
        elif link == "down":
            block = index_of(y if row == 0 else 1 - y, z + dz - 1 + 8, core)
        elif link == "y":
            block = index_of(y, z + dz + 8, core)
        else:
            block = index_of(y if row == 0 else 1 - y, z + dz + 8, core)
        ref = buf.at[2 * half + kv, block]
        i = INDEX[name]
        return pltpu.make_async_remote_copy(
            src_ref=ref,
            dst_ref=ref,
            send_sem=send.at[i],
            recv_sem=recv.at[i],
            device_id=(target[link], h),
            device_id_type=MESH,
        )

    def by_core(function):
        for which, order in enumerate(ORDERS):
            pl.when(core == which)(lambda order=order: function(order))

    def link_order(names, order):
        return sorted(names, key=lambda name: (name[-1], order.index(TRANSFERS[name][0]) if TRANSFERS[name][0] in order else 3))

    @by_core
    def _(order):
        for half in "LH":
            first = [n + half + kv for kv in "kv" for n in ("U1", "D1", "Y0")]
            for name in link_order(first, order):
                copy_of(name).start()
            for kv in "kv":
                copy_of("C0" + half + kv).start()

    def arrive(names):
        names = [n + kv for kv in "kv" for n in names]

        @by_core
        def _(order):
            for name in link_order(names, order):
                copy_of(name).wait_recv()
                for onward in link_order(FORWARDS[name], order):
                    if TRANSFERS[onward][0] != "core":
                        copy_of(onward).start()
            for name in names:
                copy_of("C" + name).start()

    seg = seg_ref[...]
    lane = lax.broadcasted_iota(jnp.int32, (1, DH), 1)
    low = jnp.zeros((1, DH), jnp.float32)
    high = jnp.zeros((1, DH), jnp.float32)
    for s in range(4):
        below = jnp.sum(jnp.where(seg < s, 1.0, 0.0), axis=(0, 1), keepdims=True)
        upto = jnp.sum(jnp.where(seg <= s, 1.0, 0.0), axis=(0, 1), keepdims=True)
        low = jnp.where(lane == s, below, low)
        high = jnp.where(lane == s, upto, high)
    used = jnp.where(lane < 4, 1.0, 0.0)

    def inside(first, rows):
        at = (lax.broadcasted_iota(jnp.int32, (rows, DH), 0) + first).astype(jnp.float32)
        return jnp.where((at >= low) & (at < high), 1.0, 0.0)

    def prepare_keys(i, carry):
        kfeat[i] = inside(i * ROWS, ROWS).astype(jnp.bfloat16)
        return carry

    for s in range(2):
        feature = ((used - inside(s * CTX * ROWS + c * ROWS, ROWS)) * OTHER).astype(jnp.bfloat16)
        for g in range(GROUPS):
            qx[s, g, :, :DH] = q_ref[s, :, g * DH : (g + 1) * DH]
            qx[s, g, :, DH:] = feature
    lax.fori_loop(0, 2 * CTX, prepare_keys, 0)
    peak[...] = jnp.full(peak.shape, START, jnp.float32)
    acc[...] = jnp.zeros(acc.shape, jnp.float32)

    rows = TILE * ROWS
    lanes = KEYS // DH
    ones = jnp.ones((KEYS, DH), jnp.bfloat16)

    def attend(qs, half, block, causal):
        first = block * 4
        keys = buf[2 * half, pl.ds(first, 4)].reshape(KEYS, DH)
        values = buf[2 * half + 1, pl.ds(first, 4)].reshape(KEYS, DH)
        features = kfeat[pl.ds(half * CTX + first, 4)].reshape(KEYS, DH)
        keys = jnp.concatenate([keys, features], axis=1)
        values = jnp.concatenate([values, ones], axis=1)
        if causal:
            at = c * ROWS - first * ROWS
            row = lax.broadcasted_iota(jnp.int32, (ROWS, KEYS), 0) + at
            col = lax.broadcasted_iota(jnp.int32, (ROWS, KEYS), 1)
            seen = jnp.concatenate([row >= col] * TILE, axis=0)
        def scores_of(t):
            queries = qx[qs, pl.ds(t * TILE, TILE)].reshape(rows, 2 * DH)
            return lax.dot_general(
                queries, keys, (((1,), (1,)), ((), ())), preferred_element_type=jnp.float32
            )

        tiles = GROUPS // TILE
        scores = scores_of(0)
        for t in range(tiles):
            later = scores_of(t + 1) if t + 1 < tiles else None
            heads = pl.ds(t * TILE, TILE)
            if causal:
                scores = jnp.where(seen, scores, LATER)
            parts = [scores[:, i * DH : (i + 1) * DH] for i in range(lanes)]
            top = parts[0]
            for part in parts[1:]:
                top = jnp.maximum(top, part)
            old = peak[qs, heads].reshape(rows, DH)
            new = jnp.maximum(old, jnp.max(top, axis=1, keepdims=True))
            weights = jnp.concatenate(
                [jnp.exp2((part - new) * SCALE).astype(jnp.bfloat16) for part in parts], axis=1
            )
            factor = jnp.exp2((old - new) * SCALE)
            product = jnp.dot(weights, values, preferred_element_type=jnp.float32)
            held = acc[qs, heads].reshape(rows, 2 * DH)
            held = held * jnp.concatenate([factor, factor], axis=1) + product
            acc[qs, heads] = held.reshape(TILE, ROWS, 2 * DH)
            peak[qs, heads] = new.reshape(TILE, ROWS, DH)
            scores = later

    zb = z // 2
    own = y * 4 + zb
    toward = 1 - 2 * (z % 2)

    for names in ARRIVALS[:4]:
        arrive(names)
    for name in needs(OWN, 0, LOW) + needs(OWN, 0, HIGH):
        copy_of(name).wait_recv()

    def own_step(half, carry):
        attend(half, half, own, True)
        return carry

    lax.fori_loop(0, 2, own_step, 0)

    def step_body(step, carry):
        def pick(values):
            value = jnp.int32(values[0])
            for i in range(1, len(values)):
                if values[i] != values[0]:
                    value = jnp.where(step == i, jnp.int32(values[i]), value)
            return value

        for i, (events, names) in enumerate(BEFORE):
            if events or names:

                @pl.when(step == i)
                def _(events=events, names=names):
                    for event in events:
                        arrive(ARRIVALS[event])
                    for name in names:
                        copy_of(name).wait_recv()

        row = pick([job[1] for job in JOBS])
        half = pick([job[2] for job in JOBS])
        move = pick([{OWN: 0, NEAR: 0, FAR: 0, OPP: 2}[job[0]] for job in JOBS]) + toward * pick(
            [{OWN: 0, NEAR: -1, FAR: 1, OPP: 0}[job[0]] for job in JOBS]
        )
        block = jnp.where(row == 0, y, 1 - y) * 4 + (zb + move + 4) % 4
        qs = jnp.where(jnp.logical_or(half == 1, block >= own), 1, 0)

        @pl.when(jnp.logical_or(half == 0, block < own))
        def _():
            attend(qs, half, block, False)

        return carry

    lax.fori_loop(0, len(JOBS), step_body, 0)

    half = c // 16

    def cache_source(kv, to):
        return buf.at[2 * half + kv, 2 * (c % 16) + to // 4, pl.ds(pl.multiple_of(CACHE * (to % 4), 16), CACHE)]

    columns = pl.ds(pl.multiple_of(h * DH, DH), DH)

    def cache_copies(d):
        to = (h + d) % HEAD
        return [
            pltpu.make_async_remote_copy(
                src_ref=cache_source(kv, to),
                dst_ref=ref.at[:, columns],
                send_sem=csend.at[kv, d],
                recv_sem=crecv.at[kv, d],
                device_id=(c, to),
                device_id_type=MESH,
            )
            for kv, ref in ((0, kc_ref), (1, vc_ref))
        ]

    for d in range(1, HEAD):
        for copy in cache_copies(d):
            copy.start()
    for kv, ref in ((0, kc_ref), (1, vc_ref)):
        ref[:, columns] = buf[2 * half + kv, 2 * (c % 16) + h // 4, pl.ds(pl.multiple_of(CACHE * (h % 4), 16), CACHE)]

    def finish(g, carry):
        for s in range(2):
            held = acc[s, g]
            out_ref[s, :, pl.ds(pl.multiple_of(g * DH, DH), DH)] = (held[:, :DH] / held[:, DH:]).astype(jnp.bfloat16)
        return carry

    lax.fori_loop(0, GROUPS, finish, 0)

    for name in TRANSFERS:
        copy_of(name).wait_send()
    for d in range(1, HEAD):
        for copy in cache_copies(d):
            copy.wait()


def body(queries, key_states, value_states, segment_ids):
    vmem = pl.BlockSpec(memory_space=pltpu.VMEM)
    count = len(TRANSFERS)
    return pl.pallas_call(
        kernel,
        out_shape=(
            jax.ShapeDtypeStruct((2, ROWS, GROUPS * DH), jnp.bfloat16),
            jax.ShapeDtypeStruct((CACHE, HEAD * DH), jnp.bfloat16),
            jax.ShapeDtypeStruct((CACHE, HEAD * DH), jnp.bfloat16),
        ),
        in_specs=[vmem] * 4,
        out_specs=(vmem,) * 3,
        scratch_shapes=[
            pltpu.VMEM((4, CTX, ROWS, DH), jnp.bfloat16),
            pltpu.VMEM((2 * CTX, ROWS, DH), jnp.bfloat16),
            pltpu.VMEM((2, GROUPS, ROWS, 2 * DH), jnp.bfloat16),
            pltpu.VMEM((2, GROUPS, ROWS, 2 * DH), jnp.float32),
            pltpu.VMEM((2, GROUPS, ROWS, DH), jnp.float32),
            pltpu.SemaphoreType.DMA((count,)),
            pltpu.SemaphoreType.DMA((count,)),
            pltpu.SemaphoreType.DMA((2, HEAD)),
            pltpu.SemaphoreType.DMA((2, HEAD)),
        ],
        compiler_params=pltpu.CompilerParams(
            collective_id=0, has_side_effects=True, vmem_limit_bytes=56 * 1024 * 1024
        ),
        name="attend_gather",
    )(queries, key_states, value_states, segment_ids.reshape(-1, DH))


def solution(mesh):
    in_specs = (P(None, "ctx", "head"), P(None, "ctx", "head"), P(None, "ctx", "head"), P())
    out_specs = (P(None, "ctx", "head"), P(("ctx", "head"), None), P(("ctx", "head"), None))
    return jax.shard_map(body, mesh=mesh, in_specs=in_specs, out_specs=out_specs, check_vma=False)
```

```python
import math

import jax
import jax.numpy as jnp
from jax import lax
from jax.experimental import pallas as pl
from jax.experimental.pallas import tpu as pltpu
from jax.sharding import PartitionSpec as P

MESH = pl.DeviceIdType.MESH
DH = 128
GROUPS = 8
ROWS = 192
CTX = 32
HEAD = 8
KEYS = 4 * ROWS
CACHE = 48
TILE = 4
OTHER = -(2.0 ** 20)
LATER = -(2.0 ** 22)
START = -(2.0 ** 23)
SCALE = math.log2(math.e) / math.sqrt(DH)

LOW, HIGH = 0, 1


def transfers():
    out = {}

    def add(name, link, row, dz, half, source):
        out[name] = (link, row, dz, half, source)

    for half, tag in ((LOW, "L"), (HIGH, "H")):
        for d in (1, 2, 3):
            add(f"U{d}{tag}", "up", 0, -d, half, f"U{d - 1}{tag}" if d > 1 else None)
            add(f"D{d}{tag}", "down", 0, d, half, f"D{d - 1}{tag}" if d > 1 else None)
        add(f"Y0{tag}", "y", 1, 0, half, None)
        for d in (1, 2):
            add(f"YU{d}{tag}", "y", 1, -d, half, f"U{d}{tag}")
            add(f"YD{d}{tag}", "y", 1, d, half, f"D{d}{tag}")
        add(f"OU3{tag}", "up", 1, -3, half, f"YU2{tag}")
        add(f"OD3{tag}", "down", 1, 3, half, f"YD2{tag}")
    add("U4L", "up", 0, -4, LOW, "U3L")
    add("D4H", "down", 0, 4, HIGH, "D3H")
    add("OU4L", "up", 1, -4, LOW, "OU3L")
    add("OD4H", "down", 1, 4, HIGH, "OD3H")
    for name in list(out):
        link, row, dz, half, source = out[name]
        add("C" + name, "core", row, dz, half, name)
    add("C0L", "core", 0, 0, LOW, None)
    add("C0H", "core", 0, 0, HIGH, None)
    return {
        name + tag: (link, row, dz, half, kv, source and source + tag)
        for name, (link, row, dz, half, source) in out.items()
        for kv, tag in ((0, "k"), (1, "v"))
    }


TRANSFERS = transfers()
INDEX = {name: i for i, name in enumerate(TRANSFERS)}
FORWARDS = {name: [k for k, v in TRANSFERS.items() if v[5] == name] for name in TRANSFERS}
LATE, LATE_AFTER = ["YU1Hk", "YU1Hv", "YD1Hk", "YD1Hv"], 5
ORDERS = (("up", "y", "down"), ("down", "up", "y"))

ARRIVALS = [
    ["U1L", "D1L", "Y0L"],
    ["U1H", "D1H", "Y0H"],
    ["U2L", "D2L", "YU1L"],
    ["U2H", "D2H", "YD1L"],
    ["U3L", "D3L", "YU2L"],
    ["U3H", "D3H", "YD2L"],
    ["U4L", "D4H", "YU2H"],
    ["OU3L", "OD3L", "YD2H"],
    ["OU3H", "OD3H", "YU1H"],
    ["OU4L", "OD4H", "YD1H"],
]
OWN, NEAR, FAR, OPP = 0, 1, 2, 3
PLAN = [
    2,
    3,
    (OWN, 0, LOW),
    (NEAR, 0, LOW),
    (NEAR, 0, HIGH),
    4,
    5,
    (OWN, 1, LOW),
    (FAR, 0, LOW),
    (FAR, 0, HIGH),
    6,
    7,
    (NEAR, 1, LOW),
    (OPP, 0, LOW),
    (OPP, 0, HIGH),
    8,
    (FAR, 1, LOW),
    (FAR, 1, HIGH),
    9,
    (OWN, 1, HIGH),
    (NEAR, 1, HIGH),
    (OPP, 1, LOW),
    (OPP, 1, HIGH),
]


REACH = {OWN: (0, 1), NEAR: (1, 2), FAR: (2, 3), OPP: (3, 4)}


def needs(kind, row, half):
    return [
        name
        for name, (link, r, dz, hf, kv, _) in TRANSFERS.items()
        if link == "core" and r == row and hf == half and abs(dz) in REACH[kind]
    ]


def steps_of(plan):
    jobs, before, pending, seen = [], [], [], set(needs(OWN, 0, LOW) + needs(OWN, 0, HIGH))
    for entry in plan:
        if isinstance(entry, int):
            pending.append(entry)
        else:
            jobs.append(entry)
            fresh = [name for name in needs(*entry) if name not in seen]
            seen.update(fresh)
            before.append((pending, fresh))
            pending = []
    assert seen == {name for name in TRANSFERS if TRANSFERS[name][0] == "core"}
    return jobs, before


JOBS, BEFORE = steps_of(PLAN)


def kernel(q_ref, k_ref, v_ref, seg_ref, out_ref, kc_ref, vc_ref, buf, kfeat, qx, acc, peak, send, recv, csend, crecv):
    c = lax.axis_index("ctx")
    h = lax.axis_index("head")
    y, z, core = c // 16, (c % 16) // 2, c % 2

    def index_of(row, zz, kk):
        return row * 16 + (zz % 8) * 2 + kk

    up_to = index_of(y, z + 1, core)
    down_to = index_of(y, z + 7, core)
    y_to = index_of(1 - y, z, core)
    core_to = index_of(y, z, 1 - core)
    target = {"up": up_to, "down": down_to, "y": y_to, "core": core_to}

    barrier = pltpu.get_barrier_semaphore()
    for peer in (up_to, down_to, y_to, core_to):
        pl.semaphore_signal(barrier, inc=1, device_id=(peer, h), device_id_type=MESH)
    for d in range(1, HEAD):
        pl.semaphore_signal(barrier, inc=1, device_id=(c, (h + d) % HEAD), device_id_type=MESH)

    buf[0, c] = k_ref[0]
    buf[1, c] = v_ref[0]
    buf[2, c] = k_ref[1]
    buf[3, c] = v_ref[1]
    pl.semaphore_wait(barrier, 4 + HEAD - 1)

    def copy_of(name):
        link, row, dz, half, kv, _ = TRANSFERS[name]
        if link == "up":
            block = index_of(y if row == 0 else 1 - y, z + dz + 1 + 8, core)
        elif link == "down":
            block = index_of(y if row == 0 else 1 - y, z + dz - 1 + 8, core)
        elif link == "y":
            block = index_of(y, z + dz + 8, core)
        else:
            block = index_of(y if row == 0 else 1 - y, z + dz + 8, core)
        ref = buf.at[2 * half + kv, block]
        i = INDEX[name]
        return pltpu.make_async_remote_copy(
            src_ref=ref,
            dst_ref=ref,
            send_sem=send.at[i],
            recv_sem=recv.at[i],
            device_id=(target[link], h),
            device_id_type=MESH,
        )

    def by_core(function):
        for which, order in enumerate(ORDERS):
            pl.when(core == which)(lambda order=order: function(order))

    def link_order(names, order):
        return sorted(names, key=lambda name: (name[-1], order.index(TRANSFERS[name][0]) if TRANSFERS[name][0] in order else 3))

    @by_core
    def _(order):
        for half in "LH":
            first = [n + half + kv for kv in "kv" for n in ("U1", "D1", "Y0")]
            for name in link_order(first, order):
                copy_of(name).start()
            for kv in "kv":
                copy_of("C0" + half + kv).start()

    def arrive(event):
        names = [n + kv for kv in "kv" for n in ARRIVALS[event]]

        @by_core
        def _(order):
            for name in link_order(names, order):
                copy_of(name).wait_recv()
                for onward in link_order(FORWARDS[name], order):
                    if TRANSFERS[onward][0] != "core" and onward not in LATE:
                        copy_of(onward).start()
            if event == LATE_AFTER:
                for name in LATE:
                    copy_of(name).start()
            for name in names:
                copy_of("C" + name).start()

    seg = seg_ref[...]
    lane = lax.broadcasted_iota(jnp.int32, (1, DH), 1)
    low = jnp.zeros((1, DH), jnp.float32)
    high = jnp.zeros((1, DH), jnp.float32)
    for s in range(4):
        below = jnp.sum(jnp.where(seg < s, 1.0, 0.0), axis=(0, 1), keepdims=True)
        upto = jnp.sum(jnp.where(seg <= s, 1.0, 0.0), axis=(0, 1), keepdims=True)
        low = jnp.where(lane == s, below, low)
        high = jnp.where(lane == s, upto, high)
    used = jnp.where(lane < 4, 1.0, 0.0)

    def inside(first, rows):
        at = (lax.broadcasted_iota(jnp.int32, (rows, DH), 0) + first).astype(jnp.float32)
        return jnp.where((at >= low) & (at < high), 1.0, 0.0)

    def prepare_keys(i, carry):
        kfeat[i] = inside(i * ROWS, ROWS).astype(jnp.bfloat16)
        return carry

    for s in range(2):
        feature = ((used - inside(s * CTX * ROWS + c * ROWS, ROWS)) * OTHER).astype(jnp.bfloat16)
        for g in range(GROUPS):
            qx[s, g, :, :DH] = q_ref[s, :, g * DH : (g + 1) * DH]
            qx[s, g, :, DH:] = feature
    lax.fori_loop(0, 2 * CTX, prepare_keys, 0)
    peak[...] = jnp.full(peak.shape, START, jnp.float32)
    acc[...] = jnp.zeros(acc.shape, jnp.float32)

    rows = TILE * ROWS
    lanes = KEYS // DH
    ones = jnp.ones((KEYS, DH), jnp.bfloat16)

    def attend(qs, half, block, causal):
        first = block * 4
        keys = buf[2 * half, pl.ds(first, 4)].reshape(KEYS, DH)
        values = buf[2 * half + 1, pl.ds(first, 4)].reshape(KEYS, DH)
        features = kfeat[pl.ds(half * CTX + first, 4)].reshape(KEYS, DH)
        keys = jnp.concatenate([keys, features], axis=1)
        values = jnp.concatenate([values, ones], axis=1)
        if causal:
            at = c * ROWS - first * ROWS
            row = lax.broadcasted_iota(jnp.int32, (ROWS, KEYS), 0) + at
            col = lax.broadcasted_iota(jnp.int32, (ROWS, KEYS), 1)
            seen = jnp.concatenate([row >= col] * TILE, axis=0)
        def scores_of(t):
            queries = qx[qs, pl.ds(t * TILE, TILE)].reshape(rows, 2 * DH)
            return lax.dot_general(
                queries, keys, (((1,), (1,)), ((), ())), preferred_element_type=jnp.float32
            )

        tiles = GROUPS // TILE
        scores = scores_of(0)
        for t in range(tiles):
            later = scores_of(t + 1) if t + 1 < tiles else None
            heads = pl.ds(t * TILE, TILE)
            if causal:
                scores = jnp.where(seen, scores, LATER)
            parts = [scores[:, i * DH : (i + 1) * DH] for i in range(lanes)]
            top = parts[0]
            for part in parts[1:]:
                top = jnp.maximum(top, part)
            old = peak[qs, heads].reshape(rows, DH)
            new = jnp.maximum(old, jnp.max(top, axis=1, keepdims=True))
            weights = jnp.concatenate(
                [jnp.exp2((part - new) * SCALE).astype(jnp.bfloat16) for part in parts], axis=1
            )
            factor = jnp.exp2((old - new) * SCALE)
            product = jnp.dot(weights, values, preferred_element_type=jnp.float32)
            held = acc[qs, heads].reshape(rows, 2 * DH)
            held = held * jnp.concatenate([factor, factor], axis=1) + product
            acc[qs, heads] = held.reshape(TILE, ROWS, 2 * DH)
            peak[qs, heads] = new.reshape(TILE, ROWS, DH)
            scores = later

    zb = z // 2
    own = y * 4 + zb
    toward = 1 - 2 * (z % 2)

    arrive(0)
    arrive(1)
    for name in needs(OWN, 0, LOW) + needs(OWN, 0, HIGH):
        copy_of(name).wait_recv()

    def own_step(half, carry):
        attend(half, half, own, True)
        return carry

    lax.fori_loop(0, 2, own_step, 0)

    def step_body(step, carry):
        def pick(values):
            value = jnp.int32(values[0])
            for i in range(1, len(values)):
                if values[i] != values[0]:
                    value = jnp.where(step == i, jnp.int32(values[i]), value)
            return value

        for i, (events, names) in enumerate(BEFORE):
            if events or names:

                @pl.when(step == i)
                def _(events=events, names=names):
                    for event in events:
                        arrive(event)
                    for name in names:
                        copy_of(name).wait_recv()

        row = pick([job[1] for job in JOBS])
        half = pick([job[2] for job in JOBS])
        move = pick([{OWN: 0, NEAR: 0, FAR: 0, OPP: 2}[job[0]] for job in JOBS]) + toward * pick(
            [{OWN: 0, NEAR: -1, FAR: 1, OPP: 0}[job[0]] for job in JOBS]
        )
        block = jnp.where(row == 0, y, 1 - y) * 4 + (zb + move + 4) % 4
        qs = jnp.where(jnp.logical_or(half == 1, block >= own), 1, 0)

        @pl.when(jnp.logical_or(half == 0, block < own))
        def _():
            attend(qs, half, block, False)

        return carry

    lax.fori_loop(0, len(JOBS), step_body, 0)

    half = c // 16

    def cache_source(kv, to):
        return buf.at[2 * half + kv, 2 * (c % 16) + to // 4, pl.ds(pl.multiple_of(CACHE * (to % 4), 16), CACHE)]

    columns = pl.ds(pl.multiple_of(h * DH, DH), DH)

    def cache_copies(d):
        to = (h + d) % HEAD
        return [
            pltpu.make_async_remote_copy(
                src_ref=cache_source(kv, to),
                dst_ref=ref.at[:, columns],
                send_sem=csend.at[kv, d],
                recv_sem=crecv.at[kv, d],
                device_id=(c, to),
                device_id_type=MESH,
            )
            for kv, ref in ((0, kc_ref), (1, vc_ref))
        ]

    for d in range(1, HEAD):
        for copy in cache_copies(d):
            copy.start()
    for kv, ref in ((0, kc_ref), (1, vc_ref)):
        ref[:, columns] = buf[2 * half + kv, 2 * (c % 16) + h // 4, pl.ds(pl.multiple_of(CACHE * (h % 4), 16), CACHE)]

    def finish(g, carry):
        for s in range(2):
            held = acc[s, g]
            out_ref[s, :, pl.ds(pl.multiple_of(g * DH, DH), DH)] = (held[:, :DH] / held[:, DH:]).astype(jnp.bfloat16)
        return carry

    lax.fori_loop(0, GROUPS, finish, 0)

    for name in TRANSFERS:
        copy_of(name).wait_send()
    for d in range(1, HEAD):
        for copy in cache_copies(d):
            copy.wait()


def body(queries, key_states, value_states, segment_ids):
    vmem = pl.BlockSpec(memory_space=pltpu.VMEM)
    count = len(TRANSFERS)
    return pl.pallas_call(
        kernel,
        out_shape=(
            jax.ShapeDtypeStruct((2, ROWS, GROUPS * DH), jnp.bfloat16),
            jax.ShapeDtypeStruct((CACHE, HEAD * DH), jnp.bfloat16),
            jax.ShapeDtypeStruct((CACHE, HEAD * DH), jnp.bfloat16),
        ),
        in_specs=[vmem] * 4,
        out_specs=(vmem,) * 3,
        scratch_shapes=[
            pltpu.VMEM((4, CTX, ROWS, DH), jnp.bfloat16),
            pltpu.VMEM((2 * CTX, ROWS, DH), jnp.bfloat16),
            pltpu.VMEM((2, GROUPS, ROWS, 2 * DH), jnp.bfloat16),
            pltpu.VMEM((2, GROUPS, ROWS, 2 * DH), jnp.float32),
            pltpu.VMEM((2, GROUPS, ROWS, DH), jnp.float32),
            pltpu.SemaphoreType.DMA((count,)),
            pltpu.SemaphoreType.DMA((count,)),
            pltpu.SemaphoreType.DMA((2, HEAD)),
            pltpu.SemaphoreType.DMA((2, HEAD)),
        ],
        compiler_params=pltpu.CompilerParams(
            collective_id=0, has_side_effects=True, vmem_limit_bytes=56 * 1024 * 1024
        ),
        name="attend_gather",
    )(queries, key_states, value_states, segment_ids.reshape(-1, DH))


def solution(mesh):
    in_specs = (P(None, "ctx", "head"), P(None, "ctx", "head"), P(None, "ctx", "head"), P())
    out_specs = (P(None, "ctx", "head"), P(("ctx", "head"), None), P(("ctx", "head"), None))
    return jax.shard_map(body, mesh=mesh, in_specs=in_specs, out_specs=out_specs, check_vma=False)
```

```python
import math

import jax
import jax.numpy as jnp
from jax import lax
from jax.experimental import pallas as pl
from jax.experimental.pallas import tpu as pltpu
from jax.sharding import PartitionSpec as P

MESH = pl.DeviceIdType.MESH
DH = 128
GROUPS = 8
ROWS = 192
CTX = 32
HEAD = 8
KEYS = 4 * ROWS
CACHE = 48
TILE = 2
OTHER = -(2.0 ** 20)
LATER = -(2.0 ** 22)
LARGEST = 1e30
START = -(2.0 ** 23)
SCALE = 1.0 / math.sqrt(DH)

LOW, HIGH = 0, 1
PARTS = 2
PIECES = range(2 * PARTS)
GATHER_VMEM = 16 * 1024 * 1024
ATTEND_VMEM = 40 * 1024 * 1024


def transfers():
    out = {}

    def add(name, link, row, dz, half, source):
        out[name] = (link, row, dz, half, source)

    for half, tag in ((LOW, "L"), (HIGH, "H")):
        for d in (1, 2, 3):
            add(f"U{d}{tag}", "up", 0, -d, half, f"U{d - 1}{tag}" if d > 1 else None)
            add(f"D{d}{tag}", "down", 0, d, half, f"D{d - 1}{tag}" if d > 1 else None)
        add(f"Y0{tag}", "y", 1, 0, half, None)
        for d in (1, 2):
            add(f"YU{d}{tag}", "y", 1, -d, half, f"U{d}{tag}")
            add(f"YD{d}{tag}", "y", 1, d, half, f"D{d}{tag}")
        add(f"OU3{tag}", "up", 1, -3, half, f"YU2{tag}")
        add(f"OD3{tag}", "down", 1, 3, half, f"YD2{tag}")
    add("U4L", "up", 0, -4, LOW, "U3L")
    add("D4H", "down", 0, 4, HIGH, "D3H")
    add("OU4L", "up", 1, -4, LOW, "OU3L")
    add("OD4H", "down", 1, 4, HIGH, "OD3H")
    for name in list(out):
        link, row, dz, half, source = out[name]
        add("C" + name, "core", row, dz, half, name)
    add("C0L", "core", 0, 0, LOW, None)
    add("C0H", "core", 0, 0, HIGH, None)
    return {
        f"{name}{tag}": (link, row, dz, half, tag, source and f"{source}{tag}")
        for name, (link, row, dz, half, source) in out.items()
        for tag in PIECES
    }


TRANSFERS = transfers()
INDEX = {name: i for i, name in enumerate(TRANSFERS)}
FORWARDS = {name: [k for k, v in TRANSFERS.items() if v[5] == name] for name in TRANSFERS}
FIRST = [f"{n}{half}{p}" for half in "LH" for p in PIECES for n in ("U1", "D1", "Y0")]
FIRST += [f"C0{half}{p}" for half in "LH" for p in PIECES]

ARRIVALS = [
    ["U1L", "D1L", "Y0L"],
    ["U1H", "D1H", "Y0H"],
    ["U2L", "D2L", "YU1L"],
    ["U2H", "D2H", "YD1L"],
    ["U3L", "D3L", "YU2L"],
    ["U3H", "D3H", "YD2L"],
    ["U4L", "D4H", "YU2H"],
    ["OU3L", "OD3L", "YD2H"],
    ["OU3H", "OD3H", "YU1H"],
    ["OU4L", "OD4H", "YD1H"],
]
LATE, LATE_AFTER = [f"{n}{p}" for p in PIECES for n in ("YU1H", "YD1H")], 5


def gather_kernel(k_ref, v_ref, buf, kc_ref, vc_ref, send, recv, csend, crecv, own):
    c = lax.axis_index("ctx")
    h = lax.axis_index("head")
    y, z, core = c // 16, (c % 16) // 2, c % 2

    def index_of(row, zz, kk):
        return row * 16 + (zz % 8) * 2 + kk

    up_to = index_of(y, z + 1, core)
    down_to = index_of(y, z + 7, core)
    y_to = index_of(1 - y, z, core)
    core_to = index_of(y, z, 1 - core)
    target = {"up": up_to, "down": down_to, "y": y_to, "core": core_to}

    barrier = pltpu.get_barrier_semaphore()
    for peer in (up_to, down_to, y_to, core_to):
        pl.semaphore_signal(barrier, inc=1, device_id=(peer, h), device_id_type=MESH)
    for d in range(1, HEAD):
        pl.semaphore_signal(barrier, inc=1, device_id=(c, (h + d) % HEAD), device_id_type=MESH)
    own_copies = [
        pltpu.make_async_copy((k_ref, v_ref)[kv].at[half], buf.at[2 * half + kv, c], own.at[2 * half + kv])
        for half in range(2)
        for kv in range(2)
    ]
    for copy in own_copies:
        copy.start()
    pl.semaphore_wait(barrier, 4 + HEAD - 1)

    def copy_of(name):
        link, row, dz, half, piece, source = TRANSFERS[name]
        shift = {"up": 1, "down": -1}.get(link, 0)
        there = y if (row == 0) != (link == "y") else 1 - y
        block = index_of(there, z + dz + shift + 8, core)
        part = pl.ds(piece % PARTS * (ROWS // PARTS), ROWS // PARTS)
        dst = buf.at[2 * half + piece // PARTS, block, part]
        return pltpu.make_async_remote_copy(
            src_ref=dst if source else (k_ref, v_ref)[piece // PARTS].at[half, part],
            dst_ref=dst,
            send_sem=send.at[0],
            recv_sem=recv.at[INDEX[name]],
            device_id=(target[link], h),
            device_id_type=MESH,
        )

    for name in FIRST:
        copy_of(name).start()

    for event, names in enumerate(ARRIVALS):
        names = [f"{n}{p}" for p in PIECES for n in names]
        for name in names:
            copy_of(name).wait_recv()
            for onward in FORWARDS[name]:
                if TRANSFERS[onward][0] != "core" and onward not in LATE:
                    copy_of(onward).start()
        for name in names:
            copy_of("C" + name).start()
        if event == LATE_AFTER:
            for name in LATE:
                copy_of(name).start()
    for name in TRANSFERS:
        if TRANSFERS[name][0] == "core":
            copy_of(name).wait_recv()
    for copy in own_copies:
        copy.wait()

    page = c // 16
    columns = pl.ds(pl.multiple_of(h * DH, DH), DH)

    def cache_source(kv, to):
        return buf.at[2 * page + kv, 2 * (c % 16) + to // 4, pl.ds(pl.multiple_of(CACHE * (to % 4), 16), CACHE)]

    def cache_copies(d):
        to = (h + d) % HEAD
        return [
            pltpu.make_async_remote_copy(
                src_ref=cache_source(kv, to),
                dst_ref=ref.at[:, columns],
                send_sem=csend.at[kv, d],
                recv_sem=crecv.at[kv, d],
                device_id=(c, to),
                device_id_type=MESH,
            )
            for kv, ref in ((0, kc_ref), (1, vc_ref))
        ]

    for d in range(1, HEAD):
        for copy in cache_copies(d):
            copy.start()
    mine = [
        pltpu.make_async_copy(cache_source(kv, h), ref.at[:, columns], own.at[kv])
        for kv, ref in ((0, kc_ref), (1, vc_ref))
    ]
    for copy in mine:
        copy.start()

    sent = buf.at[:, pl.ds(0, len(TRANSFERS) // (4 * PARTS))]
    pltpu.make_async_remote_copy(
        src_ref=sent, dst_ref=sent, send_sem=send.at[0], recv_sem=recv.at[0], device_id=(core_to, h), device_id_type=MESH
    ).wait_send()
    for copy in mine:
        copy.wait()
    for d in range(1, HEAD):
        for copy in cache_copies(d):
            copy.wait()


def attend_kernel(q_ref, seg_ref, kin_ref, vin_ref, buf, out_ref, kc_ref, vc_ref, qx, acc, peak, state):
    c = lax.axis_index("ctx")
    kc_ref[...] = kin_ref[...]
    vc_ref[...] = vin_ref[...]

    seg = seg_ref[...]
    starts = [jnp.int32(0)] + [
        jnp.sum(jnp.where(seg < s, 1.0, 0.0)).astype(jnp.int32) for s in range(1, 4)
    ] + [jnp.int32(2 * CTX * ROWS)]
    lane = lax.broadcasted_iota(jnp.int32, (1, DH), 1)
    low = jnp.zeros((1, DH), jnp.int32)
    high = jnp.zeros((1, DH), jnp.int32)
    for s in range(4):
        low = jnp.where(lane == s, starts[s], low)
        high = jnp.where(lane == s, starts[s + 1], high)
    used = jnp.where(lane < 4, 1.0, 0.0)

    def inside(first, rows):
        at = lax.broadcasted_iota(jnp.int32, (rows, DH), 0) + first
        return jnp.where(jnp.logical_and(at >= low, at < high), 1.0, 0.0)

    def segment_start(at):
        begin = jnp.int32(0)
        for start in starts[1:4]:
            begin = jnp.where(start <= at, start, begin)
        return begin

    own, first_block, inner = [], [], []
    for s in range(2):
        at = s * CTX * ROWS + c * ROWS
        own.append(at // KEYS)
        first_block.append(segment_start(at) // KEYS)
        inner.append(segment_start(at + ROWS - 1))
    count = own[0] - first_block[0] + 1
    total = count + own[1] - first_block[1] + 1

    for s in range(2):
        feature = ((used - inside(s * CTX * ROWS + c * ROWS, ROWS)) * OTHER).astype(jnp.bfloat16)
        for g in range(GROUPS):
            qx[s, g, :, :DH] = q_ref[s, :, g * DH : (g + 1) * DH]
            qx[s, g, :, DH:] = feature
    peak[...] = jnp.full(peak.shape, START, jnp.float32)
    acc[0] = jnp.zeros(acc.shape[1:], jnp.float32)
    state[0] = 0
    state[1] = 0

    rows = TILE * ROWS
    lanes = KEYS // DH
    ones = jnp.ones((KEYS, DH), jnp.bfloat16)

    def operands(block, featured):
        half, chunk = block // 8, (block % 8) * 4
        keys = buf[2 * half, pl.ds(chunk, 4)].reshape(KEYS, DH)
        values = buf[2 * half + 1, pl.ds(chunk, 4)].reshape(KEYS, DH)
        if featured:
            keys = jnp.concatenate([keys, inside(block * KEYS, KEYS).astype(jnp.bfloat16)], axis=1)
        return keys, values

    def scores_of(qs, t, keys):
        width = keys.shape[1]
        queries = qx[qs, pl.ds(t * TILE, TILE), :, :width].reshape(rows, width)
        return lax.dot_general(queries, keys, (((1,), (1,)), ((), ())), preferred_element_type=jnp.float32)

    tiles = GROUPS // TILE

    def attend(qs, block):
        keys, values = operands(block, True)
        now = state[qs]
        at = c * ROWS + qs * CTX * ROWS - block * KEYS
        key_row = lax.broadcasted_iota(jnp.int32, (KEYS, DH), 0)
        values = jnp.where(key_row < at + ROWS, values, jnp.zeros_like(values))
        values = jnp.concatenate([values, ones], axis=1)
        row = lax.broadcasted_iota(jnp.int32, (ROWS, KEYS), 0) + at
        col = lax.broadcasted_iota(jnp.int32, (ROWS, KEYS), 1)
        seen = jnp.concatenate([row >= col] * TILE, axis=0)
        scores = scores_of(qs, 0, keys)
        for t in range(tiles):
            later = scores_of(qs, t + 1, keys) if t + 1 < tiles else None
            heads = pl.ds(t * TILE, TILE)
            scores = jnp.where(seen, scores, LATER)
            parts = [scores[:, i * DH : (i + 1) * DH] for i in range(lanes)]
            top = parts[0]
            for part in parts[1:]:
                top = jnp.maximum(top, part)
            old = peak[qs, heads].reshape(rows, DH)
            new = jnp.maximum(old, jnp.max(top, axis=1, keepdims=True))
            weights = jnp.concatenate(
                [jnp.exp((part - new) * SCALE).astype(jnp.bfloat16) for part in parts], axis=1
            )
            factor = jnp.exp((old - new) * SCALE)
            product = jnp.dot(weights, values, preferred_element_type=jnp.float32)
            held = acc[now, qs, heads].reshape(rows, 2 * DH)
            held = held * jnp.concatenate([factor, factor], axis=1) + product
            acc[now, qs, heads] = held.reshape(TILE, ROWS, 2 * DH)
            peak[qs, heads] = new.reshape(TILE, ROWS, DH)
            scores = later

    def attend_kept(qs, block, featured):
        keys, values = operands(block, featured)
        values = jnp.concatenate([values, ones], axis=1)
        now = state[qs]
        scores = scores_of(qs, 0, keys)
        largest = jnp.zeros((8, DH), jnp.float32)
        for t in range(tiles):
            later = scores_of(qs, t + 1, keys) if t + 1 < tiles else None
            heads = pl.ds(t * TILE, TILE)
            top = peak[qs, heads].reshape(rows, DH)
            weights = jnp.concatenate(
                [
                    jnp.exp((scores[:, i * DH : (i + 1) * DH] - top) * SCALE).astype(jnp.bfloat16)
                    for i in range(lanes)
                ],
                axis=1,
            )
            product = jnp.dot(weights, values, preferred_element_type=jnp.float32)
            held = acc[now, qs, heads].reshape(rows, 2 * DH) + product
            acc[1 - now, qs, heads] = held.reshape(TILE, ROWS, 2 * DH)
            largest = jnp.maximum(largest, jnp.max(held[:, DH:].reshape(rows // 8, 8, DH), axis=0))
            scores = later
        fits = jnp.max(largest) <= LARGEST
        state[qs] = jnp.where(fits, 1 - now, now)
        state[2] = jnp.where(fits, 0, 1)

    def step(j, carry):
        upper = j >= count
        qs = jnp.where(upper, 1, 0)
        mine = jnp.where(upper, own[1], own[0])
        block = mine - jnp.where(upper, j - count, j)
        plain = block * KEYS >= jnp.where(upper, inner[1], inner[0])
        state[2] = jnp.where(block == mine, 1, 0)

        @pl.when(jnp.logical_and(block < mine, plain))
        def _():
            attend_kept(qs, block, False)

        @pl.when(jnp.logical_and(block < mine, jnp.logical_not(plain)))
        def _():
            attend_kept(qs, block, True)

        @pl.when(state[2] == 1)
        def _():
            attend(qs, block)

        return carry

    lax.fori_loop(0, total, step, 0)

    def finish(g, carry):
        for s in range(2):
            held = acc[state[s], s, g]
            out_ref[s, :, pl.ds(pl.multiple_of(g * DH, DH), DH)] = (held[:, :DH] / held[:, DH:]).astype(jnp.bfloat16)
        return carry

    lax.fori_loop(0, GROUPS, finish, 0)


def body(queries, key_states, value_states, segment_ids):
    vmem = pl.BlockSpec(memory_space=pltpu.VMEM)
    anywhere = pl.BlockSpec(memory_space=pl.ANY)
    cache = jax.ShapeDtypeStruct((CACHE, HEAD * DH), jnp.bfloat16)
    gathered, keys, values = pl.pallas_call(
        gather_kernel,
        out_shape=(jax.ShapeDtypeStruct((4, CTX, ROWS, DH), jnp.bfloat16), cache, cache),
        in_specs=[anywhere] * 2,
        out_specs=(anywhere,) * 3,
        scratch_shapes=[
            pltpu.SemaphoreType.DMA((1,)),
            pltpu.SemaphoreType.DMA((len(TRANSFERS),)),
            pltpu.SemaphoreType.DMA((2, HEAD)),
            pltpu.SemaphoreType.DMA((2, HEAD)),
            pltpu.SemaphoreType.DMA((4,)),
        ],
        compiler_params=pltpu.CompilerParams(
            collective_id=0, has_side_effects=True, vmem_limit_bytes=GATHER_VMEM
        ),
        name="gather",
    )(key_states, value_states)
    return pl.pallas_call(
        attend_kernel,
        out_shape=(jax.ShapeDtypeStruct((2, ROWS, GROUPS * DH), jnp.bfloat16), cache, cache),
        in_specs=[vmem] * 5,
        out_specs=(vmem,) * 3,
        scratch_shapes=[
            pltpu.VMEM((2, GROUPS, ROWS, 2 * DH), jnp.bfloat16),
            pltpu.VMEM((2, 2, GROUPS, ROWS, 2 * DH), jnp.float32),
            pltpu.VMEM((2, GROUPS, ROWS, DH), jnp.float32),
            pltpu.SMEM((3,), jnp.int32),
        ],
        compiler_params=pltpu.CompilerParams(vmem_limit_bytes=ATTEND_VMEM),
        name="attend",
    )(queries, segment_ids.reshape(-1, DH), keys, values, gathered)


def solution(mesh):
    in_specs = (P(None, "ctx", "head"), P(None, "ctx", "head"), P(None, "ctx", "head"), P())
    out_specs = (P(None, "ctx", "head"), P(("ctx", "head"), None), P(("ctx", "head"), None))
    return jax.shard_map(body, mesh=mesh, in_specs=in_specs, out_specs=out_specs, check_vma=False)
```

```python
import math

import jax
import jax.numpy as jnp
from jax import lax
from jax.experimental import pallas as pl
from jax.experimental.pallas import tpu as pltpu
from jax.sharding import PartitionSpec as P

MESH = pl.DeviceIdType.MESH
DH = 128
GROUPS = 8
ROWS = 192
CTX = 32
HEAD = 8
KEYS = 4 * ROWS
CACHE = 48
TILE = 4
OTHER = -(2.0 ** 20)
LATER = -(2.0 ** 22)
LARGEST = 1e30
START = -(2.0 ** 23)
SCALE = 1.0 / math.sqrt(DH)

LOW, HIGH = 0, 1
PARTS = 1
PIECES = range(2 * PARTS)
GATHER_VMEM = 36 * 1024 * 1024
ATTEND_VMEM = 36 * 1024 * 1024


def transfers():
    out = {}

    def add(name, link, row, dz, half, source):
        out[name] = (link, row, dz, half, source)

    for half, tag in ((LOW, "L"), (HIGH, "H")):
        for d in (1, 2, 3):
            add(f"U{d}{tag}", "up", 0, -d, half, f"U{d - 1}{tag}" if d > 1 else None)
            add(f"D{d}{tag}", "down", 0, d, half, f"D{d - 1}{tag}" if d > 1 else None)
        add(f"Y0{tag}", "y", 1, 0, half, None)
        for d in (1, 2):
            add(f"YU{d}{tag}", "y", 1, -d, half, f"U{d}{tag}")
            add(f"YD{d}{tag}", "y", 1, d, half, f"D{d}{tag}")
        add(f"OU3{tag}", "up", 1, -3, half, f"YU2{tag}")
        add(f"OD3{tag}", "down", 1, 3, half, f"YD2{tag}")
    add("U4L", "up", 0, -4, LOW, "U3L")
    add("D4H", "down", 0, 4, HIGH, "D3H")
    add("OU4L", "up", 1, -4, LOW, "OU3L")
    add("OD4H", "down", 1, 4, HIGH, "OD3H")
    for name in list(out):
        link, row, dz, half, source = out[name]
        add("C" + name, "core", row, dz, half, name)
    add("C0L", "core", 0, 0, LOW, None)
    add("C0H", "core", 0, 0, HIGH, None)
    return {
        f"{name}{tag}": (link, row, dz, half, tag, source and f"{source}{tag}")
        for name, (link, row, dz, half, source) in out.items()
        for tag in PIECES
    }


TRANSFERS = transfers()
INDEX = {name: i for i, name in enumerate(TRANSFERS)}
FORWARDS = {name: [k for k, v in TRANSFERS.items() if v[5] == name] for name in TRANSFERS}
FIRST = [f"{n}{half}{p}" for half in "LH" for p in PIECES for n in ("U1", "D1", "Y0")]
FIRST += [f"C0{half}{p}" for half in "LH" for p in PIECES]

ARRIVALS = [
    ["U1L", "D1L", "Y0L"],
    ["U1H", "D1H", "Y0H"],
    ["U2L", "D2L", "YU1L"],
    ["U2H", "D2H", "YD1L"],
    ["U3L", "D3L", "YU2L"],
    ["U3H", "D3H", "YD2L"],
    ["U4L", "D4H", "YU2H"],
    ["OU3L", "OD3L", "YD2H"],
    ["OU3H", "OD3H", "YU1H"],
    ["OU4L", "OD4H", "YD1H"],
]
LATE, LATE_AFTER = [f"{n}{p}" for p in PIECES for n in ("YU1H", "YD1H")], 5

OWN, NEAR, FAR, OPP = 0, 1, 2, 3
PLAN = [2, 3, (NEAR, LOW), (NEAR, HIGH), 4, 5, (FAR, LOW), (FAR, HIGH), 6, 7, (OPP, LOW), (OPP, HIGH)]
REACH = {OWN: (0, 1), NEAR: (1, 2), FAR: (2, 3), OPP: (3, 4)}


def needs(kind, half):
    return [
        name
        for name, (link, r, dz, hf, _, _) in TRANSFERS.items()
        if link == "core" and r == 0 and hf == half and abs(dz) in REACH[kind]
    ]


def steps_of(plan):
    jobs, before, pending, seen = [], [], [], set(needs(OWN, LOW) + needs(OWN, HIGH))
    for entry in plan:
        if isinstance(entry, int):
            pending.append(entry)
        else:
            jobs.append(entry)
            fresh = [name for name in needs(*entry) if name not in seen]
            seen.update(fresh)
            before.append((pending, fresh))
            pending = []
    rest = [name for name in TRANSFERS if TRANSFERS[name][0] == "core" and name not in seen]
    return jobs, before, rest


JOBS, BEFORE, REST = steps_of(PLAN)


def online(scores, old, held, values):
    parts = [scores[:, i : i + DH] for i in range(0, KEYS, DH)]
    top = parts[0]
    for part in parts[1:]:
        top = jnp.maximum(top, part)
    new = jnp.maximum(old, jnp.max(top, axis=1, keepdims=True))
    weights = jnp.concatenate([jnp.exp((part - new) * SCALE).astype(jnp.bfloat16) for part in parts], axis=1)
    factor = jnp.exp((old - new) * SCALE)
    product = jnp.dot(weights, values, preferred_element_type=jnp.float32)
    return new, held * jnp.concatenate([factor, factor], axis=1) + product


def gather_kernel(q_ref, k_ref, v_ref, seg_ref, buf, kc_ref, vc_ref, qx, acc, peak, send, recv, csend, crecv, own):
    c = lax.axis_index("ctx")
    h = lax.axis_index("head")
    y, z, core = c // 16, (c % 16) // 2, c % 2

    def index_of(row, zz, kk):
        return row * 16 + (zz % 8) * 2 + kk

    up_to = index_of(y, z + 1, core)
    down_to = index_of(y, z + 7, core)
    y_to = index_of(1 - y, z, core)
    core_to = index_of(y, z, 1 - core)
    target = {"up": up_to, "down": down_to, "y": y_to, "core": core_to}

    barrier = pltpu.get_barrier_semaphore()
    for peer in (up_to, down_to, y_to, core_to):
        pl.semaphore_signal(barrier, inc=1, device_id=(peer, h), device_id_type=MESH)
    for d in range(1, HEAD):
        pl.semaphore_signal(barrier, inc=1, device_id=(c, (h + d) % HEAD), device_id_type=MESH)
    for half in range(2):
        buf[2 * half, c] = k_ref[half]
        buf[2 * half + 1, c] = v_ref[half]
    pl.semaphore_wait(barrier, 4 + HEAD - 1)

    def copy_of(name):
        link, row, dz, half, piece, source = TRANSFERS[name]
        shift = {"up": 1, "down": -1}.get(link, 0)
        there = y if (row == 0) != (link == "y") else 1 - y
        block = index_of(there, z + dz + shift + 8, core)
        part = pl.ds(piece % PARTS * (ROWS // PARTS), ROWS // PARTS)
        dst = buf.at[2 * half + piece // PARTS, block, part]
        return pltpu.make_async_remote_copy(
            src_ref=dst,
            dst_ref=dst,
            send_sem=send.at[0],
            recv_sem=recv.at[INDEX[name]],
            device_id=(target[link], h),
            device_id_type=MESH,
        )

    for name in FIRST:
        copy_of(name).start()

    def arrive(event):
        names = [f"{n}{p}" for p in PIECES for n in ARRIVALS[event]]
        for name in names:
            copy_of(name).wait_recv()
            for onward in FORWARDS[name]:
                if TRANSFERS[onward][0] != "core" and onward not in LATE:
                    copy_of(onward).start()
        for name in names:
            copy_of("C" + name).start()
        if event == LATE_AFTER:
            for name in LATE:
                copy_of(name).start()

    seg = seg_ref[...]
    lane = lax.broadcasted_iota(jnp.int32, (1, DH), 1)
    low = jnp.zeros((1, DH), jnp.float32)
    high = jnp.zeros((1, DH), jnp.float32)
    for s in range(4):
        below = jnp.sum(jnp.where(seg < s, 1.0, 0.0), axis=(0, 1), keepdims=True)
        upto = jnp.sum(jnp.where(seg <= s, 1.0, 0.0), axis=(0, 1), keepdims=True)
        low = jnp.where(lane == s, below, low)
        high = jnp.where(lane == s, upto, high)
    used = jnp.where(lane < 4, 1.0, 0.0)

    def inside(first, rows):
        at = (lax.broadcasted_iota(jnp.int32, (rows, DH), 0) + first).astype(jnp.float32)
        return jnp.where((at >= low) & (at < high), 1.0, 0.0)

    for s in range(2):
        feature = ((used - inside(s * CTX * ROWS + c * ROWS, ROWS)) * OTHER).astype(jnp.bfloat16)
        for g in range(GROUPS):
            qx[s, g, :, :DH] = q_ref[s, :, g * DH : (g + 1) * DH]
            qx[s, g, :, DH:] = feature
    peak[...] = jnp.full(peak.shape, START, jnp.float32)
    acc[...] = jnp.zeros(acc.shape, jnp.float32)

    rows = TILE * ROWS
    ones = jnp.ones((KEYS, DH), jnp.bfloat16)

    def attend(qs, half, block, causal):
        first = block * 4
        keys = buf[2 * half, pl.ds(first, 4)].reshape(KEYS, DH)
        values = buf[2 * half + 1, pl.ds(first, 4)].reshape(KEYS, DH)
        features = inside((half * CTX + first) * ROWS, KEYS).astype(jnp.bfloat16)
        keys = jnp.concatenate([keys, features], axis=1)
        values = jnp.concatenate([values, ones], axis=1)
        seen = None
        if causal:
            row = lax.broadcasted_iota(jnp.int32, (ROWS, KEYS), 0) + (c - first) * ROWS
            col = lax.broadcasted_iota(jnp.int32, (ROWS, KEYS), 1)
            seen = jnp.concatenate([row >= col] * TILE, axis=0)

        def scores_of(t):
            queries = qx[qs, pl.ds(t * TILE, TILE)].reshape(rows, 2 * DH)
            return lax.dot_general(
                queries, keys, (((1,), (1,)), ((), ())), preferred_element_type=jnp.float32
            )

        scores = scores_of(0)
        for t in range(GROUPS // TILE):
            later = scores_of(t + 1) if t + 1 < GROUPS // TILE else None
            heads = pl.ds(t * TILE, TILE)
            if causal:
                scores = jnp.where(seen, scores, LATER)
            old = peak[qs, heads].reshape(rows, DH)
            held = acc[qs, heads].reshape(rows, 2 * DH)
            new, held = online(scores, old, held, values)
            acc[qs, heads] = held.reshape(TILE, ROWS, 2 * DH)
            peak[qs, heads] = new.reshape(TILE, ROWS, DH)
            scores = later

    zb = z // 2
    mine = y * 4 + zb
    toward = 1 - 2 * (z % 2)

    arrive(0)
    arrive(1)
    for name in needs(OWN, LOW) + needs(OWN, HIGH):
        copy_of(name).wait_recv()

    def own_step(half, carry):
        attend(half, half, mine, True)
        return carry

    lax.fori_loop(0, 2, own_step, 0)

    def step_body(step, carry):
        def pick(values):
            value = jnp.int32(values[0])
            for i in range(1, len(values)):
                value = jnp.where(step == i, jnp.int32(values[i]), value)
            return value

        for i, (events, names) in enumerate(BEFORE):
            if events or names:

                @pl.when(step == i)
                def _(events=events, names=names):
                    for event in events:
                        arrive(event)
                    for name in names:
                        copy_of(name).wait_recv()

        half = pick([job[1] for job in JOBS])
        move = pick([{NEAR: 0, FAR: 0, OPP: 2}[job[0]] for job in JOBS]) + toward * pick(
            [{NEAR: -1, FAR: 1, OPP: 0}[job[0]] for job in JOBS]
        )
        block = y * 4 + (zb + move + 4) % 4
        qs = jnp.where(jnp.logical_or(half == 1, block > mine), 1, 0)

        @pl.when(jnp.logical_or(half == 0, block < mine))
        def _():
            attend(qs, half, block, False)

        return carry

    lax.fori_loop(0, len(JOBS), step_body, 0)
    arrive(8)
    arrive(9)
    for name in REST:
        copy_of(name).wait_recv()

    page = c // 16
    columns = pl.ds(pl.multiple_of(h * DH, DH), DH)

    def cache_source(kv, to):
        return buf.at[2 * page + kv, 2 * (c % 16) + to // 4, pl.ds(pl.multiple_of(CACHE * (to % 4), 16), CACHE)]

    def cache_copies(d):
        to = (h + d) % HEAD
        return [
            pltpu.make_async_remote_copy(
                src_ref=cache_source(kv, to),
                dst_ref=ref.at[:, columns],
                send_sem=csend.at[kv, d],
                recv_sem=crecv.at[kv, d],
                device_id=(c, to),
                device_id_type=MESH,
            )
            for kv, ref in ((0, kc_ref), (1, vc_ref))
        ]

    for d in range(1, HEAD):
        for copy in cache_copies(d):
            copy.start()
    mine = [
        pltpu.make_async_copy(cache_source(kv, h), ref.at[:, columns], own.at[kv])
        for kv, ref in ((0, kc_ref), (1, vc_ref))
    ]
    for copy in mine:
        copy.start()

    sent = buf.at[:, pl.ds(0, len(TRANSFERS) // (4 * PARTS))]
    pltpu.make_async_remote_copy(
        src_ref=sent, dst_ref=sent, send_sem=send.at[0], recv_sem=recv.at[0], device_id=(core_to, h), device_id_type=MESH
    ).wait_send()
    for copy in mine:
        copy.wait()
    for d in range(1, HEAD):
        for copy in cache_copies(d):
            copy.wait()


def attend_kernel(seg_ref, kin_ref, vin_ref, buf, qx, sums, peaks, out_ref, kc_ref, vc_ref, acc, peak, state):
    c = lax.axis_index("ctx")
    y, mine = c // 16, c // 4
    kc_ref[...] = kin_ref[...]
    vc_ref[...] = vin_ref[...]
    acc[0] = sums[...]
    peak[...] = peaks[...]
    state[0] = 0
    state[1] = 0

    seg = seg_ref[...]
    starts = [jnp.int32(0)] + [
        jnp.sum(jnp.where(seg < s, 1.0, 0.0)).astype(jnp.int32) for s in range(1, 4)
    ] + [jnp.int32(2 * CTX * ROWS)]
    lane = lax.broadcasted_iota(jnp.int32, (1, DH), 1)
    low = jnp.zeros((1, DH), jnp.int32)
    high = jnp.zeros((1, DH), jnp.int32)
    for s in range(4):
        low = jnp.where(lane == s, starts[s], low)
        high = jnp.where(lane == s, starts[s + 1], high)

    def inside(first, rows):
        at = lax.broadcasted_iota(jnp.int32, (rows, DH), 0) + first
        return jnp.where(jnp.logical_and(at >= low, at < high), 1.0, 0.0)

    def segment_start(at):
        begin = jnp.int32(0)
        for start in starts[1:4]:
            begin = jnp.where(start <= at, start, begin)
        return begin

    first, inner = [], []
    for s in range(2):
        at = s * CTX * ROWS + c * ROWS
        first.append(segment_start(at) // KEYS)
        inner.append(segment_start(at + ROWS - 1))
    count = jnp.where(y == 1, jnp.maximum(4 - first[0], 0), 0)
    upper_first = jnp.maximum(first[1], 4 + 4 * y)
    upper_count = jnp.maximum(8 + 4 * y - upper_first, 0)
    total = count + upper_count + jnp.where(first[1] <= mine, 1, 0)

    rows = TILE * ROWS
    every = GROUPS * ROWS
    ones = jnp.ones((KEYS, DH), jnp.bfloat16)

    def operands(block, featured):
        half, chunk = block // 8, (block % 8) * 4
        keys = buf[2 * half, pl.ds(chunk, 4)].reshape(KEYS, DH)
        values = buf[2 * half + 1, pl.ds(chunk, 4)].reshape(KEYS, DH)
        if featured:
            keys = jnp.concatenate([keys, inside(block * KEYS, KEYS).astype(jnp.bfloat16)], axis=1)
        return keys, values

    def attend(qs, block):
        keys, values = operands(block, True)
        values = jnp.concatenate([values, ones], axis=1)
        now = state[qs]
        for t in range(GROUPS // TILE):
            heads = pl.ds(t * TILE, TILE)
            queries = qx[qs, heads].reshape(rows, 2 * DH)
            scores = lax.dot_general(
                queries, keys, (((1,), (1,)), ((), ())), preferred_element_type=jnp.float32
            )
            old = peak[qs, heads].reshape(rows, DH)
            held = acc[now, qs, heads].reshape(rows, 2 * DH)
            new, held = online(scores, old, held, values)
            acc[now, qs, heads] = held.reshape(TILE, ROWS, 2 * DH)
            peak[qs, heads] = new.reshape(TILE, ROWS, DH)

    def attend_kept(qs, block, featured):
        keys, values = operands(block, featured)
        values = jnp.concatenate([values, ones], axis=1)
        now = state[qs]
        width = keys.shape[1]
        queries = qx[qs, :, :, :width].reshape(every, width)
        top = peak[qs].reshape(every, DH)

        def scores_of(i):
            part = keys[i * 2 * DH : (i + 1) * 2 * DH]
            return lax.dot_general(
                queries, part, (((1,), (1,)), ((), ())), preferred_element_type=jnp.float32
            )

        pieces = KEYS // (2 * DH)
        weights = []
        scores = scores_of(0)
        for i in range(pieces):
            later = scores_of(i + 1) if i + 1 < pieces else None
            for half in (scores[:, :DH], scores[:, DH:]):
                weights.append(jnp.exp((half - top) * SCALE).astype(jnp.bfloat16))
            scores = later
        product = jnp.dot(jnp.concatenate(weights, axis=1), values, preferred_element_type=jnp.float32)
        held = acc[now, qs].reshape(every, 2 * DH) + product
        acc[1 - now, qs] = held.reshape(GROUPS, ROWS, 2 * DH)
        fits = jnp.max(jnp.max(held[:, DH:].reshape(every // 8, 8, DH), axis=0)) <= LARGEST
        state[qs] = jnp.where(fits, 1 - now, now)
        state[2] = jnp.where(fits, 0, 1)

    def step(j, carry):
        upper = j >= count
        qs = jnp.where(upper, 1, 0)
        block = jnp.where(upper, jnp.where(j - count < upper_count, upper_first + j - count, mine), first[0] + j)
        plain = block * KEYS >= jnp.where(upper, inner[1], inner[0])

        @pl.when(plain)
        def _():
            attend_kept(qs, block, False)

        @pl.when(jnp.logical_not(plain))
        def _():
            attend_kept(qs, block, True)

        @pl.when(state[2] == 1)
        def _():
            attend(qs, block)

        return carry

    lax.fori_loop(0, total, step, 0)

    def finish(g, carry):
        for s in range(2):
            held = acc[state[s], s, g]
            out_ref[s, :, pl.ds(pl.multiple_of(g * DH, DH), DH)] = (held[:, :DH] / held[:, DH:]).astype(jnp.bfloat16)
        return carry

    lax.fori_loop(0, GROUPS, finish, 0)


def body(queries, key_states, value_states, segment_ids):
    vmem = pl.BlockSpec(memory_space=pltpu.VMEM)
    anywhere = pl.BlockSpec(memory_space=pl.ANY)
    cache = jax.ShapeDtypeStruct((CACHE, HEAD * DH), jnp.bfloat16)
    segments = segment_ids.reshape(-1, DH)
    gathered, keys, values, prepared, sums, peaks = pl.pallas_call(
        gather_kernel,
        out_shape=(
            jax.ShapeDtypeStruct((4, CTX, ROWS, DH), jnp.bfloat16),
            cache,
            cache,
            jax.ShapeDtypeStruct((2, GROUPS, ROWS, 2 * DH), jnp.bfloat16),
            jax.ShapeDtypeStruct((2, GROUPS, ROWS, 2 * DH), jnp.float32),
            jax.ShapeDtypeStruct((2, GROUPS, ROWS, DH), jnp.float32),
        ),
        in_specs=[vmem] * 4,
        out_specs=(vmem, anywhere, anywhere, vmem, vmem, vmem),
        scratch_shapes=[
            pltpu.SemaphoreType.DMA((1,)),
            pltpu.SemaphoreType.DMA((len(TRANSFERS),)),
            pltpu.SemaphoreType.DMA((2, HEAD)),
            pltpu.SemaphoreType.DMA((2, HEAD)),
            pltpu.SemaphoreType.DMA((2,)),
        ],
        compiler_params=pltpu.CompilerParams(
            collective_id=0, has_side_effects=True, vmem_limit_bytes=GATHER_VMEM
        ),
        name="gather",
    )(queries, key_states, value_states, segments)
    return pl.pallas_call(
        attend_kernel,
        out_shape=(jax.ShapeDtypeStruct((2, ROWS, GROUPS * DH), jnp.bfloat16), cache, cache),
        in_specs=[vmem] * 7,
        out_specs=(vmem,) * 3,
        scratch_shapes=[
            pltpu.VMEM((2, 2, GROUPS, ROWS, 2 * DH), jnp.float32),
            pltpu.VMEM((2, GROUPS, ROWS, DH), jnp.float32),
            pltpu.SMEM((3,), jnp.int32),
        ],
        compiler_params=pltpu.CompilerParams(vmem_limit_bytes=ATTEND_VMEM),
        name="attend",
    )(segments, keys, values, gathered, prepared, sums, peaks)


def solution(mesh):
    in_specs = (P(None, "ctx", "head"), P(None, "ctx", "head"), P(None, "ctx", "head"), P())
    out_specs = (P(None, "ctx", "head"), P(("ctx", "head"), None), P(("ctx", "head"), None))
    return jax.shard_map(body, mesh=mesh, in_specs=in_specs, out_specs=out_specs, check_vma=False)
```

```python
import math

import jax
import jax.numpy as jnp
from jax import lax
from jax.experimental import pallas as pl
from jax.experimental.pallas import tpu as pltpu
from jax.sharding import PartitionSpec as P

MESH = pl.DeviceIdType.MESH
DH = 128
GROUPS = 8
ROWS = 192
CTX = 32
HEAD = 8
KEYS = 4 * ROWS
CACHE = 48
TILE = 4
OTHER = -(2.0 ** 20)
LATER = -(2.0 ** 22)
LARGEST = 1e30
START = -(2.0 ** 23)
SCALE = 1.0 / math.sqrt(DH)

LOW, HIGH = 0, 1
PARTS = 1
PIECES = range(2 * PARTS)
GATHER_VMEM = 36 * 1024 * 1024
ATTEND_VMEM = 36 * 1024 * 1024


def transfers():
    out = {}

    def add(name, link, row, dz, half, source):
        out[name] = (link, row, dz, half, source)

    for half, tag in ((LOW, "L"), (HIGH, "H")):
        for d in (1, 2, 3):
            add(f"U{d}{tag}", "up", 0, -d, half, f"U{d - 1}{tag}" if d > 1 else None)
            add(f"D{d}{tag}", "down", 0, d, half, f"D{d - 1}{tag}" if d > 1 else None)
        add(f"Y0{tag}", "y", 1, 0, half, None)
        for d in (1, 2):
            add(f"YU{d}{tag}", "y", 1, -d, half, f"U{d}{tag}")
            add(f"YD{d}{tag}", "y", 1, d, half, f"D{d}{tag}")
        add(f"OU3{tag}", "up", 1, -3, half, f"YU2{tag}")
        add(f"OD3{tag}", "down", 1, 3, half, f"YD2{tag}")
    add("U4L", "up", 0, -4, LOW, "U3L")
    add("D4H", "down", 0, 4, HIGH, "D3H")
    add("OU4L", "up", 1, -4, LOW, "OU3L")
    add("OD4H", "down", 1, 4, HIGH, "OD3H")
    for name in list(out):
        link, row, dz, half, source = out[name]
        add("C" + name, "core", row, dz, half, name)
    add("C0L", "core", 0, 0, LOW, None)
    add("C0H", "core", 0, 0, HIGH, None)
    return {
        f"{name}{tag}": (link, row, dz, half, tag, source and f"{source}{tag}")
        for name, (link, row, dz, half, source) in out.items()
        for tag in PIECES
    }


TRANSFERS = transfers()
INDEX = {name: i for i, name in enumerate(TRANSFERS)}
FORWARDS = {name: [k for k, v in TRANSFERS.items() if v[5] == name] for name in TRANSFERS}
FIRST = [f"{n}{half}{p}" for half in "LH" for p in PIECES for n in ("U1", "D1", "Y0")]
FIRST += [f"C0{half}{p}" for half in "LH" for p in PIECES]

ARRIVALS = [
    ["U1L", "D1L", "Y0L"],
    ["U1H", "D1H", "Y0H"],
    ["U2L", "D2L", "YU1L"],
    ["U2H", "D2H", "YD1L"],
    ["U3L", "D3L", "YU2L"],
    ["U3H", "D3H", "YD2L"],
    ["U4L", "D4H", "YU2H"],
    ["OU3L", "OD3L", "YD2H"],
    ["OU3H", "OD3H", "YU1H"],
    ["OU4L", "OD4H", "YD1H"],
]
LATE, LATE_AFTER = [f"{n}{p}" for p in PIECES for n in ("YU1H", "YD1H")], 5

OWN, NEAR, FAR, OPP = 0, 1, 2, 3
HALVES = 2
PLAN = [
    0, 1, (OWN, 0, LOW), 2, (OWN, 0, LOW), (OWN, 0, HIGH), 3, (OWN, 0, HIGH), (NEAR, 0, LOW), 4, (NEAR, 0, LOW),
    (NEAR, 0, HIGH), 5, (NEAR, 0, HIGH), (OWN, 1, LOW), (OWN, 1, LOW), 6, (FAR, 0, LOW), (FAR, 0, LOW), 7,
    (FAR, 0, HIGH), (FAR, 0, HIGH), (NEAR, 1, LOW), 8, (NEAR, 1, LOW), (OPP, 0, LOW), (OPP, 0, LOW),
    (OPP, 0, HIGH), 9, (OPP, 0, HIGH), (FAR, 1, LOW), (FAR, 1, LOW),
]
REACH = {OWN: (0, 1), NEAR: (1, 2), FAR: (2, 3), OPP: (3, 4)}


def needs(kind, row, half):
    return [
        name
        for name, (link, r, dz, hf, _, _) in TRANSFERS.items()
        if link == "core" and r == row and hf == half and abs(dz) in REACH[kind]
    ]


def steps_of(plan):
    jobs, before, pending, seen = [], [], [], set()
    for entry in plan:
        if isinstance(entry, int):
            pending.append(entry)
        else:
            jobs.append(entry)
            fresh = [name for name in needs(*entry) if name not in seen]
            seen.update(fresh)
            before.append((pending, fresh))
            pending = []
    assert not pending and all(jobs[i] == jobs[i + 1] for i in range(0, len(jobs), HALVES))
    rest = [name for name in TRANSFERS if TRANSFERS[name][0] == "core" and name not in seen]
    return jobs, before, rest


JOBS, BEFORE, REST = steps_of(PLAN)


def online(scores, old, held, values):
    parts = [scores[:, i : i + DH] for i in range(0, KEYS, DH)]
    top = parts[0]
    for part in parts[1:]:
        top = jnp.maximum(top, part)
    new = jnp.maximum(old, jnp.max(top, axis=1, keepdims=True))
    weights = jnp.concatenate([jnp.exp((part - new) * SCALE).astype(jnp.bfloat16) for part in parts], axis=1)
    factor = jnp.exp((old - new) * SCALE)
    product = jnp.dot(weights, values, preferred_element_type=jnp.float32)
    return new, held * jnp.concatenate([factor, factor], axis=1) + product


def gather_kernel(q_ref, k_ref, v_ref, seg_ref, buf, kc_ref, vc_ref, qx, acc, peak, feature, send, recv, csend, crecv, own):
    c = lax.axis_index("ctx")
    h = lax.axis_index("head")
    y, z, core = c // 16, (c % 16) // 2, c % 2

    def index_of(row, zz, kk):
        return row * 16 + (zz % 8) * 2 + kk

    up_to = index_of(y, z + 1, core)
    down_to = index_of(y, z + 7, core)
    y_to = index_of(1 - y, z, core)
    core_to = index_of(y, z, 1 - core)
    target = {"up": up_to, "down": down_to, "y": y_to, "core": core_to}

    barrier = pltpu.get_barrier_semaphore()
    for peer in (up_to, down_to, y_to, core_to):
        pl.semaphore_signal(barrier, inc=1, device_id=(peer, h), device_id_type=MESH)
    for d in range(1, HEAD):
        pl.semaphore_signal(barrier, inc=1, device_id=(c, (h + d) % HEAD), device_id_type=MESH)
    for half in range(2):
        buf[2 * half, c] = k_ref[half]
        buf[2 * half + 1, c] = v_ref[half]
    pl.semaphore_wait(barrier, 4 + HEAD - 1)

    def copy_of(name):
        link, row, dz, half, piece, source = TRANSFERS[name]
        shift = {"up": 1, "down": -1}.get(link, 0)
        there = y if (row == 0) != (link == "y") else 1 - y
        block = index_of(there, z + dz + shift + 8, core)
        part = pl.ds(piece % PARTS * (ROWS // PARTS), ROWS // PARTS)
        dst = buf.at[2 * half + piece // PARTS, block, part]
        return pltpu.make_async_remote_copy(
            src_ref=dst,
            dst_ref=dst,
            send_sem=send.at[0],
            recv_sem=recv.at[INDEX[name]],
            device_id=(target[link], h),
            device_id_type=MESH,
        )

    for name in FIRST:
        copy_of(name).start()

    def arrive(event):
        names = [f"{n}{p}" for p in PIECES for n in ARRIVALS[event]]
        for name in names:
            copy_of(name).wait_recv()
            for onward in FORWARDS[name]:
                if TRANSFERS[onward][0] != "core" and onward not in LATE:
                    copy_of(onward).start()
        for name in names:
            copy_of("C" + name).start()
        if event == LATE_AFTER:
            for name in LATE:
                copy_of(name).start()

    seg = seg_ref[...]
    lane = lax.broadcasted_iota(jnp.int32, (1, DH), 1)
    low = jnp.zeros((1, DH), jnp.float32)
    high = jnp.zeros((1, DH), jnp.float32)
    for s in range(4):
        below = jnp.sum(jnp.where(seg < s, 1.0, 0.0), axis=(0, 1), keepdims=True)
        upto = jnp.sum(jnp.where(seg <= s, 1.0, 0.0), axis=(0, 1), keepdims=True)
        low = jnp.where(lane == s, below, low)
        high = jnp.where(lane == s, upto, high)
    used = jnp.where(lane < 4, 1.0, 0.0)

    def inside(first, rows):
        at = (lax.broadcasted_iota(jnp.int32, (rows, DH), 0) + first).astype(jnp.float32)
        return jnp.where((at >= low) & (at < high), 1.0, 0.0)

    for s in range(2):
        outside = ((used - inside(s * CTX * ROWS + c * ROWS, ROWS)) * OTHER).astype(jnp.bfloat16)
        for g in range(GROUPS):
            qx[s, g, :, :DH] = q_ref[s, :, g * DH : (g + 1) * DH]
            qx[s, g, :, DH:] = outside
    peak[...] = jnp.full(peak.shape, START, jnp.float32)
    acc[...] = jnp.zeros(acc.shape, jnp.float32)

    rows = TILE * ROWS
    ones = jnp.ones((KEYS, DH), jnp.bfloat16)

    def attend(qs, half, block, part):
        first = block * 4
        keys = buf[2 * half, pl.ds(first, 4)].reshape(KEYS, DH)
        values = buf[2 * half + 1, pl.ds(first, 4)].reshape(KEYS, DH)

        @pl.when(part == 0)
        def _():
            feature[...] = inside((half * CTX + first) * ROWS, KEYS).astype(jnp.bfloat16)

        keys = jnp.concatenate([keys, feature[...]], axis=1)
        values = jnp.concatenate([values, ones], axis=1)
        at = (qs * CTX + c - half * CTX - first) * ROWS
        row = lax.broadcasted_iota(jnp.int32, (ROWS, KEYS), 0) + at
        col = lax.broadcasted_iota(jnp.int32, (ROWS, KEYS), 1)
        seen = jnp.concatenate([row >= col] * TILE, axis=0)
        heads = pl.ds(part * TILE, TILE)
        queries = qx[qs, heads].reshape(rows, 2 * DH)
        scores = lax.dot_general(
            queries, keys, (((1,), (1,)), ((), ())), preferred_element_type=jnp.float32
        )
        scores = jnp.where(seen, scores, LATER)
        old = peak[qs, heads].reshape(rows, DH)
        held = acc[qs, heads].reshape(rows, 2 * DH)
        new, held = online(scores, old, held, values)
        acc[qs, heads] = held.reshape(TILE, ROWS, 2 * DH)
        peak[qs, heads] = new.reshape(TILE, ROWS, DH)

    zb = z // 2
    mine = y * 4 + zb
    toward = 1 - 2 * (z % 2)

    def step_body(step, carry):
        def pick(values):
            value = jnp.int32(values[0])
            for i in range(1, len(values)):
                value = jnp.where(job == i, jnp.int32(values[i]), value)
            return value

        for i, (events, names) in enumerate(BEFORE):
            if events or names:

                @pl.when(step == i)
                def _(events=events, names=names):
                    for event in events:
                        arrive(event)
                    for name in names:
                        copy_of(name).wait_recv()

        job, part = step // HALVES, step % HALVES
        jobs = JOBS[::HALVES]
        row = pick([entry[1] for entry in jobs])
        half = pick([entry[2] for entry in jobs])
        move = pick([{OWN: 0, NEAR: 0, FAR: 0, OPP: 2}[entry[0]] for entry in jobs]) + toward * pick(
            [{OWN: 0, NEAR: -1, FAR: 1, OPP: 0}[entry[0]] for entry in jobs]
        )
        block = jnp.where(row == 0, y, 1 - y) * 4 + (zb + move + 4) % 4
        qs = jnp.where(jnp.logical_or(half == 1, block > mine), 1, 0)

        @pl.when(jnp.logical_or(half == 0, block <= mine))
        def _():
            attend(qs, half, block, part)

        return carry

    lax.fori_loop(0, len(JOBS), step_body, 0)
    for name in REST:
        copy_of(name).wait_recv()

    page = c // 16
    columns = pl.ds(pl.multiple_of(h * DH, DH), DH)

    def cache_source(kv, to):
        return buf.at[2 * page + kv, 2 * (c % 16) + to // 4, pl.ds(pl.multiple_of(CACHE * (to % 4), 16), CACHE)]

    def cache_copies(d):
        to = (h + d) % HEAD
        return [
            pltpu.make_async_remote_copy(
                src_ref=cache_source(kv, to),
                dst_ref=ref.at[:, columns],
                send_sem=csend.at[kv, d],
                recv_sem=crecv.at[kv, d],
                device_id=(c, to),
                device_id_type=MESH,
            )
            for kv, ref in ((0, kc_ref), (1, vc_ref))
        ]

    for d in range(1, HEAD):
        for copy in cache_copies(d):
            copy.start()
    mine = [
        pltpu.make_async_copy(cache_source(kv, h), ref.at[:, columns], own.at[kv])
        for kv, ref in ((0, kc_ref), (1, vc_ref))
    ]
    for copy in mine:
        copy.start()

    sent = buf.at[:, pl.ds(0, len(TRANSFERS) // (4 * PARTS))]
    pltpu.make_async_remote_copy(
        src_ref=sent, dst_ref=sent, send_sem=send.at[0], recv_sem=recv.at[0], device_id=(core_to, h), device_id_type=MESH
    ).wait_send()
    for copy in mine:
        copy.wait()
    for d in range(1, HEAD):
        for copy in cache_copies(d):
            copy.wait()


def attend_kernel(seg_ref, kin_ref, vin_ref, buf, qx, sums, peaks, out_ref, kc_ref, vc_ref, acc, peak, state):
    c = lax.axis_index("ctx")
    y, mine = c // 16, c // 4
    kc_ref[...] = kin_ref[...]
    vc_ref[...] = vin_ref[...]
    acc[0] = sums[...]
    peak[...] = peaks[...]
    state[0] = 0
    state[1] = 0

    seg = seg_ref[...]
    starts = [jnp.int32(0)] + [
        jnp.sum(jnp.where(seg < s, 1.0, 0.0)).astype(jnp.int32) for s in range(1, 4)
    ] + [jnp.int32(2 * CTX * ROWS)]
    lane = lax.broadcasted_iota(jnp.int32, (1, DH), 1)
    low = jnp.zeros((1, DH), jnp.int32)
    high = jnp.zeros((1, DH), jnp.int32)
    for s in range(4):
        low = jnp.where(lane == s, starts[s], low)
        high = jnp.where(lane == s, starts[s + 1], high)

    def inside(first, rows):
        at = lax.broadcasted_iota(jnp.int32, (rows, DH), 0) + first
        return jnp.where(jnp.logical_and(at >= low, at < high), 1.0, 0.0)

    def segment_start(at):
        begin = jnp.int32(0)
        for start in starts[1:4]:
            begin = jnp.where(start <= at, start, begin)
        return begin

    first, inner = [], []
    for s in range(2):
        at = s * CTX * ROWS + c * ROWS
        first.append(segment_start(at) // KEYS)
        inner.append(segment_start(at + ROWS - 1))
    opposite = (1 - y) * 4 + (mine + 2) % 4
    count = jnp.where(jnp.where(y == 1, first[0], first[1]) <= opposite, 1, 0)
    high_first = jnp.maximum(first[1], 8)
    high_count = jnp.where(y == 1, jnp.maximum(12 - high_first, 0), 0)
    total = count + high_count + jnp.where(first[1] <= mine, 1, 0)

    rows = TILE * ROWS
    every = GROUPS * ROWS
    ones = jnp.ones((KEYS, DH), jnp.bfloat16)

    def operands(block, featured):
        half, chunk = block // 8, (block % 8) * 4
        keys = buf[2 * half, pl.ds(chunk, 4)].reshape(KEYS, DH)
        values = buf[2 * half + 1, pl.ds(chunk, 4)].reshape(KEYS, DH)
        if featured:
            keys = jnp.concatenate([keys, inside(block * KEYS, KEYS).astype(jnp.bfloat16)], axis=1)
        return keys, values

    def attend(qs, block):
        keys, values = operands(block, True)
        values = jnp.concatenate([values, ones], axis=1)
        now = state[qs]
        for t in range(GROUPS // TILE):
            heads = pl.ds(t * TILE, TILE)
            queries = qx[qs, heads].reshape(rows, 2 * DH)
            scores = lax.dot_general(
                queries, keys, (((1,), (1,)), ((), ())), preferred_element_type=jnp.float32
            )
            old = peak[qs, heads].reshape(rows, DH)
            held = acc[now, qs, heads].reshape(rows, 2 * DH)
            new, held = online(scores, old, held, values)
            acc[now, qs, heads] = held.reshape(TILE, ROWS, 2 * DH)
            peak[qs, heads] = new.reshape(TILE, ROWS, DH)

    def attend_kept(qs, block, featured):
        keys, values = operands(block, featured)
        values = jnp.concatenate([values, ones], axis=1)
        now = state[qs]
        width = keys.shape[1]
        queries = qx[qs, :, :, :width].reshape(every, width)
        top = peak[qs].reshape(every, DH)

        def scores_of(i):
            part = keys[i * 2 * DH : (i + 1) * 2 * DH]
            return lax.dot_general(
                queries, part, (((1,), (1,)), ((), ())), preferred_element_type=jnp.float32
            )

        pieces = KEYS // (2 * DH)
        weights = []
        scores = scores_of(0)
        for i in range(pieces):
            later = scores_of(i + 1) if i + 1 < pieces else None
            for half in (scores[:, :DH], scores[:, DH:]):
                weights.append(jnp.exp((half - top) * SCALE).astype(jnp.bfloat16))
            scores = later
        product = jnp.dot(jnp.concatenate(weights, axis=1), values, preferred_element_type=jnp.float32)
        held = acc[now, qs].reshape(every, 2 * DH) + product
        acc[1 - now, qs] = held.reshape(GROUPS, ROWS, 2 * DH)
        fits = jnp.max(jnp.max(held[:, DH:].reshape(every // 8, 8, DH), axis=0)) <= LARGEST
        state[qs] = jnp.where(fits, 1 - now, now)
        state[2] = jnp.where(fits, 0, 1)

    def step(j, carry):
        upper = jnp.logical_or(j >= count, y == 0)
        qs = jnp.where(upper, 1, 0)
        high = j - count
        block = jnp.where(high < 0, opposite, jnp.where(high < high_count, high_first + high, mine))
        plain = block * KEYS >= jnp.where(upper, inner[1], inner[0])

        @pl.when(plain)
        def _():
            attend_kept(qs, block, False)

        @pl.when(jnp.logical_not(plain))
        def _():
            attend_kept(qs, block, True)

        @pl.when(state[2] == 1)
        def _():
            attend(qs, block)

        return carry

    lax.fori_loop(0, total, step, 0)

    def finish(g, carry):
        for s in range(2):
            held = acc[state[s], s, g]
            out_ref[s, :, pl.ds(pl.multiple_of(g * DH, DH), DH)] = (held[:, :DH] / held[:, DH:]).astype(jnp.bfloat16)
        return carry

    lax.fori_loop(0, GROUPS, finish, 0)


def body(queries, key_states, value_states, segment_ids):
    vmem = pl.BlockSpec(memory_space=pltpu.VMEM)
    anywhere = pl.BlockSpec(memory_space=pl.ANY)
    cache = jax.ShapeDtypeStruct((CACHE, HEAD * DH), jnp.bfloat16)
    segments = segment_ids.reshape(-1, DH)
    gathered, keys, values, prepared, sums, peaks = pl.pallas_call(
        gather_kernel,
        out_shape=(
            jax.ShapeDtypeStruct((4, CTX, ROWS, DH), jnp.bfloat16),
            cache,
            cache,
            jax.ShapeDtypeStruct((2, GROUPS, ROWS, 2 * DH), jnp.bfloat16),
            jax.ShapeDtypeStruct((2, GROUPS, ROWS, 2 * DH), jnp.float32),
            jax.ShapeDtypeStruct((2, GROUPS, ROWS, DH), jnp.float32),
        ),
        in_specs=[vmem] * 4,
        out_specs=(vmem, anywhere, anywhere, vmem, vmem, vmem),
        scratch_shapes=[
            pltpu.VMEM((KEYS, DH), jnp.bfloat16),
            pltpu.SemaphoreType.DMA((1,)),
            pltpu.SemaphoreType.DMA((len(TRANSFERS),)),
            pltpu.SemaphoreType.DMA((2, HEAD)),
            pltpu.SemaphoreType.DMA((2, HEAD)),
            pltpu.SemaphoreType.DMA((2,)),
        ],
        compiler_params=pltpu.CompilerParams(
            collective_id=0, has_side_effects=True, vmem_limit_bytes=GATHER_VMEM
        ),
        name="gather",
    )(queries, key_states, value_states, segments)
    return pl.pallas_call(
        attend_kernel,
        out_shape=(jax.ShapeDtypeStruct((2, ROWS, GROUPS * DH), jnp.bfloat16), cache, cache),
        in_specs=[vmem] * 7,
        out_specs=(vmem,) * 3,
        scratch_shapes=[
            pltpu.VMEM((2, 2, GROUPS, ROWS, 2 * DH), jnp.float32),
            pltpu.VMEM((2, GROUPS, ROWS, DH), jnp.float32),
            pltpu.SMEM((3,), jnp.int32),
        ],
        compiler_params=pltpu.CompilerParams(vmem_limit_bytes=ATTEND_VMEM),
        name="attend",
    )(segments, keys, values, gathered, prepared, sums, peaks)


def solution(mesh):
    in_specs = (P(None, "ctx", "head"), P(None, "ctx", "head"), P(None, "ctx", "head"), P())
    out_specs = (P(None, "ctx", "head"), P(("ctx", "head"), None), P(("ctx", "head"), None))
    return jax.shard_map(body, mesh=mesh, in_specs=in_specs, out_specs=out_specs, check_vma=False)
```

```python
import math

import jax
import jax.numpy as jnp
from jax import lax
from jax.experimental import pallas as pl
from jax.experimental.pallas import tpu as pltpu
from jax.sharding import PartitionSpec as P

MESH = pl.DeviceIdType.MESH
DH = 128
GROUPS = 8
ROWS = 192
CTX = 32
HEAD = 8
KEYS = 4 * ROWS
CACHE = 48
TILE = 4
OTHER = -(2.0 ** 20)
LATER = -(2.0 ** 22)
LARGEST = 1e30
START = -(2.0 ** 23)
SCALE = 1.0 / math.sqrt(DH)

LOW, HIGH = 0, 1
PARTS = 1
PIECES = range(2 * PARTS)
GATHER_VMEM = 36 * 1024 * 1024
ATTEND_VMEM = 36 * 1024 * 1024


def transfers():
    out = {}

    def add(name, link, row, dz, half, source):
        out[name] = (link, row, dz, half, source)

    for half, tag in ((LOW, "L"), (HIGH, "H")):
        for d in (1, 2, 3):
            add(f"U{d}{tag}", "up", 0, -d, half, f"U{d - 1}{tag}" if d > 1 else None)
            add(f"D{d}{tag}", "down", 0, d, half, f"D{d - 1}{tag}" if d > 1 else None)
        add(f"Y0{tag}", "y", 1, 0, half, None)
        for d in (1, 2):
            add(f"YU{d}{tag}", "y", 1, -d, half, f"U{d}{tag}")
            add(f"YD{d}{tag}", "y", 1, d, half, f"D{d}{tag}")
        add(f"OU3{tag}", "up", 1, -3, half, f"YU2{tag}")
        add(f"OD3{tag}", "down", 1, 3, half, f"YD2{tag}")
    add("U4L", "up", 0, -4, LOW, "U3L")
    add("D4H", "down", 0, 4, HIGH, "D3H")
    add("OU4L", "up", 1, -4, LOW, "OU3L")
    add("OD4H", "down", 1, 4, HIGH, "OD3H")
    for name in list(out):
        link, row, dz, half, source = out[name]
        add("C" + name, "core", row, dz, half, name)
    add("C0L", "core", 0, 0, LOW, None)
    add("C0H", "core", 0, 0, HIGH, None)
    return {
        f"{name}{tag}": (link, row, dz, half, tag, source and f"{source}{tag}")
        for name, (link, row, dz, half, source) in out.items()
        for tag in PIECES
    }


TRANSFERS = transfers()
SPECIAL = [name for name, entry in TRANSFERS.items() if entry[1] == 1 and entry[3] == HIGH]
INDEX = {name: i for i, name in enumerate(TRANSFERS)}
FORWARDS = {name: [k for k, v in TRANSFERS.items() if v[5] == name] for name in TRANSFERS}
FIRST = [f"{n}{half}{p}" for half in "LH" for p in PIECES for n in ("U1", "D1", "Y0")]
FIRST += [f"C0{half}{p}" for half in "LH" for p in PIECES]

ARRIVALS = [
    ["U1L", "D1L", "Y0L"],
    ["U1H", "D1H", "Y0H"],
    ["U2L", "D2L", "YU1L"],
    ["U2H", "D2H", "YD1L"],
    ["U3L", "D3L", "YU2L"],
    ["U3H", "D3H", "YD2L"],
    ["U4L", "D4H", "YU2H"],
    ["OU3L", "OD3L", "YD2H"],
    ["OU3H", "OD3H", "YU1H"],
    ["OU4L", "OD4H", "YD1H"],
]
LATE, LATE_AFTER = [f"{n}{p}" for p in PIECES for n in ("YU1H", "YD1H")], 5

OWN, NEAR, FAR, OPP = 0, 1, 2, 3
PLAN = [2, 3, (NEAR, LOW), (NEAR, HIGH), 4, 5, (FAR, LOW), (FAR, HIGH), 6, 7, (OPP, LOW), (OPP, HIGH)]
REACH = {OWN: (0, 1), NEAR: (1, 2), FAR: (2, 3), OPP: (3, 4)}


def needs(kind, half):
    return [
        name
        for name, (link, r, dz, hf, _, _) in TRANSFERS.items()
        if link == "core" and r == 0 and hf == half and abs(dz) in REACH[kind]
    ]


def steps_of(plan):
    jobs, before, pending, seen = [], [], [], set(needs(OWN, LOW) + needs(OWN, HIGH))
    for entry in plan:
        if isinstance(entry, int):
            pending.append(entry)
        else:
            jobs.append(entry)
            fresh = [name for name in needs(*entry) if name not in seen]
            seen.update(fresh)
            before.append((pending, fresh))
            pending = []
    rest = [name for name in TRANSFERS if TRANSFERS[name][0] == "core" and name not in seen]
    return jobs, before, rest


JOBS, BEFORE, REST = steps_of(PLAN)


def online(scores, old, held, values):
    parts = [scores[:, i : i + DH] for i in range(0, KEYS, DH)]
    top = parts[0]
    for part in parts[1:]:
        top = jnp.maximum(top, part)
    new = jnp.maximum(old, jnp.max(top, axis=1, keepdims=True))
    weights = jnp.concatenate([jnp.exp((part - new) * SCALE).astype(jnp.bfloat16) for part in parts], axis=1)
    factor = jnp.exp((old - new) * SCALE)
    product = jnp.dot(weights, values, preferred_element_type=jnp.float32)
    return new, held * jnp.concatenate([factor, factor], axis=1) + product


def gather_kernel(q_ref, k_ref, v_ref, seg_ref, buf, kc_ref, vc_ref, qx, acc, peak, kfeat, send, recv, csend, crecv, own):
    c = lax.axis_index("ctx")
    h = lax.axis_index("head")
    y, z, core = c // 16, (c % 16) // 2, c % 2

    def index_of(row, zz, kk):
        return row * 16 + (zz % 8) * 2 + kk

    up_to = index_of(y, z + 1, core)
    down_to = index_of(y, z + 7, core)
    y_to = index_of(1 - y, z, core)
    core_to = index_of(y, z, 1 - core)
    target = {"up": up_to, "down": down_to, "y": y_to, "core": core_to}

    barrier = pltpu.get_barrier_semaphore()
    for peer in (up_to, down_to, y_to, core_to):
        pl.semaphore_signal(barrier, inc=1, device_id=(peer, h), device_id_type=MESH)
    for d in range(1, HEAD):
        pl.semaphore_signal(barrier, inc=1, device_id=(c, (h + d) % HEAD), device_id_type=MESH)
    for half in range(2):
        buf[2 * half, c] = k_ref[half]
        buf[2 * half + 1, c] = v_ref[half]
    pl.semaphore_wait(barrier, 4 + HEAD - 1)

    def copy_of(name):
        link, row, dz, half, piece, source = TRANSFERS[name]
        shift = {"up": 1, "down": -1}.get(link, 0)
        there = y if (row == 0) != (link == "y") else 1 - y
        block = index_of(there, z + dz + shift + 8, core)
        part = pl.ds(piece % PARTS * (ROWS // PARTS), ROWS // PARTS)
        dst = buf.at[2 * half + piece // PARTS, block, part]
        return pltpu.make_async_remote_copy(
            src_ref=dst,
            dst_ref=dst,
            send_sem=send.at[1 if name in SPECIAL else 0],
            recv_sem=recv.at[INDEX[name]],
            device_id=(target[link], h),
            device_id_type=MESH,
        )

    def start(name):
        if name not in SPECIAL:
            copy_of(name).start()
        else:
            pl.when(y == (0 if TRANSFERS[name][0] == "y" else 1))(lambda: copy_of(name).start())

    def wait(name):
        if name not in SPECIAL:
            copy_of(name).wait_recv()
        else:
            pl.when(y == 1)(lambda: copy_of(name).wait_recv())

    for name in FIRST:
        start(name)

    def arrive(event):
        names = [f"{n}{p}" for p in PIECES for n in ARRIVALS[event]]
        for name in names:
            wait(name)
            for onward in FORWARDS[name]:
                if TRANSFERS[onward][0] != "core" and onward not in LATE:
                    start(onward)
        for name in names:
            start("C" + name)
        if event == LATE_AFTER:
            for name in LATE:
                start(name)

    seg = seg_ref[...]
    lane = lax.broadcasted_iota(jnp.int32, (1, DH), 1)
    low = jnp.zeros((1, DH), jnp.float32)
    high = jnp.zeros((1, DH), jnp.float32)
    for s in range(4):
        below = jnp.sum(jnp.where(seg < s, 1.0, 0.0), axis=(0, 1), keepdims=True)
        upto = jnp.sum(jnp.where(seg <= s, 1.0, 0.0), axis=(0, 1), keepdims=True)
        low = jnp.where(lane == s, below, low)
        high = jnp.where(lane == s, upto, high)
    used = jnp.where(lane < 4, 1.0, 0.0)

    def inside(first, rows):
        at = (lax.broadcasted_iota(jnp.int32, (rows, DH), 0) + first).astype(jnp.float32)
        return jnp.where((at >= low) & (at < high), 1.0, 0.0)

    for s in range(2):
        feature = ((used - inside(s * CTX * ROWS + c * ROWS, ROWS)) * OTHER).astype(jnp.bfloat16)
        for g in range(GROUPS):
            qx[s, g, :, :DH] = q_ref[s, :, g * DH : (g + 1) * DH]
            qx[s, g, :, DH:] = feature

    def prepare_keys(i, carry):
        for half in range(2):
            kfeat[half, i] = inside((half * CTX + y * 16 + i) * ROWS, ROWS).astype(jnp.bfloat16)
        return carry

    lax.fori_loop(0, 16, prepare_keys, 0)
    peak[...] = jnp.full(peak.shape, START, jnp.float32)
    acc[...] = jnp.zeros(acc.shape, jnp.float32)

    rows = TILE * ROWS
    ones = jnp.ones((KEYS, DH), jnp.bfloat16)

    def attend(qs, half, block, causal):
        first = block * 4
        keys = buf[2 * half, pl.ds(first, 4)].reshape(KEYS, DH)
        values = buf[2 * half + 1, pl.ds(first, 4)].reshape(KEYS, DH)
        features = kfeat[half, pl.ds(first - y * 16, 4)].reshape(KEYS, DH)
        keys = jnp.concatenate([keys, features], axis=1)
        values = jnp.concatenate([values, ones], axis=1)
        seen = None
        if causal:
            row = lax.broadcasted_iota(jnp.int32, (ROWS, KEYS), 0) + (c - first) * ROWS
            col = lax.broadcasted_iota(jnp.int32, (ROWS, KEYS), 1)
            seen = jnp.concatenate([row >= col] * TILE, axis=0)

        def scores_of(t):
            queries = qx[qs, pl.ds(t * TILE, TILE)].reshape(rows, 2 * DH)
            return lax.dot_general(
                queries, keys, (((1,), (1,)), ((), ())), preferred_element_type=jnp.float32
            )

        scores = scores_of(0)
        for t in range(GROUPS // TILE):
            later = scores_of(t + 1) if t + 1 < GROUPS // TILE else None
            heads = pl.ds(t * TILE, TILE)
            if causal:
                scores = jnp.where(seen, scores, LATER)
            old = peak[qs, heads].reshape(rows, DH)
            held = acc[qs, heads].reshape(rows, 2 * DH)
            new, held = online(scores, old, held, values)
            acc[qs, heads] = held.reshape(TILE, ROWS, 2 * DH)
            peak[qs, heads] = new.reshape(TILE, ROWS, DH)
            scores = later

    zb = z // 2
    mine = y * 4 + zb
    toward = 1 - 2 * (z % 2)

    arrive(0)
    arrive(1)
    for name in needs(OWN, LOW) + needs(OWN, HIGH):
        copy_of(name).wait_recv()

    def own_step(half, carry):
        attend(half, half, mine, True)
        return carry

    lax.fori_loop(0, 2, own_step, 0)

    def step_body(step, carry):
        def pick(values):
            value = jnp.int32(values[0])
            for i in range(1, len(values)):
                value = jnp.where(step == i, jnp.int32(values[i]), value)
            return value

        for i, (events, names) in enumerate(BEFORE):
            if events or names:

                @pl.when(step == i)
                def _(events=events, names=names):
                    for event in events:
                        arrive(event)
                    for name in names:
                        copy_of(name).wait_recv()

        half = pick([job[1] for job in JOBS])
        move = pick([{NEAR: 0, FAR: 0, OPP: 2}[job[0]] for job in JOBS]) + toward * pick(
            [{NEAR: -1, FAR: 1, OPP: 0}[job[0]] for job in JOBS]
        )
        block = y * 4 + (zb + move + 4) % 4
        qs = jnp.where(jnp.logical_or(half == 1, block > mine), 1, 0)

        @pl.when(jnp.logical_or(half == 0, block < mine))
        def _():
            attend(qs, half, block, False)

        return carry

    lax.fori_loop(0, len(JOBS), step_body, 0)
    arrive(8)
    arrive(9)
    for name in REST:
        wait(name)

    page = c // 16
    columns = pl.ds(pl.multiple_of(h * DH, DH), DH)

    def cache_source(kv, to):
        return buf.at[2 * page + kv, 2 * (c % 16) + to // 4, pl.ds(pl.multiple_of(CACHE * (to % 4), 16), CACHE)]

    def cache_copies(d):
        to = (h + d) % HEAD
        return [
            pltpu.make_async_remote_copy(
                src_ref=cache_source(kv, to),
                dst_ref=ref.at[:, columns],
                send_sem=csend.at[kv, d],
                recv_sem=crecv.at[kv, d],
                device_id=(c, to),
                device_id_type=MESH,
            )
            for kv, ref in ((0, kc_ref), (1, vc_ref))
        ]

    for d in range(1, HEAD):
        for copy in cache_copies(d):
            copy.start()
    mine = [
        pltpu.make_async_copy(cache_source(kv, h), ref.at[:, columns], own.at[kv])
        for kv, ref in ((0, kc_ref), (1, vc_ref))
    ]
    for copy in mine:
        copy.start()

    def wait_sent(names, sem):
        halves = 4 if len(names) * 2 % (4 * PARTS * 2) == 0 else 2
        sent = buf.at[pl.ds(0, halves), pl.ds(0, len(names) // (halves * PARTS))]
        pltpu.make_async_remote_copy(
            src_ref=sent,
            dst_ref=sent,
            send_sem=send.at[sem],
            recv_sem=recv.at[0],
            device_id=(core_to, h),
            device_id_type=MESH,
        ).wait_send()

    wait_sent([name for name in TRANSFERS if name not in SPECIAL], 0)
    for row in range(2):
        sent_in_row = [name for name in SPECIAL if (TRANSFERS[name][0] == "y") == (row == 0)]
        pl.when(y == row)(lambda names=sent_in_row: wait_sent(names, 1))
    for copy in mine:
        copy.wait()
    for d in range(1, HEAD):
        for copy in cache_copies(d):
            copy.wait()


def attend_kernel(seg_ref, kin_ref, vin_ref, buf, qx, sums, peaks, out_ref, kc_ref, vc_ref, acc, peak, state):
    c = lax.axis_index("ctx")
    y, mine = c // 16, c // 4
    kc_ref[...] = kin_ref[...]
    vc_ref[...] = vin_ref[...]
    acc[0] = sums[...]
    peak[...] = peaks[...]
    state[0] = 0
    state[1] = 0

    seg = seg_ref[...]
    starts = [jnp.int32(0)] + [
        jnp.sum(jnp.where(seg < s, 1.0, 0.0)).astype(jnp.int32) for s in range(1, 4)
    ] + [jnp.int32(2 * CTX * ROWS)]
    lane = lax.broadcasted_iota(jnp.int32, (1, DH), 1)
    low = jnp.zeros((1, DH), jnp.int32)
    high = jnp.zeros((1, DH), jnp.int32)
    for s in range(4):
        low = jnp.where(lane == s, starts[s], low)
        high = jnp.where(lane == s, starts[s + 1], high)

    def inside(first, rows):
        at = lax.broadcasted_iota(jnp.int32, (rows, DH), 0) + first
        return jnp.where(jnp.logical_and(at >= low, at < high), 1.0, 0.0)

    def segment_start(at):
        begin = jnp.int32(0)
        for start in starts[1:4]:
            begin = jnp.where(start <= at, start, begin)
        return begin

    first, inner = [], []
    for s in range(2):
        at = s * CTX * ROWS + c * ROWS
        first.append(segment_start(at) // KEYS)
        inner.append(segment_start(at + ROWS - 1))
    count = jnp.where(y == 1, jnp.maximum(4 - first[0], 0), 0)
    upper_first = jnp.maximum(first[1], 4 + 4 * y)
    upper_count = jnp.maximum(8 + 4 * y - upper_first, 0)
    total = count + upper_count + jnp.where(first[1] <= mine, 1, 0)

    rows = TILE * ROWS
    ones = jnp.ones((KEYS, DH), jnp.bfloat16)

    def operands(block, featured):
        half, chunk = block // 8, (block % 8) * 4
        keys = buf[2 * half, pl.ds(chunk, 4)].reshape(KEYS, DH)
        values = buf[2 * half + 1, pl.ds(chunk, 4)].reshape(KEYS, DH)
        if featured:
            keys = jnp.concatenate([keys, inside(block * KEYS, KEYS).astype(jnp.bfloat16)], axis=1)
        return keys, values

    def attend(qs, block):
        keys, values = operands(block, True)
        values = jnp.concatenate([values, ones], axis=1)
        now = state[qs]
        for t in range(GROUPS // TILE):
            heads = pl.ds(t * TILE, TILE)
            queries = qx[qs, heads].reshape(rows, 2 * DH)
            scores = lax.dot_general(
                queries, keys, (((1,), (1,)), ((), ())), preferred_element_type=jnp.float32
            )
            old = peak[qs, heads].reshape(rows, DH)
            held = acc[now, qs, heads].reshape(rows, 2 * DH)
            new, held = online(scores, old, held, values)
            acc[now, qs, heads] = held.reshape(TILE, ROWS, 2 * DH)
            peak[qs, heads] = new.reshape(TILE, ROWS, DH)

    def attend_kept(qs, block, featured):
        keys, values = operands(block, featured)
        values = jnp.concatenate([values, ones], axis=1)
        now = state[qs]
        width = keys.shape[1]

        def scores_of(t):
            queries = qx[qs, pl.ds(t * TILE, TILE), :, :width].reshape(rows, width)
            return lax.dot_general(
                queries, keys, (((1,), (1,)), ((), ())), preferred_element_type=jnp.float32
            )

        largest = jnp.zeros((8, DH), jnp.float32)
        scores = scores_of(0)
        for t in range(GROUPS // TILE):
            later = scores_of(t + 1) if t + 1 < GROUPS // TILE else None
            heads = pl.ds(t * TILE, TILE)
            top = peak[qs, heads].reshape(rows, DH)
            weights = jnp.concatenate(
                [jnp.exp((scores[:, i : i + DH] - top) * SCALE).astype(jnp.bfloat16) for i in range(0, KEYS, DH)],
                axis=1,
            )
            product = jnp.dot(weights, values, preferred_element_type=jnp.float32)
            held = acc[now, qs, heads].reshape(rows, 2 * DH) + product
            acc[1 - now, qs, heads] = held.reshape(TILE, ROWS, 2 * DH)
            largest = jnp.maximum(largest, jnp.max(held[:, DH:].reshape(rows // 8, 8, DH), axis=0))
            scores = later
        fits = jnp.max(largest) <= LARGEST
        state[qs] = jnp.where(fits, 1 - now, now)
        state[2] = jnp.where(fits, 0, 1)

    def step(j, carry):
        upper = j >= count
        qs = jnp.where(upper, 1, 0)
        block = jnp.where(upper, jnp.where(j - count < upper_count, upper_first + j - count, mine), first[0] + j)
        plain = block * KEYS >= jnp.where(upper, inner[1], inner[0])

        @pl.when(plain)
        def _():
            attend_kept(qs, block, False)

        @pl.when(jnp.logical_not(plain))
        def _():
            attend_kept(qs, block, True)

        @pl.when(state[2] == 1)
        def _():
            attend(qs, block)

        return carry

    lax.fori_loop(0, total, step, 0)

    def finish(g, carry):
        for s in range(2):
            held = acc[state[s], s, g]
            out_ref[s, :, pl.ds(pl.multiple_of(g * DH, DH), DH)] = (held[:, :DH] / held[:, DH:]).astype(jnp.bfloat16)
        return carry

    lax.fori_loop(0, GROUPS, finish, 0)


def body(queries, key_states, value_states, segment_ids):
    vmem = pl.BlockSpec(memory_space=pltpu.VMEM)
    anywhere = pl.BlockSpec(memory_space=pl.ANY)
    cache = jax.ShapeDtypeStruct((CACHE, HEAD * DH), jnp.bfloat16)
    segments = segment_ids.reshape(-1, DH)
    gathered, keys, values, prepared, sums, peaks = pl.pallas_call(
        gather_kernel,
        out_shape=(
            jax.ShapeDtypeStruct((4, CTX, ROWS, DH), jnp.bfloat16),
            cache,
            cache,
            jax.ShapeDtypeStruct((2, GROUPS, ROWS, 2 * DH), jnp.bfloat16),
            jax.ShapeDtypeStruct((2, GROUPS, ROWS, 2 * DH), jnp.float32),
            jax.ShapeDtypeStruct((2, GROUPS, ROWS, DH), jnp.float32),
        ),
        in_specs=[vmem] * 4,
        out_specs=(vmem, anywhere, anywhere, vmem, vmem, vmem),
        scratch_shapes=[
            pltpu.VMEM((2, 16, ROWS, DH), jnp.bfloat16),
            pltpu.SemaphoreType.DMA((2,)),
            pltpu.SemaphoreType.DMA((len(TRANSFERS),)),
            pltpu.SemaphoreType.DMA((2, HEAD)),
            pltpu.SemaphoreType.DMA((2, HEAD)),
            pltpu.SemaphoreType.DMA((2,)),
        ],
        compiler_params=pltpu.CompilerParams(
            collective_id=0, has_side_effects=True, vmem_limit_bytes=GATHER_VMEM
        ),
        name="gather",
    )(queries, key_states, value_states, segments)
    return pl.pallas_call(
        attend_kernel,
        out_shape=(jax.ShapeDtypeStruct((2, ROWS, GROUPS * DH), jnp.bfloat16), cache, cache),
        in_specs=[vmem] * 7,
        out_specs=(vmem,) * 3,
        scratch_shapes=[
            pltpu.VMEM((2, 2, GROUPS, ROWS, 2 * DH), jnp.float32),
            pltpu.VMEM((2, GROUPS, ROWS, DH), jnp.float32),
            pltpu.SMEM((3,), jnp.int32),
        ],
        compiler_params=pltpu.CompilerParams(vmem_limit_bytes=ATTEND_VMEM),
        name="attend",
    )(segments, keys, values, gathered, prepared, sums, peaks)


def solution(mesh):
    in_specs = (P(None, "ctx", "head"), P(None, "ctx", "head"), P(None, "ctx", "head"), P())
    out_specs = (P(None, "ctx", "head"), P(("ctx", "head"), None), P(("ctx", "head"), None))
    return jax.shard_map(body, mesh=mesh, in_specs=in_specs, out_specs=out_specs, check_vma=False)
```

```python
import math

import jax
import jax.numpy as jnp
from jax import lax
from jax.experimental import pallas as pl
from jax.experimental.pallas import tpu as pltpu
from jax.sharding import PartitionSpec as P

MESH = pl.DeviceIdType.MESH
DH = 128
GROUPS = 8
ROWS = 192
CTX = 32
HEAD = 8
KEYS = 4 * ROWS
CACHE = 48
TILE = 4
OTHER = -(2.0 ** 20)
LATER = -(2.0 ** 22)
LARGEST = 1e30
START = -(2.0 ** 23)
SCALE = 1.0 / math.sqrt(DH)

LOW, HIGH = 0, 1
PARTS = 1
PIECES = range(2 * PARTS)
GATHER_VMEM = 36 * 1024 * 1024
ATTEND_VMEM = 36 * 1024 * 1024


def transfers():
    out = {}

    def add(name, link, row, dz, half, source):
        out[name] = (link, row, dz, half, source)

    for half, tag in ((LOW, "L"), (HIGH, "H")):
        for d in (1, 2, 3):
            add(f"U{d}{tag}", "up", 0, -d, half, f"U{d - 1}{tag}" if d > 1 else None)
            add(f"D{d}{tag}", "down", 0, d, half, f"D{d - 1}{tag}" if d > 1 else None)
        add(f"Y0{tag}", "y", 1, 0, half, None)
        for d in (1, 2):
            add(f"YU{d}{tag}", "y", 1, -d, half, f"U{d}{tag}")
            add(f"YD{d}{tag}", "y", 1, d, half, f"D{d}{tag}")
        add(f"OU3{tag}", "up", 1, -3, half, f"YU2{tag}")
        add(f"OD3{tag}", "down", 1, 3, half, f"YD2{tag}")
    add("U4L", "up", 0, -4, LOW, "U3L")
    add("D4H", "down", 0, 4, HIGH, "D3H")
    add("OU4L", "up", 1, -4, LOW, "OU3L")
    add("OD4H", "down", 1, 4, HIGH, "OD3H")
    for name in list(out):
        link, row, dz, half, source = out[name]
        add("C" + name, "core", row, dz, half, name)
    add("C0L", "core", 0, 0, LOW, None)
    add("C0H", "core", 0, 0, HIGH, None)
    return {
        f"{name}{tag}": (link, row, dz, half, tag, source and f"{source}{tag}")
        for name, (link, row, dz, half, source) in out.items()
        for tag in PIECES
    }


TRANSFERS = transfers()
SPECIAL = [name for name, entry in TRANSFERS.items() if entry[1] == 1 and entry[3] == HIGH]
INDEX = {name: i for i, name in enumerate(TRANSFERS)}
FORWARDS = {name: [k for k, v in TRANSFERS.items() if v[5] == name] for name in TRANSFERS}
FIRST = [f"{n}{half}{p}" for half in "LH" for p in PIECES for n in ("U1", "D1", "Y0")]
FIRST += [f"C0{half}{p}" for half in "LH" for p in PIECES]

ARRIVALS = [
    ["U1L", "D1L", "Y0L"],
    ["U1H", "D1H", "Y0H"],
    ["U2L", "D2L", "YU1L"],
    ["U2H", "D2H", "YD1L"],
    ["U3L", "D3L", "YU2L"],
    ["U3H", "D3H", "YD2L"],
    ["U4L", "D4H", "YU2H"],
    ["OU3L", "OD3L", "YD2H"],
    ["OU3H", "OD3H", "YU1H"],
    ["OU4L", "OD4H", "YD1H"],
]
LATE, LATE_AFTER = [f"{n}{p}" for p in PIECES for n in ("YU1H", "YD1H")], 5

OWN, NEAR, FAR, OPP = 0, 1, 2, 3
PLAN = [
    2, 3, (NEAR, 0, LOW), (NEAR, 0, HIGH), 4, 5, (FAR, 0, LOW), (FAR, 0, HIGH), (OWN, 1, LOW), 6, 7,
    (OPP, 0, LOW), (OPP, 0, HIGH), 8, (NEAR, 1, LOW), 9, (FAR, 1, LOW),
]
REACH = {OWN: (0, 1), NEAR: (1, 2), FAR: (2, 3), OPP: (3, 4)}


def needs(kind, row, half):
    return [
        name
        for name, (link, r, dz, hf, _, _) in TRANSFERS.items()
        if link == "core" and r == row and hf == half and abs(dz) in REACH[kind]
    ]


def steps_of(plan):
    jobs, before, pending, seen = [], [], [], set(needs(OWN, 0, LOW) + needs(OWN, 0, HIGH))
    for entry in plan:
        if isinstance(entry, int):
            pending.append(entry)
        else:
            jobs.append(entry)
            fresh = [name for name in needs(*entry) if name not in seen]
            seen.update(fresh)
            before.append((pending, fresh))
            pending = []
    rest = [name for name in TRANSFERS if TRANSFERS[name][0] == "core" and name not in seen]
    return jobs, before, rest


JOBS, BEFORE, REST = steps_of(PLAN)


def online(scores, old, held, values):
    parts = [scores[:, i : i + DH] for i in range(0, KEYS, DH)]
    top = parts[0]
    for part in parts[1:]:
        top = jnp.maximum(top, part)
    new = jnp.maximum(old, jnp.max(top, axis=1, keepdims=True))
    weights = jnp.concatenate([jnp.exp((part - new) * SCALE).astype(jnp.bfloat16) for part in parts], axis=1)
    factor = jnp.exp((old - new) * SCALE)
    product = jnp.dot(weights, values, preferred_element_type=jnp.float32)
    return new, held * jnp.concatenate([factor, factor], axis=1) + product


def gather_kernel(q_ref, k_ref, v_ref, seg_ref, buf, kc_ref, vc_ref, qx, acc, peak, kfeat, send, recv, csend, crecv, own):
    c = lax.axis_index("ctx")
    h = lax.axis_index("head")
    y, z, core = c // 16, (c % 16) // 2, c % 2

    def index_of(row, zz, kk):
        return row * 16 + (zz % 8) * 2 + kk

    up_to = index_of(y, z + 1, core)
    down_to = index_of(y, z + 7, core)
    y_to = index_of(1 - y, z, core)
    core_to = index_of(y, z, 1 - core)
    target = {"up": up_to, "down": down_to, "y": y_to, "core": core_to}

    barrier = pltpu.get_barrier_semaphore()
    for peer in (up_to, down_to, y_to, core_to):
        pl.semaphore_signal(barrier, inc=1, device_id=(peer, h), device_id_type=MESH)
    for d in range(1, HEAD):
        pl.semaphore_signal(barrier, inc=1, device_id=(c, (h + d) % HEAD), device_id_type=MESH)
    for half in range(2):
        buf[2 * half, c] = k_ref[half]
        buf[2 * half + 1, c] = v_ref[half]
    pl.semaphore_wait(barrier, 4 + HEAD - 1)

    def copy_of(name):
        link, row, dz, half, piece, source = TRANSFERS[name]
        shift = {"up": 1, "down": -1}.get(link, 0)
        there = y if (row == 0) != (link == "y") else 1 - y
        block = index_of(there, z + dz + shift + 8, core)
        part = pl.ds(piece % PARTS * (ROWS // PARTS), ROWS // PARTS)
        dst = buf.at[2 * half + piece // PARTS, block, part]
        return pltpu.make_async_remote_copy(
            src_ref=dst,
            dst_ref=dst,
            send_sem=send.at[1 if name in SPECIAL else 0],
            recv_sem=recv.at[INDEX[name]],
            device_id=(target[link], h),
            device_id_type=MESH,
        )

    def start(name):
        if name not in SPECIAL:
            copy_of(name).start()
        else:
            pl.when(y == (0 if TRANSFERS[name][0] == "y" else 1))(lambda: copy_of(name).start())

    def wait(name):
        if name not in SPECIAL:
            copy_of(name).wait_recv()
        else:
            pl.when(y == 1)(lambda: copy_of(name).wait_recv())

    for name in FIRST:
        start(name)

    def arrive(event):
        names = [f"{n}{p}" for p in PIECES for n in ARRIVALS[event]]
        for name in names:
            wait(name)
            for onward in FORWARDS[name]:
                if TRANSFERS[onward][0] != "core" and onward not in LATE:
                    start(onward)
        for name in names:
            start("C" + name)
        if event == LATE_AFTER:
            for name in LATE:
                start(name)

    seg = seg_ref[...]
    lane = lax.broadcasted_iota(jnp.int32, (1, DH), 1)
    low = jnp.zeros((1, DH), jnp.float32)
    high = jnp.zeros((1, DH), jnp.float32)
    for s in range(4):
        below = jnp.sum(jnp.where(seg < s, 1.0, 0.0), axis=(0, 1), keepdims=True)
        upto = jnp.sum(jnp.where(seg <= s, 1.0, 0.0), axis=(0, 1), keepdims=True)
        low = jnp.where(lane == s, below, low)
        high = jnp.where(lane == s, upto, high)
    used = jnp.where(lane < 4, 1.0, 0.0)

    def inside(first, rows):
        at = (lax.broadcasted_iota(jnp.int32, (rows, DH), 0) + first).astype(jnp.float32)
        return jnp.where((at >= low) & (at < high), 1.0, 0.0)

    for s in range(2):
        feature = ((used - inside(s * CTX * ROWS + c * ROWS, ROWS)) * OTHER).astype(jnp.bfloat16)
        for g in range(GROUPS):
            qx[s, g, :, :DH] = q_ref[s, :, g * DH : (g + 1) * DH]
            qx[s, g, :, DH:] = feature

    def prepare_keys(i, carry):
        for place, chunk in enumerate((y * 16, CTX + y * 16, (1 - y) * 16)):
            kfeat[place, i] = inside((chunk + i) * ROWS, ROWS).astype(jnp.bfloat16)
        return carry

    lax.fori_loop(0, 16, prepare_keys, 0)
    peak[...] = jnp.full(peak.shape, START, jnp.float32)
    acc[...] = jnp.zeros(acc.shape, jnp.float32)

    rows = TILE * ROWS
    ones = jnp.ones((KEYS, DH), jnp.bfloat16)

    def attend(qs, half, block, causal):
        first = block * 4
        keys = buf[2 * half, pl.ds(first, 4)].reshape(KEYS, DH)
        values = buf[2 * half + 1, pl.ds(first, 4)].reshape(KEYS, DH)
        place = jnp.where(half == 1, 1, jnp.where(first // 16 == y, 0, 2))
        features = kfeat[place, pl.ds(first % 16, 4)].reshape(KEYS, DH)
        keys = jnp.concatenate([keys, features], axis=1)
        values = jnp.concatenate([values, ones], axis=1)
        seen = None
        if causal:
            row = lax.broadcasted_iota(jnp.int32, (ROWS, KEYS), 0) + (c - first) * ROWS
            col = lax.broadcasted_iota(jnp.int32, (ROWS, KEYS), 1)
            seen = jnp.concatenate([row >= col] * TILE, axis=0)

        def scores_of(t):
            queries = qx[qs, pl.ds(t * TILE, TILE)].reshape(rows, 2 * DH)
            return lax.dot_general(
                queries, keys, (((1,), (1,)), ((), ())), preferred_element_type=jnp.float32
            )

        scores = scores_of(0)
        for t in range(GROUPS // TILE):
            later = scores_of(t + 1) if t + 1 < GROUPS // TILE else None
            heads = pl.ds(t * TILE, TILE)
            if causal:
                scores = jnp.where(seen, scores, LATER)
            old = peak[qs, heads].reshape(rows, DH)
            held = acc[qs, heads].reshape(rows, 2 * DH)
            new, held = online(scores, old, held, values)
            acc[qs, heads] = held.reshape(TILE, ROWS, 2 * DH)
            peak[qs, heads] = new.reshape(TILE, ROWS, DH)
            scores = later

    zb = z // 2
    mine = y * 4 + zb
    toward = 1 - 2 * (z % 2)

    arrive(0)
    arrive(1)
    for name in needs(OWN, 0, LOW) + needs(OWN, 0, HIGH):
        copy_of(name).wait_recv()

    def own_step(half, carry):
        attend(half, half, mine, True)
        return carry

    lax.fori_loop(0, 2, own_step, 0)

    def step_body(step, carry):
        def pick(values):
            value = jnp.int32(values[0])
            for i in range(1, len(values)):
                value = jnp.where(step == i, jnp.int32(values[i]), value)
            return value

        for i, (events, names) in enumerate(BEFORE):
            if events or names:

                @pl.when(step == i)
                def _(events=events, names=names):
                    for event in events:
                        arrive(event)
                    for name in names:
                        copy_of(name).wait_recv()

        row = pick([job[1] for job in JOBS])
        half = pick([job[2] for job in JOBS])
        move = pick([{OWN: 0, NEAR: 0, FAR: 0, OPP: 2}[job[0]] for job in JOBS]) + toward * pick(
            [{OWN: 0, NEAR: -1, FAR: 1, OPP: 0}[job[0]] for job in JOBS]
        )
        block = jnp.where(row == 0, y, 1 - y) * 4 + (zb + move + 4) % 4
        qs = jnp.where(jnp.logical_or(half == 1, block > mine), 1, 0)

        @pl.when(jnp.logical_or(half == 0, block < mine))
        def _():
            attend(qs, half, block, False)

        return carry

    lax.fori_loop(0, len(JOBS), step_body, 0)
    for name in REST:
        wait(name)

    page = c // 16
    columns = pl.ds(pl.multiple_of(h * DH, DH), DH)

    def cache_source(kv, to):
        return buf.at[2 * page + kv, 2 * (c % 16) + to // 4, pl.ds(pl.multiple_of(CACHE * (to % 4), 16), CACHE)]

    def cache_copies(d):
        to = (h + d) % HEAD
        return [
            pltpu.make_async_remote_copy(
                src_ref=cache_source(kv, to),
                dst_ref=ref.at[:, columns],
                send_sem=csend.at[kv, d],
                recv_sem=crecv.at[kv, d],
                device_id=(c, to),
                device_id_type=MESH,
            )
            for kv, ref in ((0, kc_ref), (1, vc_ref))
        ]

    for d in range(1, HEAD):
        for copy in cache_copies(d):
            copy.start()
    mine = [
        pltpu.make_async_copy(cache_source(kv, h), ref.at[:, columns], own.at[kv])
        for kv, ref in ((0, kc_ref), (1, vc_ref))
    ]
    for copy in mine:
        copy.start()

    def wait_sent(names, sem):
        halves = 4 if len(names) * 2 % (4 * PARTS * 2) == 0 else 2
        sent = buf.at[pl.ds(0, halves), pl.ds(0, len(names) // (halves * PARTS))]
        pltpu.make_async_remote_copy(
            src_ref=sent,
            dst_ref=sent,
            send_sem=send.at[sem],
            recv_sem=recv.at[0],
            device_id=(core_to, h),
            device_id_type=MESH,
        ).wait_send()

    wait_sent([name for name in TRANSFERS if name not in SPECIAL], 0)
    for row in range(2):
        sent_in_row = [name for name in SPECIAL if (TRANSFERS[name][0] == "y") == (row == 0)]
        pl.when(y == row)(lambda names=sent_in_row: wait_sent(names, 1))
    for copy in mine:
        copy.wait()
    for d in range(1, HEAD):
        for copy in cache_copies(d):
            copy.wait()


def attend_kernel(seg_ref, kin_ref, vin_ref, buf, qx, sums, peaks, out_ref, kc_ref, vc_ref, acc, peak, state):
    c = lax.axis_index("ctx")
    y, mine = c // 16, c // 4
    kc_ref[...] = kin_ref[...]
    vc_ref[...] = vin_ref[...]
    acc[0] = sums[...]
    peak[...] = peaks[...]
    state[0] = 0
    state[1] = 0

    seg = seg_ref[...]
    starts = [jnp.int32(0)] + [
        jnp.sum(jnp.where(seg < s, 1.0, 0.0)).astype(jnp.int32) for s in range(1, 4)
    ] + [jnp.int32(2 * CTX * ROWS)]
    lane = lax.broadcasted_iota(jnp.int32, (1, DH), 1)
    low = jnp.zeros((1, DH), jnp.int32)
    high = jnp.zeros((1, DH), jnp.int32)
    for s in range(4):
        low = jnp.where(lane == s, starts[s], low)
        high = jnp.where(lane == s, starts[s + 1], high)

    def inside(first, rows):
        at = lax.broadcasted_iota(jnp.int32, (rows, DH), 0) + first
        return jnp.where(jnp.logical_and(at >= low, at < high), 1.0, 0.0)

    def segment_start(at):
        begin = jnp.int32(0)
        for start in starts[1:4]:
            begin = jnp.where(start <= at, start, begin)
        return begin

    first, inner = [], []
    for s in range(2):
        at = s * CTX * ROWS + c * ROWS
        first.append(segment_start(at) // KEYS)
        inner.append(segment_start(at + ROWS - 1))
    opposite = (1 - y) * 4 + (mine + 2) % 4
    count = jnp.where(jnp.where(y == 1, first[0], first[1]) <= opposite, 1, 0)
    high_first = jnp.maximum(first[1], 8)
    high_count = jnp.where(y == 1, jnp.maximum(12 - high_first, 0), 0)
    total = count + high_count + jnp.where(first[1] <= mine, 1, 0)

    rows = TILE * ROWS
    ones = jnp.ones((KEYS, DH), jnp.bfloat16)

    def operands(block, featured):
        half, chunk = block // 8, (block % 8) * 4
        keys = buf[2 * half, pl.ds(chunk, 4)].reshape(KEYS, DH)
        values = buf[2 * half + 1, pl.ds(chunk, 4)].reshape(KEYS, DH)
        if featured:
            keys = jnp.concatenate([keys, inside(block * KEYS, KEYS).astype(jnp.bfloat16)], axis=1)
        return keys, values

    def attend(qs, block):
        keys, values = operands(block, True)
        values = jnp.concatenate([values, ones], axis=1)
        now = state[qs]
        for t in range(GROUPS // TILE):
            heads = pl.ds(t * TILE, TILE)
            queries = qx[qs, heads].reshape(rows, 2 * DH)
            scores = lax.dot_general(
                queries, keys, (((1,), (1,)), ((), ())), preferred_element_type=jnp.float32
            )
            old = peak[qs, heads].reshape(rows, DH)
            held = acc[now, qs, heads].reshape(rows, 2 * DH)
            new, held = online(scores, old, held, values)
            acc[now, qs, heads] = held.reshape(TILE, ROWS, 2 * DH)
            peak[qs, heads] = new.reshape(TILE, ROWS, DH)

    def attend_kept(qs, block, featured):
        keys, values = operands(block, featured)
        values = jnp.concatenate([values, ones], axis=1)
        now = state[qs]
        width = keys.shape[1]

        def scores_of(t):
            queries = qx[qs, pl.ds(t * TILE, TILE), :, :width].reshape(rows, width)
            return lax.dot_general(
                queries, keys, (((1,), (1,)), ((), ())), preferred_element_type=jnp.float32
            )

        largest = jnp.zeros((8, DH), jnp.float32)
        scores = scores_of(0)
        for t in range(GROUPS // TILE):
            later = scores_of(t + 1) if t + 1 < GROUPS // TILE else None
            heads = pl.ds(t * TILE, TILE)
            top = peak[qs, heads].reshape(rows, DH)
            weights = jnp.concatenate(
                [jnp.exp((scores[:, i : i + DH] - top) * SCALE).astype(jnp.bfloat16) for i in range(0, KEYS, DH)],
                axis=1,
            )
            product = jnp.dot(weights, values, preferred_element_type=jnp.float32)
            held = acc[now, qs, heads].reshape(rows, 2 * DH) + product
            acc[1 - now, qs, heads] = held.reshape(TILE, ROWS, 2 * DH)
            largest = jnp.maximum(largest, jnp.max(held[:, DH:].reshape(rows // 8, 8, DH), axis=0))
            scores = later
        fits = jnp.max(largest) <= LARGEST
        state[qs] = jnp.where(fits, 1 - now, now)
        state[2] = jnp.where(fits, 0, 1)

    def step(j, carry):
        upper = jnp.logical_or(j >= count, y == 0)
        qs = jnp.where(upper, 1, 0)
        high = j - count
        block = jnp.where(high < 0, opposite, jnp.where(high < high_count, high_first + high, mine))
        plain = block * KEYS >= jnp.where(upper, inner[1], inner[0])

        @pl.when(plain)
        def _():
            attend_kept(qs, block, False)

        @pl.when(jnp.logical_not(plain))
        def _():
            attend_kept(qs, block, True)

        @pl.when(state[2] == 1)
        def _():
            attend(qs, block)

        return carry

    lax.fori_loop(0, total, step, 0)

    def finish(g, carry):
        for s in range(2):
            held = acc[state[s], s, g]
            out_ref[s, :, pl.ds(pl.multiple_of(g * DH, DH), DH)] = (held[:, :DH] / held[:, DH:]).astype(jnp.bfloat16)
        return carry

    lax.fori_loop(0, GROUPS, finish, 0)


def body(queries, key_states, value_states, segment_ids):
    vmem = pl.BlockSpec(memory_space=pltpu.VMEM)
    anywhere = pl.BlockSpec(memory_space=pl.ANY)
    cache = jax.ShapeDtypeStruct((CACHE, HEAD * DH), jnp.bfloat16)
    segments = segment_ids.reshape(-1, DH)
    gathered, keys, values, prepared, sums, peaks = pl.pallas_call(
        gather_kernel,
        out_shape=(
            jax.ShapeDtypeStruct((4, CTX, ROWS, DH), jnp.bfloat16),
            cache,
            cache,
            jax.ShapeDtypeStruct((2, GROUPS, ROWS, 2 * DH), jnp.bfloat16),
            jax.ShapeDtypeStruct((2, GROUPS, ROWS, 2 * DH), jnp.float32),
            jax.ShapeDtypeStruct((2, GROUPS, ROWS, DH), jnp.float32),
        ),
        in_specs=[vmem] * 4,
        out_specs=(vmem, anywhere, anywhere, vmem, vmem, vmem),
        scratch_shapes=[
            pltpu.VMEM((3, 16, ROWS, DH), jnp.bfloat16),
            pltpu.SemaphoreType.DMA((2,)),
            pltpu.SemaphoreType.DMA((len(TRANSFERS),)),
            pltpu.SemaphoreType.DMA((2, HEAD)),
            pltpu.SemaphoreType.DMA((2, HEAD)),
            pltpu.SemaphoreType.DMA((2,)),
        ],
        compiler_params=pltpu.CompilerParams(
            collective_id=0, has_side_effects=True, vmem_limit_bytes=GATHER_VMEM
        ),
        name="gather",
    )(queries, key_states, value_states, segments)
    return pl.pallas_call(
        attend_kernel,
        out_shape=(jax.ShapeDtypeStruct((2, ROWS, GROUPS * DH), jnp.bfloat16), cache, cache),
        in_specs=[vmem] * 7,
        out_specs=(vmem,) * 3,
        scratch_shapes=[
            pltpu.VMEM((2, 2, GROUPS, ROWS, 2 * DH), jnp.float32),
            pltpu.VMEM((2, GROUPS, ROWS, DH), jnp.float32),
            pltpu.SMEM((3,), jnp.int32),
        ],
        compiler_params=pltpu.CompilerParams(vmem_limit_bytes=ATTEND_VMEM),
        name="attend",
    )(segments, keys, values, gathered, prepared, sums, peaks)


def solution(mesh):
    in_specs = (P(None, "ctx", "head"), P(None, "ctx", "head"), P(None, "ctx", "head"), P())
    out_specs = (P(None, "ctx", "head"), P(("ctx", "head"), None), P(("ctx", "head"), None))
    return jax.shard_map(body, mesh=mesh, in_specs=in_specs, out_specs=out_specs, check_vma=False)
```

```python
import math

import jax
import jax.numpy as jnp
from jax import lax
from jax.experimental import pallas as pl
from jax.experimental.pallas import tpu as pltpu
from jax.sharding import PartitionSpec as P

MESH = pl.DeviceIdType.MESH
DH = 128
GROUPS = 8
ROWS = 192
CTX = 32
HEAD = 8
KEYS = 4 * ROWS
CACHE = 48
TILE = 4
OTHER = -(2.0 ** 20)
LATER = -(2.0 ** 22)
LARGEST = 1e30
START = -(2.0 ** 23)
SCALE = 1.0 / math.sqrt(DH)

LOW, HIGH = 0, 1
PARTS = 1
PIECES = range(2 * PARTS)
GATHER_VMEM = 36 * 1024 * 1024
ATTEND_VMEM = 36 * 1024 * 1024


def transfers():
    out = {}

    def add(name, link, row, dz, half, source):
        out[name] = (link, row, dz, half, source)

    for half, tag in ((LOW, "L"), (HIGH, "H")):
        for d in (1, 2, 3):
            add(f"U{d}{tag}", "up", 0, -d, half, f"U{d - 1}{tag}" if d > 1 else None)
            add(f"D{d}{tag}", "down", 0, d, half, f"D{d - 1}{tag}" if d > 1 else None)
        add(f"Y0{tag}", "y", 1, 0, half, None)
        for d in (1, 2):
            add(f"YU{d}{tag}", "y", 1, -d, half, f"U{d}{tag}")
            add(f"YD{d}{tag}", "y", 1, d, half, f"D{d}{tag}")
        add(f"OU3{tag}", "up", 1, -3, half, f"YU2{tag}")
        add(f"OD3{tag}", "down", 1, 3, half, f"YD2{tag}")
    add("U4L", "up", 0, -4, LOW, "U3L")
    add("D4H", "down", 0, 4, HIGH, "D3H")
    add("OU4L", "up", 1, -4, LOW, "OU3L")
    add("OD4H", "down", 1, 4, HIGH, "OD3H")
    for name in list(out):
        link, row, dz, half, source = out[name]
        add("C" + name, "core", row, dz, half, name)
    add("C0L", "core", 0, 0, LOW, None)
    add("C0H", "core", 0, 0, HIGH, None)
    return {
        f"{name}{tag}": (link, row, dz, half, tag, source and f"{source}{tag}")
        for name, (link, row, dz, half, source) in out.items()
        for tag in PIECES
    }


TRANSFERS = transfers()
SPECIAL = [name for name, entry in TRANSFERS.items() if entry[1] == 1 and entry[3] == HIGH]
INDEX = {name: i for i, name in enumerate(TRANSFERS)}
FORWARDS = {name: [k for k, v in TRANSFERS.items() if v[5] == name] for name in TRANSFERS}
FIRST = [f"{n}{half}{p}" for half in "LH" for p in PIECES for n in ("U1", "D1", "Y0")]
FIRST += [f"C0{half}{p}" for half in "LH" for p in PIECES]

ARRIVALS = [
    ["U1L", "D1L", "Y0L"],
    ["U1H", "D1H", "Y0H"],
    ["U2L", "D2L", "YU1L"],
    ["U2H", "D2H", "YD1L"],
    ["U3L", "D3L", "YU2L"],
    ["U3H", "D3H", "YD2L"],
    ["U4L", "D4H", "YU2H"],
    ["OU3L", "OD3L", "YD2H"],
    ["OU3H", "OD3H", "YU1H"],
    ["OU4L", "OD4H", "YD1H"],
]
LATE, LATE_AFTER = [f"{n}{p}" for p in PIECES for n in ("YU1H", "YD1H")], 5

OWN, NEAR, FAR, OPP = 0, 1, 2, 3
PLAN = [
    6, (NEAR, 0, LOW), 7, (NEAR, 0, HIGH), (FAR, 0, LOW), 8, (FAR, 0, HIGH), (OWN, 1, LOW), 9, (OPP, 0, LOW),
    (OPP, 0, HIGH), (NEAR, 1, LOW), (FAR, 1, LOW),
]
CACHE_AT = 8
REACH = {OWN: (0, 1), NEAR: (1, 2), FAR: (2, 3), OPP: (3, 4)}


def needs(kind, row, half):
    return [
        name
        for name, (link, r, dz, hf, _, _) in TRANSFERS.items()
        if link == "core" and r == row and hf == half and abs(dz) in REACH[kind]
    ]


def steps_of(plan):
    jobs, before, pending, seen = [], [], [], set(needs(OWN, 0, LOW) + needs(OWN, 0, HIGH))
    for entry in plan:
        if isinstance(entry, int):
            pending.append(entry)
        else:
            jobs.append(entry)
            fresh = [name for name in needs(*entry) if name not in seen]
            seen.update(fresh)
            before.append((pending, fresh))
            pending = []
    rest = [name for name in TRANSFERS if TRANSFERS[name][0] == "core" and name not in seen]
    return jobs, before, rest


JOBS, BEFORE, REST = steps_of(PLAN)


def online(scores, old, held, values):
    parts = [scores[:, i : i + DH] for i in range(0, KEYS, DH)]
    top = parts[0]
    for part in parts[1:]:
        top = jnp.maximum(top, part)
    new = jnp.maximum(old, jnp.max(top, axis=1, keepdims=True))
    weights = jnp.concatenate([jnp.exp((part - new) * SCALE).astype(jnp.bfloat16) for part in parts], axis=1)
    factor = jnp.exp((old - new) * SCALE)
    product = jnp.dot(weights, values, preferred_element_type=jnp.float32)
    return new, held * jnp.concatenate([factor, factor], axis=1) + product


def gather_kernel(q_ref, k_ref, v_ref, seg_ref, buf, kc_ref, vc_ref, qx, acc, peak, kfeat, send, recv, csend, crecv, own):
    c = lax.axis_index("ctx")
    h = lax.axis_index("head")
    y, z, core = c // 16, (c % 16) // 2, c % 2

    def index_of(row, zz, kk):
        return row * 16 + (zz % 8) * 2 + kk

    up_to = index_of(y, z + 1, core)
    down_to = index_of(y, z + 7, core)
    y_to = index_of(1 - y, z, core)
    core_to = index_of(y, z, 1 - core)
    target = {"up": up_to, "down": down_to, "y": y_to, "core": core_to}

    barrier = pltpu.get_barrier_semaphore()
    for peer in (up_to, down_to, y_to, core_to):
        pl.semaphore_signal(barrier, inc=1, device_id=(peer, h), device_id_type=MESH)
    for d in range(1, HEAD):
        pl.semaphore_signal(barrier, inc=1, device_id=(c, (h + d) % HEAD), device_id_type=MESH)
    for half in range(2):
        buf[2 * half, c] = k_ref[half]
        buf[2 * half + 1, c] = v_ref[half]
    pl.semaphore_wait(barrier, 4 + HEAD - 1)

    def copy_of(name):
        link, row, dz, half, piece, source = TRANSFERS[name]
        shift = {"up": 1, "down": -1}.get(link, 0)
        there = y if (row == 0) != (link == "y") else 1 - y
        block = index_of(there, z + dz + shift + 8, core)
        part = pl.ds(piece % PARTS * (ROWS // PARTS), ROWS // PARTS)
        dst = buf.at[2 * half + piece // PARTS, block, part]
        return pltpu.make_async_remote_copy(
            src_ref=dst,
            dst_ref=dst,
            send_sem=send.at[1 if name in SPECIAL else 0],
            recv_sem=recv.at[INDEX[name]],
            device_id=(target[link], h),
            device_id_type=MESH,
        )

    def start(name):
        if name not in SPECIAL:
            copy_of(name).start()
        else:
            pl.when(y == (0 if TRANSFERS[name][0] == "y" else 1))(lambda: copy_of(name).start())

    def wait(name):
        if name not in SPECIAL:
            copy_of(name).wait_recv()
        else:
            pl.when(y == 1)(lambda: copy_of(name).wait_recv())

    for name in FIRST:
        start(name)

    def arrive(event):
        names = [f"{n}{p}" for p in PIECES for n in ARRIVALS[event]]
        for name in names:
            wait(name)
            for onward in FORWARDS[name]:
                if TRANSFERS[onward][0] != "core" and onward not in LATE:
                    start(onward)
        for name in names:
            start("C" + name)
        if event == LATE_AFTER:
            for name in LATE:
                start(name)

    seg = seg_ref[...]
    lane = lax.broadcasted_iota(jnp.int32, (1, DH), 1)
    low = jnp.zeros((1, DH), jnp.float32)
    high = jnp.zeros((1, DH), jnp.float32)
    for s in range(4):
        below = jnp.sum(jnp.where(seg < s, 1.0, 0.0), axis=(0, 1), keepdims=True)
        upto = jnp.sum(jnp.where(seg <= s, 1.0, 0.0), axis=(0, 1), keepdims=True)
        low = jnp.where(lane == s, below, low)
        high = jnp.where(lane == s, upto, high)
    used = jnp.where(lane < 4, 1.0, 0.0)

    def inside(first, rows):
        at = (lax.broadcasted_iota(jnp.int32, (rows, DH), 0) + first).astype(jnp.float32)
        return jnp.where((at >= low) & (at < high), 1.0, 0.0)

    for s in range(2):
        feature = ((used - inside(s * CTX * ROWS + c * ROWS, ROWS)) * OTHER).astype(jnp.bfloat16)
        for g in range(GROUPS):
            qx[s, g, :, :DH] = q_ref[s, :, g * DH : (g + 1) * DH]
            qx[s, g, :, DH:] = feature

    def prepare_keys(i, carry):
        for place, chunk in enumerate((y * 16, CTX + y * 16, (1 - y) * 16)):
            kfeat[place, i] = inside((chunk + i) * ROWS, ROWS).astype(jnp.bfloat16)
        return carry

    lax.fori_loop(0, 16, prepare_keys, 0)
    peak[...] = jnp.full(peak.shape, START, jnp.float32)
    acc[...] = jnp.zeros(acc.shape, jnp.float32)

    rows = TILE * ROWS
    ones = jnp.ones((KEYS, DH), jnp.bfloat16)

    def attend(qs, half, block, causal):
        first = block * 4
        keys = buf[2 * half, pl.ds(first, 4)].reshape(KEYS, DH)
        values = buf[2 * half + 1, pl.ds(first, 4)].reshape(KEYS, DH)
        place = jnp.where(half == 1, 1, jnp.where(first // 16 == y, 0, 2))
        features = kfeat[place, pl.ds(first % 16, 4)].reshape(KEYS, DH)
        keys = jnp.concatenate([keys, features], axis=1)
        values = jnp.concatenate([values, ones], axis=1)
        seen = None
        if causal:
            row = lax.broadcasted_iota(jnp.int32, (ROWS, KEYS), 0) + (c - first) * ROWS
            col = lax.broadcasted_iota(jnp.int32, (ROWS, KEYS), 1)
            seen = jnp.concatenate([row >= col] * TILE, axis=0)

        def scores_of(t):
            queries = qx[qs, pl.ds(t * TILE, TILE)].reshape(rows, 2 * DH)
            return lax.dot_general(
                queries, keys, (((1,), (1,)), ((), ())), preferred_element_type=jnp.float32
            )

        scores = scores_of(0)
        for t in range(GROUPS // TILE):
            later = scores_of(t + 1) if t + 1 < GROUPS // TILE else None
            heads = pl.ds(t * TILE, TILE)
            if causal:
                scores = jnp.where(seen, scores, LATER)
            old = peak[qs, heads].reshape(rows, DH)
            held = acc[qs, heads].reshape(rows, 2 * DH)
            new, held = online(scores, old, held, values)
            acc[qs, heads] = held.reshape(TILE, ROWS, 2 * DH)
            peak[qs, heads] = new.reshape(TILE, ROWS, DH)
            scores = later

    zb = z // 2
    mine = y * 4 + zb
    toward = 1 - 2 * (z % 2)

    for event in range(6):
        arrive(event)
    for name in needs(OWN, 0, LOW) + needs(OWN, 0, HIGH):
        copy_of(name).wait_recv()

    def own_step(half, carry):
        attend(half, half, mine, True)
        return carry

    lax.fori_loop(0, 2, own_step, 0)

    page = c // 16
    columns = pl.ds(pl.multiple_of(h * DH, DH), DH)

    def cache_source(kv, to):
        return buf.at[2 * page + kv, 2 * (c % 16) + to // 4, pl.ds(pl.multiple_of(CACHE * (to % 4), 16), CACHE)]

    def cache_copies(d):
        to = (h + d) % HEAD
        return [
            pltpu.make_async_remote_copy(
                src_ref=cache_source(kv, to),
                dst_ref=ref.at[:, columns],
                send_sem=csend.at[kv, d],
                recv_sem=crecv.at[kv, d],
                device_id=(c, to),
                device_id_type=MESH,
            )
            for kv, ref in ((0, kc_ref), (1, vc_ref))
        ]

    local_copies = [
        pltpu.make_async_copy(cache_source(kv, h), ref.at[:, columns], own.at[kv])
        for kv, ref in ((0, kc_ref), (1, vc_ref))
    ]

    def start_cache():
        for name in REST:
            wait(name)
        for d in range(1, HEAD):
            for copy in cache_copies(d):
                copy.start()
        for copy in local_copies:
            copy.start()

    def step_body(step, carry):
        def pick(values):
            value = jnp.int32(values[0])
            for i in range(1, len(values)):
                value = jnp.where(step == i, jnp.int32(values[i]), value)
            return value

        for i, (events, names) in enumerate(BEFORE):
            if events or names:

                @pl.when(step == i)
                def _(events=events, names=names):
                    for event in events:
                        arrive(event)
                    for name in names:
                        copy_of(name).wait_recv()

        pl.when(step == CACHE_AT)(start_cache)

        row = pick([job[1] for job in JOBS])
        half = pick([job[2] for job in JOBS])
        move = pick([{OWN: 0, NEAR: 0, FAR: 0, OPP: 2}[job[0]] for job in JOBS]) + toward * pick(
            [{OWN: 0, NEAR: -1, FAR: 1, OPP: 0}[job[0]] for job in JOBS]
        )
        block = jnp.where(row == 0, y, 1 - y) * 4 + (zb + move + 4) % 4
        qs = jnp.where(jnp.logical_or(half == 1, block > mine), 1, 0)

        @pl.when(jnp.logical_or(half == 0, block < mine))
        def _():
            attend(qs, half, block, False)

        return carry

    lax.fori_loop(0, len(JOBS), step_body, 0)

    def wait_sent(names, sem):
        halves = 4 if len(names) * 2 % (4 * PARTS * 2) == 0 else 2
        sent = buf.at[pl.ds(0, halves), pl.ds(0, len(names) // (halves * PARTS))]
        pltpu.make_async_remote_copy(
            src_ref=sent,
            dst_ref=sent,
            send_sem=send.at[sem],
            recv_sem=recv.at[0],
            device_id=(core_to, h),
            device_id_type=MESH,
        ).wait_send()

    wait_sent([name for name in TRANSFERS if name not in SPECIAL], 0)
    for row in range(2):
        sent_in_row = [name for name in SPECIAL if (TRANSFERS[name][0] == "y") == (row == 0)]
        pl.when(y == row)(lambda names=sent_in_row: wait_sent(names, 1))
    for copy in local_copies:
        copy.wait()
    for d in range(1, HEAD):
        for copy in cache_copies(d):
            copy.wait()


def attend_kernel(seg_ref, kin_ref, vin_ref, buf, qx, sums, peaks, out_ref, kc_ref, vc_ref, acc, peak, state):
    c = lax.axis_index("ctx")
    y, mine = c // 16, c // 4
    kc_ref[...] = kin_ref[...]
    vc_ref[...] = vin_ref[...]
    acc[0] = sums[...]
    peak[...] = peaks[...]
    state[0] = 0
    state[1] = 0

    seg = seg_ref[...]
    starts = [jnp.int32(0)] + [
        jnp.sum(jnp.where(seg < s, 1.0, 0.0)).astype(jnp.int32) for s in range(1, 4)
    ] + [jnp.int32(2 * CTX * ROWS)]
    lane = lax.broadcasted_iota(jnp.int32, (1, DH), 1)
    low = jnp.zeros((1, DH), jnp.int32)
    high = jnp.zeros((1, DH), jnp.int32)
    for s in range(4):
        low = jnp.where(lane == s, starts[s], low)
        high = jnp.where(lane == s, starts[s + 1], high)

    def inside(first, rows):
        at = lax.broadcasted_iota(jnp.int32, (rows, DH), 0) + first
        return jnp.where(jnp.logical_and(at >= low, at < high), 1.0, 0.0)

    def segment_start(at):
        begin = jnp.int32(0)
        for start in starts[1:4]:
            begin = jnp.where(start <= at, start, begin)
        return begin

    first, inner = [], []
    for s in range(2):
        at = s * CTX * ROWS + c * ROWS
        first.append(segment_start(at) // KEYS)
        inner.append(segment_start(at + ROWS - 1))
    opposite = (1 - y) * 4 + (mine + 2) % 4
    count = jnp.where(jnp.where(y == 1, first[0], first[1]) <= opposite, 1, 0)
    high_first = jnp.maximum(first[1], 8)
    high_count = jnp.where(y == 1, jnp.maximum(12 - high_first, 0), 0)
    total = count + high_count + jnp.where(first[1] <= mine, 1, 0)

    rows = TILE * ROWS
    ones = jnp.ones((KEYS, DH), jnp.bfloat16)

    def operands(block, featured):
        half, chunk = block // 8, (block % 8) * 4
        keys = buf[2 * half, pl.ds(chunk, 4)].reshape(KEYS, DH)
        values = buf[2 * half + 1, pl.ds(chunk, 4)].reshape(KEYS, DH)
        if featured:
            keys = jnp.concatenate([keys, inside(block * KEYS, KEYS).astype(jnp.bfloat16)], axis=1)
        return keys, values

    def attend(qs, block):
        keys, values = operands(block, True)
        values = jnp.concatenate([values, ones], axis=1)
        now = state[qs]
        for t in range(GROUPS // TILE):
            heads = pl.ds(t * TILE, TILE)
            queries = qx[qs, heads].reshape(rows, 2 * DH)
            scores = lax.dot_general(
                queries, keys, (((1,), (1,)), ((), ())), preferred_element_type=jnp.float32
            )
            old = peak[qs, heads].reshape(rows, DH)
            held = acc[now, qs, heads].reshape(rows, 2 * DH)
            new, held = online(scores, old, held, values)
            acc[now, qs, heads] = held.reshape(TILE, ROWS, 2 * DH)
            peak[qs, heads] = new.reshape(TILE, ROWS, DH)

    def attend_kept(qs, block, featured):
        keys, values = operands(block, featured)
        values = jnp.concatenate([values, ones], axis=1)
        now = state[qs]
        width = keys.shape[1]

        def scores_of(t):
            queries = qx[qs, pl.ds(t * TILE, TILE), :, :width].reshape(rows, width)
            return lax.dot_general(
                queries, keys, (((1,), (1,)), ((), ())), preferred_element_type=jnp.float32
            )

        largest = jnp.zeros((8, DH), jnp.float32)
        scores = scores_of(0)
        for t in range(GROUPS // TILE):
            later = scores_of(t + 1) if t + 1 < GROUPS // TILE else None
            heads = pl.ds(t * TILE, TILE)
            top = peak[qs, heads].reshape(rows, DH)
            weights = jnp.concatenate(
                [jnp.exp((scores[:, i : i + DH] - top) * SCALE).astype(jnp.bfloat16) for i in range(0, KEYS, DH)],
                axis=1,
            )
            product = jnp.dot(weights, values, preferred_element_type=jnp.float32)
            held = acc[now, qs, heads].reshape(rows, 2 * DH) + product
            acc[1 - now, qs, heads] = held.reshape(TILE, ROWS, 2 * DH)
            largest = jnp.maximum(largest, jnp.max(held[:, DH:].reshape(rows // 8, 8, DH), axis=0))
            scores = later
        fits = jnp.max(largest) <= LARGEST
        state[qs] = jnp.where(fits, 1 - now, now)
        state[2] = jnp.where(fits, 0, 1)

    def step(j, carry):
        upper = jnp.logical_or(j >= count, y == 0)
        qs = jnp.where(upper, 1, 0)
        high = j - count
        block = jnp.where(high < 0, opposite, jnp.where(high < high_count, high_first + high, mine))
        plain = block * KEYS >= jnp.where(upper, inner[1], inner[0])

        @pl.when(plain)
        def _():
            attend_kept(qs, block, False)

        @pl.when(jnp.logical_not(plain))
        def _():
            attend_kept(qs, block, True)

        @pl.when(state[2] == 1)
        def _():
            attend(qs, block)

        return carry

    lax.fori_loop(0, total, step, 0)

    def finish(g, carry):
        for s in range(2):
            held = acc[state[s], s, g]
            out_ref[s, :, pl.ds(pl.multiple_of(g * DH, DH), DH)] = (held[:, :DH] / held[:, DH:]).astype(jnp.bfloat16)
        return carry

    lax.fori_loop(0, GROUPS, finish, 0)


def body(queries, key_states, value_states, segment_ids):
    vmem = pl.BlockSpec(memory_space=pltpu.VMEM)
    anywhere = pl.BlockSpec(memory_space=pl.ANY)
    cache = jax.ShapeDtypeStruct((CACHE, HEAD * DH), jnp.bfloat16)
    segments = segment_ids.reshape(-1, DH)
    gathered, keys, values, prepared, sums, peaks = pl.pallas_call(
        gather_kernel,
        out_shape=(
            jax.ShapeDtypeStruct((4, CTX, ROWS, DH), jnp.bfloat16),
            cache,
            cache,
            jax.ShapeDtypeStruct((2, GROUPS, ROWS, 2 * DH), jnp.bfloat16),
            jax.ShapeDtypeStruct((2, GROUPS, ROWS, 2 * DH), jnp.float32),
            jax.ShapeDtypeStruct((2, GROUPS, ROWS, DH), jnp.float32),
        ),
        in_specs=[vmem] * 4,
        out_specs=(vmem, anywhere, anywhere, vmem, vmem, vmem),
        scratch_shapes=[
            pltpu.VMEM((3, 16, ROWS, DH), jnp.bfloat16),
            pltpu.SemaphoreType.DMA((2,)),
            pltpu.SemaphoreType.DMA((len(TRANSFERS),)),
            pltpu.SemaphoreType.DMA((2, HEAD)),
            pltpu.SemaphoreType.DMA((2, HEAD)),
            pltpu.SemaphoreType.DMA((2,)),
        ],
        compiler_params=pltpu.CompilerParams(
            collective_id=0, has_side_effects=True, vmem_limit_bytes=GATHER_VMEM
        ),
        name="gather",
    )(queries, key_states, value_states, segments)
    return pl.pallas_call(
        attend_kernel,
        out_shape=(jax.ShapeDtypeStruct((2, ROWS, GROUPS * DH), jnp.bfloat16), cache, cache),
        in_specs=[vmem] * 7,
        out_specs=(vmem,) * 3,
        scratch_shapes=[
            pltpu.VMEM((2, 2, GROUPS, ROWS, 2 * DH), jnp.float32),
            pltpu.VMEM((2, GROUPS, ROWS, DH), jnp.float32),
            pltpu.SMEM((3,), jnp.int32),
        ],
        compiler_params=pltpu.CompilerParams(vmem_limit_bytes=ATTEND_VMEM),
        name="attend",
    )(segments, keys, values, gathered, prepared, sums, peaks)


def solution(mesh):
    in_specs = (P(None, "ctx", "head"), P(None, "ctx", "head"), P(None, "ctx", "head"), P())
    out_specs = (P(None, "ctx", "head"), P(("ctx", "head"), None), P(("ctx", "head"), None))
    return jax.shard_map(body, mesh=mesh, in_specs=in_specs, out_specs=out_specs, check_vma=False)
```

```python
import math

import jax
import jax.numpy as jnp
from jax import lax
from jax.experimental import pallas as pl
from jax.experimental.pallas import tpu as pltpu
from jax.sharding import PartitionSpec as P

MESH = pl.DeviceIdType.MESH
DH = 128
GROUPS = 8
ROWS = 192
CTX = 32
HEAD = 8
KEYS = 4 * ROWS
CACHE = 48
TILE = 4
OTHER = -(2.0 ** 20)
LATER = -(2.0 ** 22)
LARGEST = 1e30
START = -(2.0 ** 23)
SCALE = 1.0 / math.sqrt(DH)

LOW, HIGH = 0, 1
PARTS = 1
PIECES = range(2 * PARTS)
GATHER_VMEM = 36 * 1024 * 1024
ATTEND_VMEM = 36 * 1024 * 1024


def transfers():
    out = {}

    def add(name, link, row, dz, half, source):
        out[name] = (link, row, dz, half, source)

    for half, tag in ((LOW, "L"), (HIGH, "H")):
        for d in (1, 2, 3):
            add(f"U{d}{tag}", "up", 0, -d, half, f"U{d - 1}{tag}" if d > 1 else None)
            add(f"D{d}{tag}", "down", 0, d, half, f"D{d - 1}{tag}" if d > 1 else None)
        add(f"Y0{tag}", "y", 1, 0, half, None)
        for d in (1, 2):
            add(f"YU{d}{tag}", "y", 1, -d, half, f"U{d}{tag}")
            add(f"YD{d}{tag}", "y", 1, d, half, f"D{d}{tag}")
        add(f"OU3{tag}", "up", 1, -3, half, f"YU2{tag}")
        add(f"OD3{tag}", "down", 1, 3, half, f"YD2{tag}")
    add("U4L", "up", 0, -4, LOW, "U3L")
    add("D4H", "down", 0, 4, HIGH, "D3H")
    add("OU4L", "up", 1, -4, LOW, "OU3L")
    add("OD4H", "down", 1, 4, HIGH, "OD3H")
    for name in list(out):
        link, row, dz, half, source = out[name]
        add("C" + name, "core", row, dz, half, name)
    add("C0L", "core", 0, 0, LOW, None)
    add("C0H", "core", 0, 0, HIGH, None)
    return {
        f"{name}{tag}": (link, row, dz, half, tag, source and f"{source}{tag}")
        for name, (link, row, dz, half, source) in out.items()
        for tag in PIECES
    }


TRANSFERS = transfers()
SPECIAL = [name for name, entry in TRANSFERS.items() if entry[1] == 1 and entry[3] == HIGH]
INDEX = {name: i for i, name in enumerate(TRANSFERS)}
FORWARDS = {name: [k for k, v in TRANSFERS.items() if v[5] == name] for name in TRANSFERS}
FIRST = [f"{n}{half}{p}" for half in "LH" for p in PIECES for n in ("U1", "D1", "Y0")]
FIRST += [f"C0{half}{p}" for half in "LH" for p in PIECES]

ARRIVALS = [
    ["U1L", "D1L", "Y0L"],
    ["U1H", "D1H", "Y0H"],
    ["U2L", "D2L", "YU1L"],
    ["U2H", "D2H", "YD1L"],
    ["U3L", "D3L", "YU2L"],
    ["U3H", "D3H", "YD2L"],
    ["U4L", "D4H", "YU2H"],
    ["OU3L", "OD3L", "YD2H"],
    ["OU3H", "OD3H", "YU1H"],
    ["OU4L", "OD4H", "YD1H"],
]
LATE, LATE_AFTER = [f"{n}{p}" for p in PIECES for n in ("YU1H", "YD1H")], 5

OWN, NEAR, FAR, OPP = 0, 1, 2, 3
PLAN = [
    6, (NEAR, 0, LOW), 7, (NEAR, 0, HIGH), (FAR, 0, LOW), 8, (FAR, 0, HIGH), 9, (OPP, 0, LOW), (OPP, 0, HIGH),
]
CACHE_AT = 5
REACH = {OWN: (0, 1), NEAR: (1, 2), FAR: (2, 3), OPP: (3, 4)}


def needs(kind, row, half):
    return [
        name
        for name, (link, r, dz, hf, _, _) in TRANSFERS.items()
        if link == "core" and r == row and hf == half and abs(dz) in REACH[kind]
    ]


def steps_of(plan):
    jobs, before, pending, seen = [], [], [], set(needs(OWN, 0, LOW) + needs(OWN, 0, HIGH))
    for entry in plan:
        if isinstance(entry, int):
            pending.append(entry)
        else:
            jobs.append(entry)
            fresh = [name for name in needs(*entry) if name not in seen]
            seen.update(fresh)
            before.append((pending, fresh))
            pending = []
    rest = [name for name in TRANSFERS if TRANSFERS[name][0] == "core" and name not in seen]
    return jobs, before, rest


JOBS, BEFORE, REST = steps_of(PLAN)


def online(scores, old, held, values):
    parts = [scores[:, i : i + DH] for i in range(0, KEYS, DH)]
    top = parts[0]
    for part in parts[1:]:
        top = jnp.maximum(top, part)
    new = jnp.maximum(old, jnp.max(top, axis=1, keepdims=True))
    weights = jnp.concatenate([jnp.exp((part - new) * SCALE).astype(jnp.bfloat16) for part in parts], axis=1)
    factor = jnp.exp((old - new) * SCALE)
    product = jnp.dot(weights, values, preferred_element_type=jnp.float32)
    return new, held * jnp.concatenate([factor, factor], axis=1) + product


def gather_kernel(q_ref, k_ref, v_ref, seg_ref, buf, kc_ref, vc_ref, qx, acc, peak, kfeat, send, recv, csend, crecv, own):
    c = lax.axis_index("ctx")
    h = lax.axis_index("head")
    y, z, core = c // 16, (c % 16) // 2, c % 2

    def index_of(row, zz, kk):
        return row * 16 + (zz % 8) * 2 + kk

    up_to = index_of(y, z + 1, core)
    down_to = index_of(y, z + 7, core)
    y_to = index_of(1 - y, z, core)
    core_to = index_of(y, z, 1 - core)
    target = {"up": up_to, "down": down_to, "y": y_to, "core": core_to}

    barrier = pltpu.get_barrier_semaphore()
    for peer in (up_to, down_to, y_to, core_to):
        pl.semaphore_signal(barrier, inc=1, device_id=(peer, h), device_id_type=MESH)
    for d in range(1, HEAD):
        pl.semaphore_signal(barrier, inc=1, device_id=(c, (h + d) % HEAD), device_id_type=MESH)
    for half in range(2):
        buf[2 * half, c] = k_ref[half]
        buf[2 * half + 1, c] = v_ref[half]
    pl.semaphore_wait(barrier, 4 + HEAD - 1)

    def copy_of(name):
        link, row, dz, half, piece, source = TRANSFERS[name]
        shift = {"up": 1, "down": -1}.get(link, 0)
        there = y if (row == 0) != (link == "y") else 1 - y
        block = index_of(there, z + dz + shift + 8, core)
        part = pl.ds(piece % PARTS * (ROWS // PARTS), ROWS // PARTS)
        dst = buf.at[2 * half + piece // PARTS, block, part]
        return pltpu.make_async_remote_copy(
            src_ref=dst,
            dst_ref=dst,
            send_sem=send.at[1 if name in SPECIAL else 0],
            recv_sem=recv.at[INDEX[name]],
            device_id=(target[link], h),
            device_id_type=MESH,
        )

    def start(name):
        if name not in SPECIAL:
            copy_of(name).start()
        else:
            pl.when(y == (0 if TRANSFERS[name][0] == "y" else 1))(lambda: copy_of(name).start())

    def wait(name):
        if name not in SPECIAL:
            copy_of(name).wait_recv()
        else:
            pl.when(y == 1)(lambda: copy_of(name).wait_recv())

    for name in FIRST:
        start(name)

    def arrive(event):
        names = [f"{n}{p}" for p in PIECES for n in ARRIVALS[event]]
        for name in names:
            wait(name)
            for onward in FORWARDS[name]:
                if TRANSFERS[onward][0] != "core" and onward not in LATE:
                    start(onward)
        for name in names:
            start("C" + name)
        if event == LATE_AFTER:
            for name in LATE:
                start(name)

    seg = seg_ref[...]
    lane = lax.broadcasted_iota(jnp.int32, (1, DH), 1)
    low = jnp.zeros((1, DH), jnp.float32)
    high = jnp.zeros((1, DH), jnp.float32)
    for s in range(4):
        below = jnp.sum(jnp.where(seg < s, 1.0, 0.0), axis=(0, 1), keepdims=True)
        upto = jnp.sum(jnp.where(seg <= s, 1.0, 0.0), axis=(0, 1), keepdims=True)
        low = jnp.where(lane == s, below, low)
        high = jnp.where(lane == s, upto, high)
    used = jnp.where(lane < 4, 1.0, 0.0)

    def inside(first, rows):
        at = (lax.broadcasted_iota(jnp.int32, (rows, DH), 0) + first).astype(jnp.float32)
        return jnp.where((at >= low) & (at < high), 1.0, 0.0)

    for s in range(2):
        feature = ((used - inside(s * CTX * ROWS + c * ROWS, ROWS)) * OTHER).astype(jnp.bfloat16)
        for g in range(GROUPS):
            qx[s, g, :, :DH] = q_ref[s, :, g * DH : (g + 1) * DH]
            qx[s, g, :, DH:] = feature

    def prepare_keys(i, carry):
        for place, chunk in enumerate((y * 16, CTX + y * 16, (1 - y) * 16)):
            kfeat[place, i] = inside((chunk + i) * ROWS, ROWS).astype(jnp.bfloat16)
        return carry

    lax.fori_loop(0, 16, prepare_keys, 0)
    peak[...] = jnp.full(peak.shape, START, jnp.float32)
    acc[...] = jnp.zeros(acc.shape, jnp.float32)

    rows = TILE * ROWS
    ones = jnp.ones((KEYS, DH), jnp.bfloat16)

    def attend(qs, half, block, causal):
        first = block * 4
        keys = buf[2 * half, pl.ds(first, 4)].reshape(KEYS, DH)
        values = buf[2 * half + 1, pl.ds(first, 4)].reshape(KEYS, DH)
        place = jnp.where(half == 1, 1, jnp.where(first // 16 == y, 0, 2))
        features = kfeat[place, pl.ds(first % 16, 4)].reshape(KEYS, DH)
        keys = jnp.concatenate([keys, features], axis=1)
        values = jnp.concatenate([values, ones], axis=1)
        seen = None
        if causal:
            row = lax.broadcasted_iota(jnp.int32, (ROWS, KEYS), 0) + (c - first) * ROWS
            col = lax.broadcasted_iota(jnp.int32, (ROWS, KEYS), 1)
            seen = jnp.concatenate([row >= col] * TILE, axis=0)

        def scores_of(t):
            queries = qx[qs, pl.ds(t * TILE, TILE)].reshape(rows, 2 * DH)
            return lax.dot_general(
                queries, keys, (((1,), (1,)), ((), ())), preferred_element_type=jnp.float32
            )

        scores = scores_of(0)
        for t in range(GROUPS // TILE):
            later = scores_of(t + 1) if t + 1 < GROUPS // TILE else None
            heads = pl.ds(t * TILE, TILE)
            if causal:
                scores = jnp.where(seen, scores, LATER)
            old = peak[qs, heads].reshape(rows, DH)
            held = acc[qs, heads].reshape(rows, 2 * DH)
            new, held = online(scores, old, held, values)
            acc[qs, heads] = held.reshape(TILE, ROWS, 2 * DH)
            peak[qs, heads] = new.reshape(TILE, ROWS, DH)
            scores = later

    zb = z // 2
    mine = y * 4 + zb
    toward = 1 - 2 * (z % 2)

    for event in range(6):
        arrive(event)
    for name in needs(OWN, 0, LOW) + needs(OWN, 0, HIGH):
        copy_of(name).wait_recv()

    def own_step(half, carry):
        attend(half, half, mine, True)
        return carry

    lax.fori_loop(0, 2, own_step, 0)

    page = c // 16
    columns = pl.ds(pl.multiple_of(h * DH, DH), DH)

    def cache_source(kv, to):
        return buf.at[2 * page + kv, 2 * (c % 16) + to // 4, pl.ds(pl.multiple_of(CACHE * (to % 4), 16), CACHE)]

    def cache_copies(d):
        to = (h + d) % HEAD
        return [
            pltpu.make_async_remote_copy(
                src_ref=cache_source(kv, to),
                dst_ref=ref.at[:, columns],
                send_sem=csend.at[kv, d],
                recv_sem=crecv.at[kv, d],
                device_id=(c, to),
                device_id_type=MESH,
            )
            for kv, ref in ((0, kc_ref), (1, vc_ref))
        ]

    local_copies = [
        pltpu.make_async_copy(cache_source(kv, h), ref.at[:, columns], own.at[kv])
        for kv, ref in ((0, kc_ref), (1, vc_ref))
    ]

    def start_cache():
        for name in REST:
            wait(name)
        for d in range(1, HEAD):
            for copy in cache_copies(d):
                copy.start()
        for copy in local_copies:
            copy.start()

    def step_body(step, carry):
        def pick(values):
            value = jnp.int32(values[0])
            for i in range(1, len(values)):
                value = jnp.where(step == i, jnp.int32(values[i]), value)
            return value

        for i, (events, names) in enumerate(BEFORE):
            if events or names:

                @pl.when(step == i)
                def _(events=events, names=names):
                    for event in events:
                        arrive(event)
                    for name in names:
                        copy_of(name).wait_recv()

        pl.when(step == CACHE_AT)(start_cache)

        row = pick([job[1] for job in JOBS])
        half = pick([job[2] for job in JOBS])
        move = pick([{OWN: 0, NEAR: 0, FAR: 0, OPP: 2}[job[0]] for job in JOBS]) + toward * pick(
            [{OWN: 0, NEAR: -1, FAR: 1, OPP: 0}[job[0]] for job in JOBS]
        )
        block = jnp.where(row == 0, y, 1 - y) * 4 + (zb + move + 4) % 4
        qs = jnp.where(jnp.logical_or(half == 1, block > mine), 1, 0)

        @pl.when(jnp.logical_or(half == 0, block < mine))
        def _():
            attend(qs, half, block, False)

        return carry

    lax.fori_loop(0, len(JOBS), step_body, 0)

    def wait_sent(names, sem):
        halves = 4 if len(names) * 2 % (4 * PARTS * 2) == 0 else 2
        sent = buf.at[pl.ds(0, halves), pl.ds(0, len(names) // (halves * PARTS))]
        pltpu.make_async_remote_copy(
            src_ref=sent,
            dst_ref=sent,
            send_sem=send.at[sem],
            recv_sem=recv.at[0],
            device_id=(core_to, h),
            device_id_type=MESH,
        ).wait_send()

    wait_sent([name for name in TRANSFERS if name not in SPECIAL], 0)
    for row in range(2):
        sent_in_row = [name for name in SPECIAL if (TRANSFERS[name][0] == "y") == (row == 0)]
        pl.when(y == row)(lambda names=sent_in_row: wait_sent(names, 1))
    for copy in local_copies:
        copy.wait()
    for d in range(1, HEAD):
        for copy in cache_copies(d):
            copy.wait()


def attend_kernel(seg_ref, kin_ref, vin_ref, buf, qx, sums, peaks, out_ref, kc_ref, vc_ref, acc, peak, state):
    c = lax.axis_index("ctx")
    y, mine = c // 16, c // 4
    kc_ref[...] = kin_ref[...]
    vc_ref[...] = vin_ref[...]
    acc[0] = sums[...]
    peak[...] = peaks[...]
    state[0] = 0
    state[1] = 0

    seg = seg_ref[...]
    starts = [jnp.int32(0)] + [
        jnp.sum(jnp.where(seg < s, 1.0, 0.0)).astype(jnp.int32) for s in range(1, 4)
    ] + [jnp.int32(2 * CTX * ROWS)]
    lane = lax.broadcasted_iota(jnp.int32, (1, DH), 1)
    low = jnp.zeros((1, DH), jnp.int32)
    high = jnp.zeros((1, DH), jnp.int32)
    for s in range(4):
        low = jnp.where(lane == s, starts[s], low)
        high = jnp.where(lane == s, starts[s + 1], high)

    def inside(first, rows):
        at = lax.broadcasted_iota(jnp.int32, (rows, DH), 0) + first
        return jnp.where(jnp.logical_and(at >= low, at < high), 1.0, 0.0)

    def segment_start(at):
        begin = jnp.int32(0)
        for start in starts[1:4]:
            begin = jnp.where(start <= at, start, begin)
        return begin

    first, inner = [], []
    for s in range(2):
        at = s * CTX * ROWS + c * ROWS
        first.append(segment_start(at) // KEYS)
        inner.append(segment_start(at + ROWS - 1))
    count = jnp.where(y == 1, jnp.maximum(4 - first[0], 0), 0)
    upper_first = jnp.maximum(first[1], 4 + 4 * y)
    upper_count = jnp.maximum(8 + 4 * y - upper_first, 0)
    total = count + upper_count + jnp.where(first[1] <= mine, 1, 0)

    rows = TILE * ROWS
    ones = jnp.ones((KEYS, DH), jnp.bfloat16)

    def operands(block, featured):
        half, chunk = block // 8, (block % 8) * 4
        keys = buf[2 * half, pl.ds(chunk, 4)].reshape(KEYS, DH)
        values = buf[2 * half + 1, pl.ds(chunk, 4)].reshape(KEYS, DH)
        if featured:
            keys = jnp.concatenate([keys, inside(block * KEYS, KEYS).astype(jnp.bfloat16)], axis=1)
        return keys, values

    def attend(qs, block):
        keys, values = operands(block, True)
        values = jnp.concatenate([values, ones], axis=1)
        now = state[qs]
        for t in range(GROUPS // TILE):
            heads = pl.ds(t * TILE, TILE)
            queries = qx[qs, heads].reshape(rows, 2 * DH)
            scores = lax.dot_general(
                queries, keys, (((1,), (1,)), ((), ())), preferred_element_type=jnp.float32
            )
            old = peak[qs, heads].reshape(rows, DH)
            held = acc[now, qs, heads].reshape(rows, 2 * DH)
            new, held = online(scores, old, held, values)
            acc[now, qs, heads] = held.reshape(TILE, ROWS, 2 * DH)
            peak[qs, heads] = new.reshape(TILE, ROWS, DH)

    def attend_kept(qs, block, featured):
        keys, values = operands(block, featured)
        values = jnp.concatenate([values, ones], axis=1)
        now = state[qs]
        width = keys.shape[1]

        def scores_of(t):
            queries = qx[qs, pl.ds(t * TILE, TILE), :, :width].reshape(rows, width)
            return lax.dot_general(
                queries, keys, (((1,), (1,)), ((), ())), preferred_element_type=jnp.float32
            )

        largest = jnp.zeros((8, DH), jnp.float32)
        scores = scores_of(0)
        for t in range(GROUPS // TILE):
            later = scores_of(t + 1) if t + 1 < GROUPS // TILE else None
            heads = pl.ds(t * TILE, TILE)
            top = peak[qs, heads].reshape(rows, DH)
            weights = jnp.concatenate(
                [jnp.exp((scores[:, i : i + DH] - top) * SCALE).astype(jnp.bfloat16) for i in range(0, KEYS, DH)],
                axis=1,
            )
            product = jnp.dot(weights, values, preferred_element_type=jnp.float32)
            held = acc[now, qs, heads].reshape(rows, 2 * DH) + product
            acc[1 - now, qs, heads] = held.reshape(TILE, ROWS, 2 * DH)
            largest = jnp.maximum(largest, jnp.max(held[:, DH:].reshape(rows // 8, 8, DH), axis=0))
            scores = later
        fits = jnp.max(largest) <= LARGEST
        state[qs] = jnp.where(fits, 1 - now, now)
        state[2] = jnp.where(fits, 0, 1)

    def step(j, carry):
        upper = j >= count
        qs = jnp.where(upper, 1, 0)
        block = jnp.where(upper, jnp.where(j - count < upper_count, upper_first + j - count, mine), first[0] + j)
        plain = block * KEYS >= jnp.where(upper, inner[1], inner[0])

        @pl.when(plain)
        def _():
            attend_kept(qs, block, False)

        @pl.when(jnp.logical_not(plain))
        def _():
            attend_kept(qs, block, True)

        @pl.when(state[2] == 1)
        def _():
            attend(qs, block)

        return carry

    lax.fori_loop(0, total, step, 0)

    def finish(g, carry):
        for s in range(2):
            held = acc[state[s], s, g]
            out_ref[s, :, pl.ds(pl.multiple_of(g * DH, DH), DH)] = (held[:, :DH] / held[:, DH:]).astype(jnp.bfloat16)
        return carry

    lax.fori_loop(0, GROUPS, finish, 0)


def body(queries, key_states, value_states, segment_ids):
    vmem = pl.BlockSpec(memory_space=pltpu.VMEM)
    anywhere = pl.BlockSpec(memory_space=pl.ANY)
    cache = jax.ShapeDtypeStruct((CACHE, HEAD * DH), jnp.bfloat16)
    segments = segment_ids.reshape(-1, DH)
    gathered, keys, values, prepared, sums, peaks = pl.pallas_call(
        gather_kernel,
        out_shape=(
            jax.ShapeDtypeStruct((4, CTX, ROWS, DH), jnp.bfloat16),
            cache,
            cache,
            jax.ShapeDtypeStruct((2, GROUPS, ROWS, 2 * DH), jnp.bfloat16),
            jax.ShapeDtypeStruct((2, GROUPS, ROWS, 2 * DH), jnp.float32),
            jax.ShapeDtypeStruct((2, GROUPS, ROWS, DH), jnp.float32),
        ),
        in_specs=[vmem] * 4,
        out_specs=(vmem, anywhere, anywhere, vmem, vmem, vmem),
        scratch_shapes=[
            pltpu.VMEM((3, 16, ROWS, DH), jnp.bfloat16),
            pltpu.SemaphoreType.DMA((2,)),
            pltpu.SemaphoreType.DMA((len(TRANSFERS),)),
            pltpu.SemaphoreType.DMA((2, HEAD)),
            pltpu.SemaphoreType.DMA((2, HEAD)),
            pltpu.SemaphoreType.DMA((2,)),
        ],
        compiler_params=pltpu.CompilerParams(
            collective_id=0, has_side_effects=True, vmem_limit_bytes=GATHER_VMEM
        ),
        name="gather",
    )(queries, key_states, value_states, segments)
    return pl.pallas_call(
        attend_kernel,
        out_shape=(jax.ShapeDtypeStruct((2, ROWS, GROUPS * DH), jnp.bfloat16), cache, cache),
        in_specs=[vmem] * 7,
        out_specs=(vmem,) * 3,
        scratch_shapes=[
            pltpu.VMEM((2, 2, GROUPS, ROWS, 2 * DH), jnp.float32),
            pltpu.VMEM((2, GROUPS, ROWS, DH), jnp.float32),
            pltpu.SMEM((3,), jnp.int32),
        ],
        compiler_params=pltpu.CompilerParams(vmem_limit_bytes=ATTEND_VMEM),
        name="attend",
    )(segments, keys, values, gathered, prepared, sums, peaks)


def solution(mesh):
    in_specs = (P(None, "ctx", "head"), P(None, "ctx", "head"), P(None, "ctx", "head"), P())
    out_specs = (P(None, "ctx", "head"), P(("ctx", "head"), None), P(("ctx", "head"), None))
    return jax.shard_map(body, mesh=mesh, in_specs=in_specs, out_specs=out_specs, check_vma=False)
```
